256 devices in a mesh: aux: 8 (over z), occ: 2 (over core), vir: 16 (over y, x).
Axes of the slice: x: 4, y: 4, z: 8, core: 2. Of those that a mesh axis runs over, the one named last changes fastest.
Arguments:
- integrals: bfloat16 [32, 4000, 4000], P('aux', 'occ', 'vir'), may hold values from -4.5 to 4.5
- occ_coeffs: bfloat16 [4000, 400], replicated, may hold values from -0.09375 to 0.09375
- vir_coeffs: bfloat16 [4000, 3600], P('vir'), may hold values from -7.404361e-05 to 7.404361e-05
- occ_energy: float32 [400], replicated, may hold values from -1.5 to -0.5
- vir_energy: float32 [3600], P('vir'), may hold values from 0.2 to 2
- trial_vectors: bfloat16 [400, 8], replicated, may hold values from -0.3125 to 0.3125
- shifts: float32 [8], P('aux'), may hold values from -1 to -0.3
Outputs:
- sigma_vectors: float32 [400, 8], P(None, 'aux')
- subspace: float32 [8, 8], P(None, 'aux')
The draws below stay inside these ranges and needn't reach their ends.
All inputs are finite; a program needn't handle non-finite values.
Results may differ from the reference program's by a relative error of at most 0.0024.
Values may be sent and summed in bfloat16 or wider, within the bound.
A program may use at most 128 MiB of HBM per device.

```python
import math
import jax
import jax.numpy as jnp
from jax import lax

AO = 4000
NOCC = 400
NVIR = 3600
NAUX = 32
NVEC = 8
N_OCC = 2


def draw_integrals(key, part):
    key = jax.random.fold_in(key, 11)
    noise_key, field_key, factor_key = jax.random.split(key, 3)
    noise = jax.random.normal(noise_key, (NAUX, AO, AO), jnp.float32)
    field = jax.random.normal(field_key, (AO, AO), jnp.float32)
    strength = 0.8
    factors = jax.random.normal(factor_key, (NAUX,), jnp.float32)
    values = (noise + strength * factors[:, None, None] * field[None, :, :]) / math.sqrt(1.0 + strength * strength)
    return jnp.clip(values, -4.5, 4.5).astype(jnp.bfloat16)


def draw_vir_coeffs(key, part):
    key = jax.random.fold_in(key, 23)
    noise_key, profile_key, weight_key = jax.random.split(key, 3)
    noise = jax.random.normal(noise_key, (AO, NVIR), jnp.float32)
    profile = jax.random.normal(profile_key, (AO,), jnp.float32)
    weights = 0.6 * jax.random.normal(weight_key, (NVIR,), jnp.float32)
    raw = (noise + profile[:, None] * weights[None, :]) / math.sqrt(1.36)
    limit = 4.0 * (1.0 - 2.0 ** (-8))
    scale = float(AO * NAUX * NOCC * (NVIR // 64 + 1)) ** (-0.5)
    return (jnp.clip(raw, -limit, limit) * scale).astype(jnp.bfloat16)


def block_scale(stream_key, dims, cuts, smallest, top_value):
    def one(position, parts):
        steps = jax.random.uniform(jax.random.fold_in(jax.random.fold_in(stream_key, 6), position), (parts,), jnp.float32, smallest / len(cuts), top_value / len(cuts))
        return jnp.repeat(jnp.exp(steps), dims[position] // parts).reshape((-1,) + (1,) * (len(dims) - position - 1))

    factor_of = one(*cuts[0])
    for cut in cuts[1:]:
        factor_of = factor_of * one(*cut)
    return factor_of


def scatter_about(key, shape, scale, most, kind=jnp.bfloat16):
    return jnp.clip(scale * jax.random.normal(key, shape, jnp.float32), -most, most).astype(kind)


def setup_inputs(seed: int = 0) -> dict:
    seeds = jax.random.split(jax.random.key(seed), 8)
    integrals = draw_integrals(jax.random.fold_in(seeds[7], 71), 0)
    occ_coeffs = scatter_about(seeds[1], (AO, NOCC), AO ** -0.5, 0.09375)
    vir_coeffs = draw_vir_coeffs(jax.random.fold_in(seeds[7], 71), 0)
    occ_energy = jnp.clip(jax.random.uniform(seeds[3], (NOCC,), jnp.float32, -1.5, -0.5), -1.5, -0.5)
    vir_energy = jnp.clip(0.2 + 1.8 * jax.random.uniform(seeds[4], (NVIR,), jnp.float32) ** block_scale(seeds[4], (NVIR,), ((0, 16),), -0.2, 0.2), 0.2, 2.0)
    trial_vectors = scatter_about(seeds[5], (NOCC, NVEC), NOCC ** -0.5, 0.3125)
    shifts = jnp.clip(-1.0 + 0.7 * jax.random.uniform(seeds[6], (NVEC,), jnp.float32) ** block_scale(seeds[6], (NVEC,), ((0, 8),), -0.2, 0.2), -1.0, -0.3)
    return dict(integrals=integrals, occ_coeffs=occ_coeffs, vir_coeffs=vir_coeffs, occ_energy=occ_energy, vir_energy=vir_energy, trial_vectors=trial_vectors, shifts=shifts)


def reference(integrals, occ_coeffs, vir_coeffs, occ_energy, vir_energy, trial_vectors, shifts):
    def transform(slab):
        halfway = jnp.dot(occ_coeffs.T, slab, preferred_element_type=jnp.float32).astype(jnp.bfloat16)
        particle = jnp.dot(halfway, vir_coeffs, preferred_element_type=jnp.float32).astype(jnp.bfloat16)
        pairing = jnp.dot(occ_coeffs.T, halfway.T, preferred_element_type=jnp.float32).astype(jnp.bfloat16)
        return particle, pairing

    hole_particle, hole_pair = lax.map(transform, integrals)
    trial_wide = trial_vectors.astype(jnp.float32)
    pair_wide = hole_pair.astype(jnp.float32)
    reduced = jnp.einsum('kn,qki->nqi', trial_wide, pair_wide).astype(jnp.bfloat16)
    reduced = lax.optimization_barrier(reduced).astype(jnp.float32)
    particle_wide = hole_particle.astype(jnp.float32)
    blocks = NOCC // N_OCC

    def per_vector(operand):
        vector_rows, energy_shift = operand
        groups = jnp.transpose(vector_rows.reshape(NAUX, NOCC // blocks, blocks), (1, 0, 2))
        energy_groups = occ_energy.reshape(NOCC // blocks, blocks)

        def per_block(operand_pair):
            values, energies = operand_pair
            coupled = jnp.einsum('qi,qja->ija', values, particle_wide)
            divisor = energy_shift + vir_energy[None, None, :] - energies[:, None, None] - occ_energy[None, :, None]
            weighted = lax.optimization_barrier((coupled / divisor).astype(jnp.bfloat16)).astype(jnp.float32)
            return jnp.einsum('ija,qja->qi', weighted, particle_wide)

        pieces = lax.map(per_block, (groups, energy_groups))
        return jnp.transpose(pieces, (1, 0, 2)).reshape(NAUX, NOCC)

    folded = lax.map(per_vector, (reduced, shifts)).astype(jnp.bfloat16)
    folded = lax.optimization_barrier(folded).astype(jnp.float32)
    sigma_vectors = occ_energy[:, None] * trial_wide + jnp.einsum('qki,nqi->kn', pair_wide, folded)
    subspace = jnp.dot(trial_wide.T, sigma_vectors, precision=lax.Precision.HIGHEST)
    return sigma_vectors, subspace
```

```python
import functools
import math

import jax
import jax.numpy as jnp
from jax import lax
from jax.experimental import pallas as pl
from jax.experimental.pallas import tpu as pltpu
from jax.sharding import PartitionSpec as P

MESH = pl.DeviceIdType.MESH
F32 = jnp.float32
BF16 = jnp.bfloat16


def dot(a, b):
    return jnp.dot(a, b, preferred_element_type=F32)


def dot_nt(a, b):
    return lax.dot_general(a, b, (((1,), (1,)), ((), ())), preferred_element_type=F32)


def split(value):
    high = value.astype(BF16)
    low = (value - high.astype(F32)).astype(BF16)
    return jnp.concatenate([high.astype(F32), low.astype(F32)], axis=0).astype(BF16)


def send(src, dst, send_sem, recv_sem, **device):
    copy = pltpu.make_async_remote_copy(
        src_ref=src, dst_ref=dst, send_sem=send_sem, recv_sem=recv_sem, device_id=device, device_id_type=MESH
    )
    copy.start()
    return copy


class Sizes:
    def __init__(self, mesh, integrals, occ_coeffs, vir_energy):
        self.nz = mesh["aux"]
        self.side = math.isqrt(mesh["vir"])
        self.nq, self.mu, self.nu = integrals.shape
        self.ao, self.nocc = occ_coeffs.shape
        self.half = self.nocc // 2
        self.jb = self.half // self.nz
        self.na = vir_energy.shape[0]
        self.block = 16 * (self.na // 16)
        self.rows = self.block + 16
        assert self.na == self.block + 1 and self.side**2 <= 16
        first = (self.jb + 1) // 2
        rows = -(-(self.nq * first) // 16) * 16
        width = -(-(first * self.na) // 256) * 256
        self.groups = [(0, first, 0, 0, width)]
        rest = self.jb - first
        self.groups.append((first, rest, rows, width, -(-(rest * self.na) // 256) * 256))
        self.pack = rows + -(-(self.nq * rest) // 16) * 16
        self.flat = self.groups[1][3] + self.groups[1][4]
        self.pairs = self.nz // 2
        self.lane0 = self.mu // 128 * 128
        self.shift = self.mu - self.lane0
        self.window = self.mu + self.shift
        self.lanes = -(-self.rows // 128) * 128
        self.q = self.nq * self.nz
        self.nvec = self.nz
        self.parts = -(-self.half // 128)
        last = 128 * (self.nu * (mesh["vir"] - 1) // 128) - 128
        self.view = self.ao - last
        for v in range(mesh["vir"]):
            start = 128 * (self.nu * v // 128) - 128 * ((v + 1) // mesh["vir"])
            assert start + self.view <= self.ao and self.nu * v - start + self.nu <= self.view


def kernel(
    s, int_h, occ_h, vir_h, trial, eo_row, eo_s, ve, shift_s,
    sigma_out, sub_out,
    ibuf, occ_v, pf, xf, hq, pk, hs, hg, vb, acc, bs, bx, bf, bflat, bj, bjt, base, sec, eob, ve8, shift,
    rp, rg, rx, rmsg, rall, rl, rmf, sh, fa, fl, fx, fz, fr, fg, fgx, spart, sgs, sgr, spp, spr, t32,
    in_sem, v_own, v_s, v_r, sh_s, sh_r, x_s, x_r, h_s, h_r, g_s, g_r, rg_s, rg_r, rx_s, rx_r, rz_s, rz_r, rc_s, rc_r,
    b_s, b_r, fc_s, fc_r, fz_s, fz_r, fg_s, fg_r, fx_s, fx_r, s1_s, s1_r, s2_s, s2_r,
):
    nz, side = s.nz, s.side
    z, c, v = lax.axis_index("aux"), lax.axis_index("occ"), lax.axis_index("vir")
    y, x = v // side, v % side
    g = y + c * (x - y)
    r = x + c * (y - x)
    sg = side - (side - 1) * c
    sr = 1 + (side - 1) * c

    def vid(gather, reduce):
        return gather * sg + reduce * sr

    started = []

    def go(*args, **device):
        copy = send(*args, **device)
        started.append(copy)
        return copy

    occ_in = pltpu.make_async_copy(occ_h, occ_v, in_sem.at[s.nq])
    occ_in.start()
    zero_rows = jnp.zeros((s.shift, s.nu), BF16)
    loads = []
    for q in range(s.nq):
        if s.shift:
            ibuf[q, 0 : s.shift, :] = zero_rows
            ibuf[q, s.mu : s.mu + s.shift, :] = zero_rows
        copy = pltpu.make_async_copy(
            int_h.at[q], ibuf.at[q, pl.ds(pl.multiple_of(s.shift * c, 16), s.mu), :], in_sem.at[q]
        )
        copy.start()
        loads.append(copy)
    own_v = []
    for w in range(side):
        start = pl.multiple_of(s.block * vid(g, w), 16)
        copy = pltpu.make_async_copy(vir_h.at[pl.ds(start, s.rows), :], vb.at[0, w], v_own.at[w])
        copy.start()
        own_v.append(copy)

    barrier = pltpu.get_barrier_semaphore()
    me = 2 * z + c
    for d in range(1, 2 * nz):
        other = (me + d) % (2 * nz)
        pl.semaphore_signal(barrier, inc=1, device_id={"aux": other // 2, "occ": other % 2}, device_id_type=MESH)
    for d in range(1, side * side):
        pl.semaphore_signal(barrier, inc=1, device_id={"vir": (v + d) % (side * side)}, device_id_type=MESH)
    pl.semaphore_wait(barrier, 2 * nz + side * side - 2)

    v_copies = {}
    for e in range(1, side):
        to = (g + e) % side
        for w in range(side):
            start = pl.multiple_of(s.block * vid(to, w), 16)
            v_copies[side - e, w] = go(
                vir_h.at[pl.ds(start, s.rows), :], vb.at[side - e, w], v_s.at[e - 1, w], v_r.at[side - e - 1, w],
                vir=vid(to, r),
            )
    shift[...] = jnp.full((8, 128), shift_s[0], F32)
    for e in range(1, nz):
        go(shift, sh.at[z], sh_s.at[e - 1], sh_r.at[z], aux=(z + e) % nz)
    sh[z] = shift[...]

    occ_in.wait()
    x_copies = []
    for q in range(s.nq):
        loads[q].wait()
        columns = occ_v[:, pl.ds(pl.multiple_of(s.lane0 * c, 128), s.window)]
        pf[q] = dot(columns, ibuf[q])
        x_copies.append(
            go(pf.at[q, pl.ds(pl.multiple_of(s.half * (1 - c), 8), s.half), :], xf.at[q], x_s.at[q], x_r.at[q], occ=1 - c)
        )
    start = 128 * ((s.nu * v) // 128) - 128 * ((v + 1) // (side * side))
    view = occ_v[:, pl.ds(pl.multiple_of(start, 128), s.view)].astype(F32)
    wide = -(-s.view // 128) * 128
    view = jnp.concatenate([view, jnp.zeros((s.nocc, wide - s.view), F32)], axis=1)
    sec[...] = pltpu.roll(view, wide - (s.nu * v - start), 1)[:, : s.nu].astype(BF16)
    t32[...] = trial[...].astype(F32)
    weights = split(dot(trial[...], sec[...]))
    pk[...] = jnp.zeros(pk.shape, F32)
    for q in range(s.nq):
        x_copies[q].wait_recv()
        xf[q] = xf[q] + pf[q, pl.ds(pl.multiple_of(s.half * c, 8), s.half), :]
        hq[q] = xf[q].astype(BF16)
        for to in range(nz):
            for j0, count, row0, _, _ in s.groups:
                pk[to, row0 + q * count : row0 + (q + 1) * count, :] = xf[q, to * s.jb + j0 : to * s.jb + j0 + count, :]
    hs[...] = pk[...].astype(BF16)
    for e in range(1, nz):
        to = (z + e) % nz
        go(hs.at[to], hg.at[0, z], h_s.at[e - 1], h_r.at[z], aux=to)
    hg[0, z] = hs[z]
    for e in range(1, side):
        go(
            hg.at[0, z], hg.at[side - e, z], g_s.at[e - 1, 0], g_r.at[side - e - 1, z], vir=vid((g + e) % side, r),
        )

    for q in range(s.nq):
        both = dot_nt(weights, hq[q])
        rp[q * s.nvec : (q + 1) * s.nvec, :] = both[: s.nvec] + both[s.nvec :]
    for e in range(1, side):
        go(rp, rg.at[side - e], rg_s.at[e - 1], rg_r.at[side - e - 1], vir=vid((g + e) % side, r))

    def arrived(dst, recv_sem):
        pltpu.make_async_remote_copy(
            src_ref=dst, dst_ref=dst, send_sem=recv_sem, recv_sem=recv_sem, device_id={"occ": c}, device_id_type=MESH
        ).wait_recv()

    for d in range(1, nz):
        source = (z + d) % nz
        arrived(hg.at[0, source], h_r.at[source])
        for e in range(1, side):
            go(
                hg.at[0, source], hg.at[side - e, source], g_s.at[e - 1, d], g_r.at[side - e - 1, source],
                vir=vid((g + e) % side, r),
            )
    total = rp[...]
    for d in range(1, side):
        arrived(rg.at[d], rg_r.at[d - 1])
        total = total + rg[d]
    rx[0] = total
    for e in range(1, side):
        go(rx.at[0], rx.at[side - e], rx_s.at[e - 1], rx_r.at[side - e - 1], vir=vid(g, (r + e) % side))

    tall = nz * s.pack
    for w in range(side):
        own_v[w].wait()

    def product(d):
        @pl.loop(0, side)
        def _(w):
            value = dot_nt(hg[d].reshape(tall, s.nu), vb[d, w])
            if d > 0:
                value = value + acc[w]
            acc[w] = value
            if d == side - 1:
                bs[w] = value.astype(BF16)

    product(0)
    total = rx[0]
    for d in range(1, side):
        arrived(rx.at[d], rx_r.at[d - 1])
        total = total + rx[d]
    rmsg[...] = total
    for e in range(1, nz):
        go(
            rmsg, rall.at[c, pl.ds(pl.multiple_of(z * s.nq * s.nvec, 8), s.nq * s.nvec), :], rz_s.at[e - 1], rz_r.at[z],
            aux=(z + e) % nz,
        )
    rall[c, pl.ds(pl.multiple_of(z * s.nq * s.nvec, 8), s.nq * s.nvec), :] = total
    for d in range(1, side):
        for source in range(nz):
            arrived(hg.at[d, source], g_r.at[d - 1, source])
        for w in range(side):
            v_copies[d, w].wait_recv()
        product(d)
    for e in range(1, side):
        to = (r + e) % side
        go(bs.at[to], bx.at[side - e], b_s.at[e - 1], b_r.at[side - e - 1], vir=vid(g, to))
    for d in range(1, nz):
        source = (z + d) % nz
        arrived(rall.at[c, pl.ds(pl.multiple_of(source * s.nq * s.nvec, 8), s.nq * s.nvec), :], rz_r.at[source])
        arrived(sh.at[source], sh_r.at[source])
    to_other = go(rall.at[c], rall.at[c], rc_s, rc_r, occ=1 - c)
    arrived(rall.at[1 - c], rc_r)
    nq8 = s.nq * s.nvec
    for h in range(2):
        for part in range(s.parts):
            width = min(128, s.half - part * 128)
            rl[h, part, :, 0:width] = rall[h, :, part * 128 : part * 128 + width]
    for n in range(s.nvec):
        for h in range(2):
            halves = []
            for part in range(s.parts):
                rows = [rl[h, part, pl.ds(q * s.nvec + n, nz, stride=nq8), :] for q in range(s.nq)]
                halves.append(jnp.concatenate(rows, axis=0))
            rmf[n, h * s.half : (h + 1) * s.half, :] = jnp.concatenate(halves, axis=1).T[: s.half]

    ve8[...] = jnp.ones(ve8.shape, F32)
    ve8[:, 0 : s.na] = jnp.broadcast_to(ve[...], (8, s.na))
    base[...] = jnp.ones(base.shape, F32)
    first = s.half * c + s.jb * z
    for j0, count, _, lane0, _ in s.groups:
        for j in range(count):
            base[:, lane0 + j * s.na : lane0 + (j + 1) * s.na] = ve8[:, 0 : s.na] - eo_s[first + j0 + j]
    square = jnp.broadcast_to(eo_row[...], (128, s.nocc))
    fill = -(-s.nocc // 128) * 128 - s.nocc
    eob[...] = jnp.concatenate([square, jnp.zeros((128, fill), F32)], axis=1).T[: s.nocc]

    for d in range(1, side):
        arrived(bx.at[d], b_r.at[d - 1])
    bflat[...] = jnp.zeros(bflat.shape, F32)

    @pl.loop(0, nz)
    def _(source):
        rows = pl.ds(pl.multiple_of(source * s.pack, 16), s.pack)
        value = acc[r, rows, :]
        for d in range(1, side):
            value = value + bx[d, rows, :].astype(F32)
        value = value.astype(BF16).astype(F32)
        full = jnp.concatenate([value, jnp.zeros((s.pack, s.lanes - s.rows), F32)], axis=1)
        full = pltpu.roll(full, s.lanes - v, 1)
        for part in range(s.lanes // 128):
            bf[part, rows, :] = full[:, part * 128 : (part + 1) * 128]

    for j0, count, row0, lane0, _ in s.groups:
        for j in range(count):
            parts = []
            for part in range(s.lanes // 128):
                rows = [bf[part, pl.ds(row0 + q * count + j, nz, stride=s.pack), :] for q in range(s.nq)]
                parts.append(jnp.concatenate(rows, axis=0))
            bflat[:, lane0 + j * s.na : lane0 + (j + 1) * s.na] = jnp.concatenate(parts, axis=1)[:, : s.na]
    bj[...] = bflat[...].astype(BF16)
    bjt[...] = bflat[...].T.astype(BF16)

    def fold(n, group):
        _, _, _, lane0, width = s.groups[group]
        rm = rmf[n].astype(BF16)
        row = jnp.broadcast_to(sh[n][0:1, :], (s.nocc, 128)) - eob[...]
        total = None
        for start in range(lane0, lane0 + width, 1536):
            size = min(1536, lane0 + width - start)
            divisor = jnp.concatenate([row] * (size // 128), axis=1) + base[0:1, start : start + size]
            coupled = dot(rm, bj[:, start : start + size])
            weighted = (coupled * pl.reciprocal(divisor, approx=True, full_range=False)).astype(BF16)
            term = dot(weighted, bjt[start : start + size, :])
            total = term if total is None else total + term
        return total

    @pl.loop(0, s.nvec)
    def _(n):
        fa[n] = fold(n, 0)

    rows2 = 2 * s.nq

    def to_core(p):
        return pltpu.make_async_remote_copy(
            src_ref=fl.at[p, 1 - c], dst_ref=fx.at[p], send_sem=fc_s.at[p], recv_sem=fc_r.at[p],
            device_id={"occ": 1 - c}, device_id_type=MESH,
        )

    def along_z(p, e):
        to = (z + e) % nz
        return pltpu.make_async_remote_copy(
            src_ref=fz.at[p, :, pl.ds(pl.multiple_of(to * rows2, 8), rows2), :], dst_ref=fr.at[p, z],
            send_sem=fz_s.at[p, e - 1], recv_sem=fz_r.at[p, z], device_id={"aux": to}, device_id_type=MESH,
        )

    def pass_on(p):
        to_core(p).wait_recv()
        fz[p] = fl[p, c] + fx[p]
        for e in range(1, nz):
            along_z(p, e).start()

    @pl.loop(0, s.pairs)
    def _(p):
        for m in range(2):
            n = 2 * p + m
            value = fa[n] + fold(n, 1)
            for h in range(2):
                flip = value[h * s.half : (h + 1) * s.half].T
                flip = jnp.concatenate([flip, jnp.zeros((s.q, s.parts * 128 - s.half), F32)], axis=1)
                for part in range(s.parts):
                    for q in range(s.nq):
                        fl[p, h, part, pl.ds(m * s.nq + q, nz, stride=rows2), :] = flip[
                            q * nz : (q + 1) * nz, part * 128 : (part + 1) * 128
                        ]
        to_core(p).start()

        @pl.when(p > 0)
        def _():
            pass_on(p - 1)

    pass_on(s.pairs - 1)
    for p in range(s.pairs):
        total = fz[p, :, pl.ds(pl.multiple_of(z * rows2, 8), rows2), :]
        for d in range(1, nz):
            source = (z + d) % nz
            arrived(fr.at[p, source], fz_r.at[p, source])
            total = total + fr[p, source]
        fg[0, p] = total
    for e in range(1, side):
        go(fg.at[0], fg.at[side - e], fg_s.at[e - 1], fg_r.at[side - e - 1], vir=vid((g + e) % side, r))
    total = fg[0]
    for d in range(1, side):
        arrived(fg.at[d], fg_r.at[d - 1])
        total = total + fg[d]
    fgx[0] = total
    for e in range(1, side):
        go(fgx.at[0], fgx.at[side - e], fx_s.at[e - 1], fx_r.at[side - e - 1], vir=vid(g, (r + e) % side))
    for d in range(1, side):
        arrived(fgx.at[d], fx_r.at[d - 1])
        total = total + fgx[d]

    tall = s.nvec * s.nq
    folded = jnp.concatenate([total[:, part].reshape(tall, 128) for part in range(s.parts)], axis=1)[:, : s.half]
    folded = split(folded)
    owner = lax.broadcasted_iota(jnp.int32, folded.shape, 0) % s.nq
    both = None
    for q in range(s.nq):
        term = dot(jnp.where(owner == q, folded.astype(F32), 0.0).astype(BF16), hq[q])
        both = term if both is None else both + term
    both = dot_nt(split(both[:tall] + both[tall:]), sec[...])
    spart[...] = both[:tall] + both[tall:]
    for n in range(s.nvec):
        value = spart[n * s.nq : n * s.nq + 1, :]
        for q in range(1, s.nq):
            value = value + spart[n * s.nq + q : n * s.nq + q + 1, :]
        sgs[n] = value
    for d in range(1, 2 * nz):
        other = (me + d) % (2 * nz)
        go(sgs.at[other // 2], sgr.at[me], s1_s.at[d - 1], s1_r.at[me], aux=other // 2, occ=other % 2)
    sgr[me] = sgs[z]
    for d in range(1, 2 * nz):
        other = (me + d) % (2 * nz)
        arrived(sgr.at[other], s1_r.at[other])
    total = sgr[0]
    for d in range(1, 2 * nz):
        total = total + sgr[d]
    spp[...] = total
    for d in range(1, side * side):
        go(spp, spr.at[v], s2_s.at[d - 1], s2_r.at[v], vir=(v + d) % (side * side))
    spr[v] = total
    for d in range(1, side * side):
        other = (v + d) % (side * side)
        arrived(spr.at[other], s2_r.at[other])
    total = spr[0]
    for d in range(1, side * side):
        total = total + spr[d]
    sigma = eo_row[...] * t32[pl.ds(z, 1), :] + total
    sigma_out[...] = sigma
    sub_out[...] = jnp.sum(t32[...] * sigma, axis=1, keepdims=True)
    for copy in started:
        copy.wait_send()
    for p in range(s.pairs):
        to_core(p).wait_send()
        for e in range(1, nz):
            along_z(p, e).wait_send()


def local(mesh, integrals, occ_coeffs, vir_coeffs, occ_energy, vir_energy, trial_vectors, shifts):
    s = Sizes(mesh, integrals, occ_coeffs, vir_energy)
    nz, side = s.nz, s.side
    vmem = pltpu.VMEM
    tall = nz * s.pack
    nq8 = s.nq * s.nvec
    rows2 = 2 * s.nq
    scratch = [
        vmem((s.nq, s.window, s.nu), BF16),
        vmem((s.nocc, s.ao), BF16),
        vmem((s.nq, s.nocc, s.nu), F32),
        vmem((s.nq, s.half, s.nu), F32),
        vmem((s.nq, s.half, s.nu), BF16),
        vmem((nz, s.pack, s.nu), F32),
        vmem((nz, s.pack, s.nu), BF16),
        vmem((side, nz, s.pack, s.nu), BF16),
        vmem((side, side, s.rows, s.nu), BF16),
        vmem((side, tall, s.rows), F32),
        vmem((side, tall, s.rows), BF16),
        vmem((side, tall, s.rows), BF16),
        vmem((s.lanes // 128, tall, 128), F32),
        vmem((s.q, s.flat), F32),
        vmem((s.q, s.flat), BF16),
        vmem((s.flat, s.q), BF16),
        vmem((8, s.flat), F32),
        vmem((s.nocc, s.nu), BF16),
        vmem((s.nocc, 128), F32),
        vmem((8, s.lanes), F32),
        vmem((8, 128), F32),
        vmem((nq8, s.half), F32),
        vmem((side, nq8, s.half), F32),
        vmem((side, nq8, s.half), F32),
        vmem((nq8, s.half), F32),
        vmem((2, nz * nq8, s.half), F32),
        vmem((2, s.parts, nz * nq8, 128), F32),
        vmem((s.nvec, s.nocc, s.q), F32),
        vmem((nz, 8, 128), F32),
        vmem((s.nvec, s.nocc, s.q), F32),
        vmem((s.pairs, 2, s.parts, nz * rows2, 128), F32),
        vmem((s.pairs, s.parts, nz * rows2, 128), F32),
        vmem((s.pairs, s.parts, nz * rows2, 128), F32),
        vmem((s.pairs, nz, s.parts, rows2, 128), F32),
        vmem((side, s.pairs, s.parts, rows2, 128), F32),
        vmem((side, s.pairs, s.parts, rows2, 128), F32),
        vmem((nq8, s.nocc), F32),
        vmem((nz, 1, s.nocc), F32),
        vmem((2 * nz, 1, s.nocc), F32),
        vmem((1, s.nocc), F32),
        vmem((side * side, 1, s.nocc), F32),
        vmem((s.nvec, s.nocc), F32),
    ]
    dma = lambda *shape: pltpu.SemaphoreType.DMA(shape)
    near = max(side - 1, 1)
    scratch += [
        dma(s.nq + 1), dma(side), dma(near, side), dma(near, side), dma(nz), dma(nz),
        dma(s.nq), dma(s.nq), dma(nz), dma(nz), dma(near, nz), dma(near, nz),
        dma(near), dma(near), dma(near), dma(near), dma(nz), dma(nz), pltpu.SemaphoreType.DMA, pltpu.SemaphoreType.DMA,
        dma(near), dma(near), dma(s.pairs), dma(s.pairs), dma(s.pairs, nz), dma(s.pairs, nz),
        dma(near), dma(near), dma(near), dma(near), dma(2 * nz), dma(2 * nz), dma(side * side), dma(side * side),
    ]
    hbm = pl.BlockSpec(memory_space=pl.ANY)
    fast = pl.BlockSpec(memory_space=pltpu.VMEM)
    scalars = pl.BlockSpec(memory_space=pltpu.SMEM)
    sigma, sub = pl.pallas_call(
        functools.partial(kernel, s),
        out_shape=(jax.ShapeDtypeStruct((1, s.nocc), F32), jax.ShapeDtypeStruct((s.nvec, 1), F32)),
        in_specs=[hbm, hbm, hbm, fast, fast, scalars, fast, scalars],
        out_specs=(fast, fast),
        scratch_shapes=scratch,
        compiler_params=pltpu.CompilerParams(
            collective_id=0, has_side_effects=True, vmem_limit_bytes=56 * 1024 * 1024
        ),
    )(
        integrals, occ_coeffs.T, vir_coeffs.T, trial_vectors.T, occ_energy[None], occ_energy, vir_energy[None], shifts,
    )
    return sigma.T, sub


def solution(mesh):
    return jax.shard_map(
        functools.partial(local, dict(mesh.shape)),
        mesh=mesh,
        in_specs=(P("aux", "occ", "vir"), P(), P("vir", None), P(), P("vir"), P(), P("aux")),
        out_specs=(P(None, "aux"), P(None, "aux")),
        check_vma=False,
    )
```

```python
import functools
import math

import jax
import jax.numpy as jnp
from jax import lax
from jax.experimental import pallas as pl
from jax.experimental.pallas import tpu as pltpu
from jax.sharding import PartitionSpec as P

MESH = pl.DeviceIdType.MESH
F32 = jnp.float32
BF16 = jnp.bfloat16


def dot(a, b):
    return jnp.dot(a, b, preferred_element_type=F32)


def dot_nt(a, b):
    return lax.dot_general(a, b, (((1,), (1,)), ((), ())), preferred_element_type=F32)


def split(value):
    high = value.astype(BF16)
    low = (value - high.astype(F32)).astype(BF16)
    return jnp.concatenate([high.astype(F32), low.astype(F32)], axis=0).astype(BF16)


def send(src, dst, send_sem, recv_sem, **device):
    copy = pltpu.make_async_remote_copy(
        src_ref=src, dst_ref=dst, send_sem=send_sem, recv_sem=recv_sem, device_id=device, device_id_type=MESH
    )
    copy.start()
    return copy


class Sizes:
    def __init__(self, mesh, integrals, occ_coeffs, vir_energy):
        self.nz = mesh["aux"]
        self.side = math.isqrt(mesh["vir"])
        self.nq, self.mu, self.nu = integrals.shape
        self.ao, self.nocc = occ_coeffs.shape
        self.half = self.nocc // 2
        self.jb = self.half // self.nz
        self.na = vir_energy.shape[0]
        self.block = 16 * (self.na // 16)
        self.rows = self.block + 16
        assert self.na == self.block + 1 and self.side == 4
        first = (self.jb + 1) // 2
        rows = -(-(self.nq * first) // 16) * 16
        self.groups = [(0, first), (first, self.jb - first)]
        rest = self.jb - first
        self.packs = (rows, -(-(self.nq * rest) // 16) * 16)
        self.tile = 512
        self.tiles = -(-(self.jb * self.na) // self.tile)
        self.pairs = self.nz // 2
        self.lane0 = self.mu // 128 * 128
        self.shift = self.mu - self.lane0
        self.window = self.mu + self.shift
        self.lanes = -(-self.rows // 128) * 128
        self.q = self.nq * self.nz
        self.nvec = self.nz
        self.parts = -(-self.half // 128)
        last = 128 * (self.nu * (mesh["vir"] - 1) // 128) - 128
        self.view = self.ao - last
        for v in range(mesh["vir"]):
            start = 128 * (self.nu * v // 128) - 128 * ((v + 1) // mesh["vir"])
            assert start + self.view <= self.ao and self.nu * v - start + self.nu <= self.view


def exchange_kernel(
    s, int_h, occ_h, vir_h, trial, eo_row, eo_s, ve, shift_s,
    bj, bjt, base, rmf, row, hq, sec,
    ibuf, occ_v, pf, xf, pk0, pk1, hs0, hs1, hg0, hg1, vb, acc0, acc1, bs0, bs1, bx0, bx1, bm0, bm1, bf, bflat, eob, ve8, shift,
    rp, rg, rx, rmsg, rall, rl, rm32, sh,
    in_sem, v_own, v_s, v_r, sh_s, sh_r, x_s, x_r, h_s, h_r, g_s, g_r, rg_s, rg_r, rx_s, rx_r, rz_s, rz_r, rc_s, rc_r,
    b_s, b_r, m_s, m_r,
):
    nz, side = s.nz, s.side
    z, c, v = lax.axis_index("aux"), lax.axis_index("occ"), lax.axis_index("vir")
    y, x = v // side, v % side
    g = y + c * (x - y)
    r = x + c * (y - x)
    sg = side - (side - 1) * c
    sr = 1 + (side - 1) * c

    def vid(gather, reduce):
        return gather * sg + reduce * sr

    pk, hs, hg, acc, bs, bx, bm = (pk0, pk1), (hs0, hs1), (hg0, hg1), (acc0, acc1), (bs0, bs1), (bx0, bx1), (bm0, bm1)
    started = []

    def go(*args, **device):
        copy = send(*args, **device)
        started.append(copy)
        return copy

    occ_in = pltpu.make_async_copy(occ_h, occ_v, in_sem.at[s.nq])
    occ_in.start()
    zero_rows = jnp.zeros((s.shift, s.nu), BF16)
    loads = []
    for q in range(s.nq):
        if s.shift:
            ibuf[q, 0 : s.shift, :] = zero_rows
            ibuf[q, s.mu : s.mu + s.shift, :] = zero_rows
        copy = pltpu.make_async_copy(
            int_h.at[q], ibuf.at[q, pl.ds(pl.multiple_of(s.shift * c, 16), s.mu), :], in_sem.at[q]
        )
        copy.start()
        loads.append(copy)
    own_v = []
    for w in range(side):
        start = pl.multiple_of(s.block * vid(g, w), 16)
        copy = pltpu.make_async_copy(vir_h.at[pl.ds(start, s.rows), :], vb.at[0, w], v_own.at[w])
        copy.start()
        own_v.append(copy)

    for group in range(2):
        pk[group][...] = jnp.zeros(pk[group].shape, F32)

    barrier = pltpu.get_barrier_semaphore()
    pl.semaphore_signal(barrier, inc=1, device_id={"occ": 1 - c}, device_id_type=MESH)
    for d in range(1, nz):
        pl.semaphore_signal(barrier, inc=1, device_id={"aux": (z + d) % nz}, device_id_type=MESH)
    for d in range(1, side):
        pl.semaphore_signal(barrier, inc=1, device_id={"vir": vid((g + d) % side, r)}, device_id_type=MESH)
        pl.semaphore_signal(barrier, inc=1, device_id={"vir": vid(g, (r + d) % side)}, device_id_type=MESH)
    pl.semaphore_wait(barrier, nz + 2 * side - 2)

    v_copies = {}
    for e in range(1, side):
        to = (g + e) % side
        for w in range(side):
            start = pl.multiple_of(s.block * vid(to, w), 16)
            v_copies[side - e, w] = go(
                vir_h.at[pl.ds(start, s.rows), :], vb.at[side - e, w], v_s.at[e - 1, w], v_r.at[side - e - 1, w],
                vir=vid(to, r),
            )
    shift[...] = jnp.full((8, 128), shift_s[0], F32)
    for e in range(1, nz):
        go(shift, sh.at[z], sh_s.at[e - 1], sh_r.at[z], aux=(z + e) % nz)
    sh[z] = shift[...]

    occ_in.wait()
    x_copies = []
    for q in range(s.nq):
        loads[q].wait()
        columns = occ_v[:, pl.ds(pl.multiple_of(s.lane0 * c, 128), s.window)]
        pf[q] = dot(columns, ibuf[q])
        x_copies.append(
            go(pf.at[q, pl.ds(pl.multiple_of(s.half * (1 - c), 8), s.half), :], xf.at[q], x_s.at[q], x_r.at[q], occ=1 - c)
        )
    start = 128 * ((s.nu * v) // 128) - 128 * ((v + 1) // (side * side))
    view = occ_v[:, pl.ds(pl.multiple_of(start, 128), s.view)].astype(F32)
    wide = -(-s.view // 128) * 128
    view = jnp.concatenate([view, jnp.zeros((s.nocc, wide - s.view), F32)], axis=1)
    sec[...] = pltpu.roll(view, wide - (s.nu * v - start), 1)[:, : s.nu].astype(BF16)
    weights = split(dot(trial[...], sec[...]))
    for q in range(s.nq):
        x_copies[q].wait_recv()
        xf[q] = xf[q] + pf[q, pl.ds(pl.multiple_of(s.half * c, 8), s.half), :]
    near_first = [d for pair in zip(range(1, nz // 2), range(nz - 1, nz // 2, -1)) for d in pair] + [nz // 2]
    for group in range(2):
        j0, count = s.groups[group]
        for q in range(s.nq):
            for to in range(nz):
                pk[group][to, q * count : (q + 1) * count, :] = xf[q, to * s.jb + j0 : to * s.jb + j0 + count, :]
        hs[group][...] = pk[group][...].astype(BF16)
        for e in near_first:
            to = (z + e) % nz
            go(hs[group].at[to], hg[group].at[0, z], h_s.at[group, e - 1], h_r.at[group, z], aux=to)
        hg[group][0, z] = hs[group][z]
    for q in range(s.nq):
        hq[q] = xf[q].astype(BF16)

    for q in range(s.nq):
        both = dot_nt(weights, hq[q])
        rp[q * s.nvec : (q + 1) * s.nvec, :] = both[: s.nvec] + both[s.nvec :]
    for e in range(1, side):
        go(rp, rg.at[side - e], rg_s.at[e - 1], rg_r.at[side - e - 1], vir=vid((g + e) % side, r))

    ve8[...] = jnp.ones(ve8.shape, F32)
    ve8[:, 0 : s.na] = jnp.broadcast_to(ve[...], (8, s.na))
    bflat[...] = jnp.ones(bflat.shape, F32)
    first = s.half * c + s.jb * z
    for j in range(s.jb):
        bflat[0:8, j * s.na : (j + 1) * s.na] = ve8[:, 0 : s.na] - eo_s[first + j]
    for tile in range(s.tiles):
        base[tile] = bflat[0:8, tile * s.tile : (tile + 1) * s.tile]
    square = jnp.broadcast_to(eo_row[...], (128, s.nocc))
    fill = -(-s.nocc // 128) * 128 - s.nocc
    eob[...] = jnp.concatenate([square, jnp.zeros((128, fill), F32)], axis=1).T[: s.nocc]

    def arrived(dst, recv_sem):
        pltpu.make_async_remote_copy(
            src_ref=dst, dst_ref=dst, send_sem=recv_sem, recv_sem=recv_sem, device_id={"occ": c}, device_id_type=MESH
        ).wait_recv()

    ahead, behind = vid((g + 1) % side, r), vid((g + 3) % side, r)
    order = [0] + near_first

    def relay(group, k):
        source = (z + order[k]) % nz
        slot, to = (1, behind) if k % 2 == 0 else (3, ahead)
        arrived(hg[group].at[slot, source], g_r.at[group, slot - 1, source])
        go(hg[group].at[slot, source], hg[group].at[2, source], g_s.at[group, 2, k], g_r.at[group, 1, source], vir=to)

    def gather(group, steps):
        for k in steps:
            source = (z + order[k]) % nz
            if k:
                arrived(hg[group].at[0, source], h_r.at[group, source])
            go(hg[group].at[0, source], hg[group].at[3, source], g_s.at[group, 0, k], g_r.at[group, 2, source], vir=ahead)
            go(hg[group].at[0, source], hg[group].at[1, source], g_s.at[group, 1, k], g_r.at[group, 0, source], vir=behind)
            if k >= 2:
                relay(group, k - 2)

    def gathered(group, slot):
        for k in range(nz):
            if (slot, k % 2) not in ((1, 0), (3, 1)):
                source = (z + order[k]) % nz
                arrived(hg[group].at[slot, source], g_r.at[group, slot - 1, source])

    def term(group, d, w):
        return dot_nt(hg[group][d].reshape(nz * s.packs[group], s.nu), vb[d, w])

    def product(group, d):
        @pl.loop(0, side)
        def _(w):
            value = term(group, d, w)
            acc[group][w] = value if d == 0 else value + acc[group][w]

    right, left = vid(g, (r + 1) % side), vid(g, (r + 3) % side)

    def parts_of(group):
        size = nz * s.packs[group] // 2
        return pl.ds(0, size), pl.ds(size, size)

    def reduce_start(group, d):
        low, high = parts_of(group)
        for e in (2, 1, 3, 0):
            w = (r + e) % side
            value = acc[group][w] + term(group, d, w)
            acc[group][w] = value
            if e:
                bs[group][e - 1] = value.astype(BF16)
            if e == 2:
                go(bs[group].at[1, low], bm[group].at[0], m_s.at[group, 0], m_r.at[group, 0], vir=right)
                go(bs[group].at[1, high], bm[group].at[1], m_s.at[group, 1], m_r.at[group, 1], vir=left)
            if e == 1:
                go(bs[group].at[0, high], bx[group].at[0, high], b_s.at[group, 0, 1], b_r.at[group, 0, 1], vir=right)
            if e == 3:
                go(bs[group].at[2, low], bx[group].at[1, low], b_s.at[group, 1, 0], b_r.at[group, 1, 0], vir=left)

    def reduce_merge(group):
        low, high = parts_of(group)
        arrived(bm[group].at[0], m_r.at[group, 0])
        merged = acc[group][(r + 1) % side, low, :] + bm[group][0].astype(F32)
        bs[group][0, low, :] = merged.astype(BF16)
        go(bs[group].at[0, low], bx[group].at[0, low], b_s.at[group, 0, 0], b_r.at[group, 0, 0], vir=right)
        arrived(bm[group].at[1], m_r.at[group, 1])
        merged = acc[group][(r + 3) % side, high, :] + bm[group][1].astype(F32)
        bs[group][2, high, :] = merged.astype(BF16)
        go(bs[group].at[2, high], bx[group].at[1, high], b_s.at[group, 1, 1], b_r.at[group, 1, 1], vir=left)

    gather(0, range(nz))
    total = rp[...]
    for d in range(1, side):
        arrived(rg.at[d], rg_r.at[d - 1])
        total = total + rg[d]
    rx[0] = total
    for e in range(1, side):
        go(rx.at[0], rx.at[side - e], rx_s.at[e - 1], rx_r.at[side - e - 1], vir=vid(g, (r + e) % side))
    relay(0, nz - 2)
    relay(0, nz - 1)
    for w in range(side):
        own_v[w].wait()
    product(0, 0)
    total = rx[0]
    for d in range(1, side):
        arrived(rx.at[d], rx_r.at[d - 1])
        total = total + rx[d]
    rmsg[...] = total
    nq8 = s.nq * s.nvec
    for e in range(1, nz):
        go(
            rmsg, rall.at[c, pl.ds(pl.multiple_of(z * nq8, 8), nq8), :], rz_s.at[e - 1], rz_r.at[z], aux=(z + e) % nz,
        )
    rall[c, pl.ds(pl.multiple_of(z * nq8, 8), nq8), :] = total
    gather(1, range(3))
    for d in (1, 3):
        gathered(0, d)
        for w in range(side):
            v_copies[d, w].wait_recv()
        product(0, d)
        gather(1, range(3, 5) if d == 1 else range(5, 6))
    gathered(0, 2)
    for w in range(side):
        v_copies[2, w].wait_recv()
    reduce_start(0, 2)
    gather(1, range(6, nz))
    relay(1, nz - 2)
    relay(1, nz - 1)
    product(1, 0)
    reduce_merge(0)
    for d in (1, 3):
        gathered(1, d)
        product(1, d)
    gathered(1, 2)
    reduce_start(1, 2)
    for d in range(1, nz):
        source = (z + d) % nz
        arrived(rall.at[c, pl.ds(pl.multiple_of(source * nq8, 8), nq8), :], rz_r.at[source])
        arrived(sh.at[source], sh_r.at[source])
    go(rall.at[c], rall.at[c], rc_s, rc_r, occ=1 - c)
    reduce_merge(1)
    arrived(rall.at[1 - c], rc_r)
    for h in range(2):
        for part in range(s.parts):
            width = min(128, s.half - part * 128)
            rl[h, part, :, 0:width] = rall[h, :, part * 128 : part * 128 + width]
    for n in range(s.nvec):
        for h in range(2):
            halves = []
            for part in range(s.parts):
                rows = [rl[h, part, pl.ds(q * s.nvec + n, nz, stride=nq8), :] for q in range(s.nq)]
                halves.append(jnp.concatenate(rows, axis=0))
            rm32[n, h * s.half : (h + 1) * s.half, :] = jnp.concatenate(halves, axis=1).T[: s.half]
        rmf[n * s.nocc : (n + 1) * s.nocc, :] = rm32[n].astype(BF16)

    def build(group):
        j0, count = s.groups[group]
        pack = s.packs[group]
        for side_of in range(2):
            for part, rows in enumerate(parts_of(group)):
                arrived(bx[group].at[side_of, rows], b_r.at[group, side_of, part])

        @pl.loop(0, nz)
        def _(source):
            rows = pl.ds(pl.multiple_of(source * pack, 16), pack)
            value = acc[group][r, rows, :] + bx[group][0, rows, :].astype(F32) + bx[group][1, rows, :].astype(F32)
            value = value.astype(BF16).astype(F32)
            full = jnp.concatenate([value, jnp.zeros((pack, s.lanes - s.rows), F32)], axis=1)
            full = pltpu.roll(full, s.lanes - v, 1)
            for part in range(s.lanes // 128):
                bf[part, rows, :] = full[:, part * 128 : (part + 1) * 128]

        for j in range(count):
            parts = []
            for part in range(s.lanes // 128):
                rows = [bf[part, pl.ds(q * count + j, nz, stride=pack), :] for q in range(s.nq)]
                parts.append(jnp.concatenate(rows, axis=0))
            bflat[:, (j0 + j) * s.na : (j0 + j + 1) * s.na] = jnp.concatenate(parts, axis=1)[:, : s.na]

    bflat[:, s.tiles * s.tile - 128 :] = jnp.zeros((s.q, 128), F32)
    build(0)
    build(1)
    for tile in range(s.tiles):
        flat = bflat[:, tile * s.tile : (tile + 1) * s.tile]
        bj[tile] = flat.astype(BF16)
        bjt[tile] = flat.T.astype(BF16)
    for n in range(s.nvec):
        row[n * s.nocc : (n + 1) * s.nocc, :] = jnp.broadcast_to(sh[n][0:1, :], (s.nocc, 128)) - eob[...]
    for copy in started:
        copy.wait_send()


def fold_kernel(s, bj, bjt, base, rm, row, fl, fa, coupled0, coupled1, weighted0, weighted1):
    nz, tall = s.nz, 2 * s.nocc
    coupled, weighted = (coupled0, coupled1), (weighted0, weighted1)
    steps = s.pairs * s.tiles

    def couple(step, slot):
        rows = rm[pl.ds(pl.multiple_of(step // s.tiles * tall, 16), tall), :]
        coupled[slot][...] = dot(rows, bj[step % s.tiles])

    def weigh(step, slot):
        own = row[pl.ds(pl.multiple_of(step // s.tiles * tall, 8), tall), :]
        divisor = jnp.concatenate([own] * (s.tile // 128), axis=1) + base[step % s.tiles, 0:1, :]
        weighted[slot][...] = (coupled[slot][...] * pl.reciprocal(divisor, approx=True, full_range=False)).astype(BF16)

    def gather(step, slot):
        rows = pl.ds(pl.multiple_of(step // s.tiles * tall, 8), tall)
        fa[rows, :] += dot(weighted[slot][...], bjt[step % s.tiles])

    fa[...] = jnp.zeros(fa.shape, F32)
    couple(0, 0)
    couple(1, 1)
    weigh(0, 0)

    @pl.loop(1, steps // 2)
    def _(half):
        for slot in range(2):
            step = 2 * half + slot
            gather(step - 2, slot)
            weigh(step - 1, 1 - slot)
            couple(step, slot)

    gather(steps - 2, 0)
    weigh(steps - 1, 1)
    gather(steps - 1, 1)
    rows2 = 2 * s.nq

    @pl.loop(0, s.pairs)
    def _(p):
        for m in range(2):
            for h in range(2):
                start = pl.multiple_of(p * tall, 8) + m * s.nocc + h * s.half
                flip = fa[pl.ds(start, s.half), :].T
                flip = jnp.concatenate([flip, jnp.zeros((s.q, s.parts * 128 - s.half), F32)], axis=1)
                for part in range(s.parts):
                    for q in range(s.nq):
                        fl[p, h, part, pl.ds(m * s.nq + q, nz, stride=rows2), :] = flip[
                            q * nz : (q + 1) * nz, part * 128 : (part + 1) * 128
                        ]


def collect_kernel(
    s, fl, hq, sec, trial, eo_row, out,
    fx, fz, fr, fg, fgx, spart, sgs, sgr, spp, spr, t32,
    fc_s, fc_r, fz_s, fz_r, fg_s, fg_r, fx_s, fx_r, s1_s, s1_r, s2_s, s2_r,
):
    nz, side = s.nz, s.side
    z, c, v = lax.axis_index("aux"), lax.axis_index("occ"), lax.axis_index("vir")
    y, x = v // side, v % side
    g = y + c * (x - y)
    r = x + c * (y - x)
    sg = side - (side - 1) * c
    sr = 1 + (side - 1) * c

    def vid(gather, reduce):
        return gather * sg + reduce * sr

    started = []

    def go(*args, **device):
        copy = send(*args, **device)
        started.append(copy)
        return copy

    def arrived(dst, recv_sem):
        pltpu.make_async_remote_copy(
            src_ref=dst, dst_ref=dst, send_sem=recv_sem, recv_sem=recv_sem, device_id={"occ": c}, device_id_type=MESH
        ).wait_recv()

    barrier = pltpu.get_barrier_semaphore()
    me = 2 * z + c
    for d in range(1, 2 * nz):
        other = (me + d) % (2 * nz)
        pl.semaphore_signal(barrier, inc=1, device_id={"aux": other // 2, "occ": other % 2}, device_id_type=MESH)
    for d in range(1, side * side):
        pl.semaphore_signal(barrier, inc=1, device_id={"vir": (v + d) % (side * side)}, device_id_type=MESH)
    pl.semaphore_wait(barrier, 2 * nz + side * side - 2)
    t32[...] = trial[...].astype(F32)

    rows2 = 2 * s.nq
    go(fl.at[:, 1 - c], fx, fc_s, fc_r, occ=1 - c)
    arrived(fx, fc_r)
    fz[...] = fl[:, c] + fx[...]
    for d in range(1, nz):
        to = (z + d) % nz
        go(fz.at[:, :, pl.ds(pl.multiple_of(to * rows2, 8), rows2), :], fr.at[z], fz_s.at[d - 1], fz_r.at[z], aux=to)
    total = fz[:, :, pl.ds(pl.multiple_of(z * rows2, 8), rows2), :]
    for d in range(1, nz):
        source = (z + d) % nz
        arrived(fr.at[source], fz_r.at[source])
        total = total + fr[source]
    fg[0] = total
    for e in range(1, side):
        go(fg.at[0], fg.at[side - e], fg_s.at[e - 1], fg_r.at[side - e - 1], vir=vid((g + e) % side, r))
    total = fg[0]
    for d in range(1, side):
        arrived(fg.at[d], fg_r.at[d - 1])
        total = total + fg[d]
    fgx[0] = total
    for e in range(1, side):
        go(fgx.at[0], fgx.at[side - e], fx_s.at[e - 1], fx_r.at[side - e - 1], vir=vid(g, (r + e) % side))
    for d in range(1, side):
        arrived(fgx.at[d], fx_r.at[d - 1])
        total = total + fgx[d]

    tall = s.nvec * s.nq
    folded = jnp.concatenate([total[:, part].reshape(tall, 128) for part in range(s.parts)], axis=1)[:, : s.half]
    folded = split(folded)
    owner = lax.broadcasted_iota(jnp.int32, folded.shape, 0) % s.nq
    both = None
    for q in range(s.nq):
        term = dot(jnp.where(owner == q, folded.astype(F32), 0.0).astype(BF16), hq[q])
        both = term if both is None else both + term
    both = dot_nt(split(both[:tall] + both[tall:]), sec[...])
    spart[...] = both[:tall] + both[tall:]
    for n in range(s.nvec):
        value = spart[n * s.nq : n * s.nq + 1, :]
        for q in range(1, s.nq):
            value = value + spart[n * s.nq + q : n * s.nq + q + 1, :]
        sgs[n] = value
    for d in range(1, 2 * nz):
        other = (me + d) % (2 * nz)
        go(sgs.at[other // 2], sgr.at[me], s1_s.at[d - 1], s1_r.at[me], aux=other // 2, occ=other % 2)
    sgr[me] = sgs[z]
    for d in range(1, 2 * nz):
        other = (me + d) % (2 * nz)
        arrived(sgr.at[other], s1_r.at[other])
    total = sgr[0]
    for d in range(1, 2 * nz):
        total = total + sgr[d]
    spp[...] = total
    for d in range(1, side * side):
        go(spp, spr.at[v], s2_s.at[d - 1], s2_r.at[v], vir=(v + d) % (side * side))
    spr[v] = total
    for d in range(1, side * side):
        other = (v + d) % (side * side)
        arrived(spr.at[other], s2_r.at[other])
    total = spr[0]
    for d in range(1, side * side):
        total = total + spr[d]
    sigma = eo_row[...] * t32[pl.ds(z, 1), :] + total
    out[:, 0 : s.nocc] = sigma
    column = jnp.sum(t32[...] * sigma, axis=1, keepdims=True)
    out[:, s.nocc : s.nocc + s.nvec] = jnp.broadcast_to(column, (s.nvec, 128)).T[0:1]
    for copy in started:
        copy.wait_send()


def local(mesh, integrals, occ_coeffs, vir_coeffs, occ_energy, vir_energy, trial_vectors, shifts):
    s = Sizes(mesh, integrals, occ_coeffs, vir_energy)
    nz, side = s.nz, s.side
    vmem = pltpu.VMEM
    nq8 = s.nq * s.nvec
    rows2 = 2 * s.nq
    dma = lambda *shape: pltpu.SemaphoreType.DMA(shape)
    near = side - 1
    one = pltpu.SemaphoreType.DMA
    scratch = [
        vmem((s.nq, s.window, s.nu), BF16),
        vmem((s.nocc, s.ao), BF16),
        vmem((s.nq, s.nocc, s.nu), F32),
        vmem((s.nq, s.half, s.nu), F32),
        *[vmem((nz, pack, s.nu), F32) for pack in s.packs],
        *[vmem((nz, pack, s.nu), BF16) for pack in s.packs],
        *[vmem((side, nz, pack, s.nu), BF16) for pack in s.packs],
        vmem((side, side, s.rows, s.nu), BF16),
        *[vmem((side, nz * pack, s.rows), F32) for pack in s.packs],
        *[vmem((side - 1, nz * pack, s.rows), BF16) for pack in s.packs],
        *[vmem((2, nz * pack, s.rows), BF16) for pack in s.packs],
        *[vmem((2, nz * pack // 2, s.rows), BF16) for pack in s.packs],
        vmem((s.lanes // 128, nz * max(s.packs), 128), F32),
        vmem((s.q, s.tiles * s.tile), F32),
        vmem((s.nocc, 128), F32),
        vmem((8, s.lanes), F32),
        vmem((8, 128), F32),
        vmem((nq8, s.half), F32),
        vmem((side, nq8, s.half), F32),
        vmem((side, nq8, s.half), F32),
        vmem((nq8, s.half), F32),
        vmem((2, nz * nq8, s.half), F32),
        vmem((2, s.parts, nz * nq8, 128), F32),
        vmem((s.nvec, s.nocc, s.q), F32),
        vmem((nz, 8, 128), F32),
        dma(s.nq + 1), dma(side), dma(near, side), dma(near, side), dma(nz), dma(nz),
        dma(s.nq), dma(s.nq), dma(2, nz), dma(2, nz), dma(2, near, nz), dma(2, near, nz),
        dma(near), dma(near), dma(near), dma(near), dma(nz), dma(nz), one, one,
        dma(2, 2, 2), dma(2, 2, 2), dma(2, 2), dma(2, 2),
    ]
    hbm = pl.BlockSpec(memory_space=pl.ANY)
    fast = pl.BlockSpec(memory_space=pltpu.VMEM)
    scalars = pl.BlockSpec(memory_space=pltpu.SMEM)
    shape = jax.ShapeDtypeStruct
    limit = 56 * 1024 * 1024
    occ_row, trial_rows = occ_energy[None], trial_vectors.T
    bj, bjt, base, rm, row, hq, sec = pl.pallas_call(
        functools.partial(exchange_kernel, s),
        out_shape=(
            shape((s.tiles, s.q, s.tile), BF16),
            shape((s.tiles, s.tile, s.q), BF16),
            shape((s.tiles, 8, s.tile), F32),
            shape((s.nvec * s.nocc, s.q), BF16),
            shape((s.nvec * s.nocc, 128), F32),
            shape((s.nq, s.half, s.nu), BF16),
            shape((s.nocc, s.nu), BF16),
        ),
        in_specs=[hbm, hbm, hbm, fast, fast, scalars, fast, scalars],
        out_specs=(fast,) * 7,
        scratch_shapes=scratch,
        compiler_params=pltpu.CompilerParams(collective_id=0, has_side_effects=True, vmem_limit_bytes=limit),
    )(integrals, occ_coeffs.T, vir_coeffs.T, trial_rows, occ_row, occ_energy, vir_energy[None], shifts)
    tall = 2 * s.nocc
    folded = pl.pallas_call(
        functools.partial(fold_kernel, s),
        out_shape=shape((s.pairs, 2, s.parts, nz * rows2, 128), F32),
        in_specs=[fast] * 5,
        out_specs=fast,
        scratch_shapes=[
            vmem((s.nvec * s.nocc, s.q), F32),
            vmem((tall, s.tile), F32),
            vmem((tall, s.tile), F32),
            vmem((tall, s.tile), BF16),
            vmem((tall, s.tile), BF16),
        ],
        compiler_params=pltpu.CompilerParams(vmem_limit_bytes=limit),
    )(bj, bjt, base, rm, row)
    out = pl.pallas_call(
        functools.partial(collect_kernel, s),
        out_shape=shape((1, s.nocc + s.nvec), F32),
        in_specs=[fast] * 5,
        out_specs=fast,
        scratch_shapes=[
            vmem((s.pairs, s.parts, nz * rows2, 128), F32),
            vmem((s.pairs, s.parts, nz * rows2, 128), F32),
            vmem((nz, s.pairs, s.parts, rows2, 128), F32),
            vmem((side, s.pairs, s.parts, rows2, 128), F32),
            vmem((side, s.pairs, s.parts, rows2, 128), F32),
            vmem((nq8, s.nocc), F32),
            vmem((nz, 1, s.nocc), F32),
            vmem((2 * nz, 1, s.nocc), F32),
            vmem((1, s.nocc), F32),
            vmem((side * side, 1, s.nocc), F32),
            vmem((s.nvec, s.nocc), F32),
            one, one, dma(nz), dma(nz), dma(near), dma(near), dma(near), dma(near),
            dma(2 * nz), dma(2 * nz), dma(side * side), dma(side * side),
        ],
        compiler_params=pltpu.CompilerParams(collective_id=1, has_side_effects=True, vmem_limit_bytes=limit),
    )(folded, hq, sec, trial_rows, occ_row)
    return out[:, : s.nocc].T, out[:, s.nocc :].T


def solution(mesh):
    return jax.shard_map(
        functools.partial(local, dict(mesh.shape)),
        mesh=mesh,
        in_specs=(P("aux", "occ", "vir"), P(), P("vir", None), P(), P("vir"), P(), P("aux")),
        out_specs=(P(None, "aux"), P(None, "aux")),
        check_vma=False,
    )
```

```python
import functools
import math

import jax
import jax.numpy as jnp
from jax import lax
from jax.experimental import pallas as pl
from jax.experimental.pallas import tpu as pltpu
from jax.sharding import PartitionSpec as P

MESH = pl.DeviceIdType.MESH
F32 = jnp.float32
BF16 = jnp.bfloat16


def dot(a, b):
    return jnp.dot(a, b, preferred_element_type=F32)


def dot_nt(a, b):
    return lax.dot_general(a, b, (((1,), (1,)), ((), ())), preferred_element_type=F32)


def split(value):
    high = value.astype(BF16)
    low = (value - high.astype(F32)).astype(BF16)
    return jnp.concatenate([high.astype(F32), low.astype(F32)], axis=0).astype(BF16)


def send(src, dst, send_sem, recv_sem, **device):
    copy = pltpu.make_async_remote_copy(
        src_ref=src, dst_ref=dst, send_sem=send_sem, recv_sem=recv_sem, device_id=device, device_id_type=MESH
    )
    copy.start()
    return copy


class Sizes:
    def __init__(self, mesh, integrals, occ_coeffs, vir_energy):
        self.nz = mesh["aux"]
        self.side = math.isqrt(mesh["vir"])
        self.nq, self.mu, self.nu = integrals.shape
        self.ao, self.nocc = occ_coeffs.shape
        self.half = self.nocc // 2
        self.jb = self.half // self.nz
        self.na = vir_energy.shape[0]
        self.block = 16 * (self.na // 16)
        self.rows = self.block + 16
        assert self.na == self.block + 1 and self.side == 4
        first = (self.jb + 1) // 2
        rows = -(-(self.nq * first) // 16) * 16
        self.groups = [(0, first), (first, self.jb - first)]
        rest = self.jb - first
        self.packs = (rows, -(-(self.nq * rest) // 16) * 16)
        self.tile = 512
        self.tiles = -(-(self.jb * self.na) // self.tile)
        self.early = first * self.na // self.tile
        self.pairs = self.nz // 2
        self.lane0 = self.mu // 128 * 128
        self.shift = self.mu - self.lane0
        self.window = self.mu + self.shift
        self.lanes = -(-self.rows // 128) * 128
        self.q = self.nq * self.nz
        self.nvec = self.nz
        self.parts = -(-self.half // 128)
        last = 128 * (self.nu * (mesh["vir"] - 1) // 128) - 128
        self.view = self.ao - last
        for v in range(mesh["vir"]):
            start = 128 * (self.nu * v // 128) - 128 * ((v + 1) // mesh["vir"])
            assert start + self.view <= self.ao and self.nu * v - start + self.nu <= self.view


def kernel(
    s, int_h, occ_h, vir_h, trial, eo_row, eo_s, ve, shift_s,
    out,
    bj, bjt, base, rm, row, hq, sec, fa, coupled0, coupled1, weighted0, weighted1,
    fl, fx, fz, fr, fg, fgx, spart, sgs, sgr, spp, spr,
    ibuf, occ_v, pf, xf, pk0, pk1, hs0, hs1, hg0, hg1, vb, acc0, acc1, bs0, bs1, bx0, bx1, bm0, bm1, bf, bflat, eob, ve8, shift,
    rp, rg, rx, rmsg, rall, rl, rm32, sh,
    in_sem, v_own, v_s, v_r, sh_s, sh_r, x_s, x_r, h_s, h_r, g_s, g_r, rg_s, rg_r, rx_s, rx_r, rz_s, rz_r, rc_s, rc_r,
    b_s, b_r, m_s, m_r, fc_s, fc_r, fz_s, fz_r, fg_s, fg_r, fx_s, fx_r, s1_s, s1_r, s2_s, s2_r,
):
    nz, side = s.nz, s.side
    z, c, v = lax.axis_index("aux"), lax.axis_index("occ"), lax.axis_index("vir")
    y, x = v // side, v % side
    g = y + c * (x - y)
    r = x + c * (y - x)
    sg = side - (side - 1) * c
    sr = 1 + (side - 1) * c

    def vid(gather, reduce):
        return gather * sg + reduce * sr

    pk, hs, hg, acc, bs, bx, bm = (pk0, pk1), (hs0, hs1), (hg0, hg1), (acc0, acc1), (bs0, bs1), (bx0, bx1), (bm0, bm1)
    started = []

    def go(*args, **device):
        copy = send(*args, **device)
        started.append(copy)
        return copy

    occ_in = pltpu.make_async_copy(occ_h, occ_v, in_sem.at[s.nq])
    occ_in.start()
    zero_rows = jnp.zeros((s.shift, s.nu), BF16)
    loads = []
    for q in range(s.nq):
        if s.shift:
            ibuf[q, 0 : s.shift, :] = zero_rows
            ibuf[q, s.mu : s.mu + s.shift, :] = zero_rows
        copy = pltpu.make_async_copy(
            int_h.at[q], ibuf.at[q, pl.ds(pl.multiple_of(s.shift * c, 16), s.mu), :], in_sem.at[q]
        )
        copy.start()
        loads.append(copy)
    own_v = []
    for w in range(side):
        start = pl.multiple_of(s.block * vid(g, w), 16)
        copy = pltpu.make_async_copy(
            vir_h.at[pl.ds(start, s.rows), :], vb.at[0, pl.ds(w * s.lanes, s.rows), :], v_own.at[w]
        )
        copy.start()
        own_v.append(copy)

    for group in range(2):
        pk[group][...] = jnp.zeros(pk[group].shape, F32)
    rp[...] = jnp.zeros(rp.shape, F32)
    for d in range(side):
        for w in range(side):
            vb[d, w * s.lanes + s.rows : (w + 1) * s.lanes, :] = jnp.zeros((s.lanes - s.rows, s.nu), BF16)

    barrier = pltpu.get_barrier_semaphore()
    me = 2 * z + c
    for d in range(1, 2 * nz):
        other = (me + d) % (2 * nz)
        pl.semaphore_signal(barrier, inc=1, device_id={"aux": other // 2, "occ": other % 2}, device_id_type=MESH)
    for d in range(1, side * side):
        pl.semaphore_signal(barrier, inc=1, device_id={"vir": (v + d) % (side * side)}, device_id_type=MESH)
    pl.semaphore_wait(barrier, 2 * nz + side * side - 2)

    v_copies = {}
    for e in range(1, side):
        to = (g + e) % side
        for w in range(side):
            start = pl.multiple_of(s.block * vid(to, w), 16)
            v_copies[side - e, w] = go(
                vir_h.at[pl.ds(start, s.rows), :], vb.at[side - e, pl.ds(w * s.lanes, s.rows), :], v_s.at[e - 1, w], v_r.at[side - e - 1, w],
                vir=vid(to, r),
            )
    shift[...] = jnp.full((8, 128), shift_s[0], F32)
    for e in range(1, nz):
        go(shift, sh.at[z], sh_s.at[e - 1], sh_r.at[z], aux=(z + e) % nz)
    sh[z] = shift[...]

    occ_in.wait()
    x_copies = []
    for q in range(s.nq):
        loads[q].wait()
        columns = occ_v[:, pl.ds(pl.multiple_of(s.lane0 * c, 128), s.window)]
        pf[q] = dot(columns, ibuf[q])
        x_copies.append(
            go(pf.at[q, pl.ds(pl.multiple_of(s.half * (1 - c), 8), s.half), :], xf.at[q], x_s.at[q], x_r.at[q], occ=1 - c)
        )
    start = 128 * ((s.nu * v) // 128) - 128 * ((v + 1) // (side * side))
    view = occ_v[:, pl.ds(pl.multiple_of(start, 128), s.view)].astype(F32)
    wide = -(-s.view // 128) * 128
    view = jnp.concatenate([view, jnp.zeros((s.nocc, wide - s.view), F32)], axis=1)
    sec[...] = pltpu.roll(view, wide - (s.nu * v - start), 1)[:, : s.nu].astype(BF16)
    weights = split(dot(trial[...], sec[...]))
    for q in range(s.nq):
        x_copies[q].wait_recv()
        xf[q] = xf[q] + pf[q, pl.ds(pl.multiple_of(s.half * c, 8), s.half), :]
    near_first = [d for pair in zip(range(1, nz // 2), range(nz - 1, nz // 2, -1)) for d in pair] + [nz // 2]
    for group in range(2):
        j0, count = s.groups[group]
        for q in range(s.nq):
            for to in range(nz):
                pk[group][to, q * count : (q + 1) * count, :] = xf[q, to * s.jb + j0 : to * s.jb + j0 + count, :]
        hs[group][...] = pk[group][...].astype(BF16)
        for e in near_first:
            to = (z + e) % nz
            go(hs[group].at[to], hg[group].at[0, z], h_s.at[group, e - 1], h_r.at[group, z], aux=to)
        hg[group][0, z] = hs[group][z]
    for q in range(s.nq):
        hq[q] = xf[q].astype(BF16)

    for q in range(s.nq):
        both = dot_nt(weights, hq[q])
        rp[q * s.nvec : (q + 1) * s.nvec, 0 : s.half] = both[: s.nvec] + both[s.nvec :]
    for e in range(1, side):
        go(rp, rg.at[side - e], rg_s.at[e - 1], rg_r.at[side - e - 1], vir=vid((g + e) % side, r))

    ve8[...] = jnp.ones(ve8.shape, F32)
    ve8[:, 0 : s.na] = jnp.broadcast_to(ve[...], (8, s.na))
    bflat[...] = jnp.ones(bflat.shape, F32)
    first = s.half * c + s.jb * z
    for j in range(s.jb):
        bflat[0:8, j * s.na : (j + 1) * s.na] = ve8[:, 0 : s.na] - eo_s[first + j]
    for tile in range(s.tiles):
        base[tile] = bflat[0:8, tile * s.tile : (tile + 1) * s.tile]
    square = jnp.broadcast_to(eo_row[...], (128, s.nocc))
    fill = -(-s.nocc // 128) * 128 - s.nocc
    eob[...] = jnp.concatenate([square, jnp.zeros((128, fill), F32)], axis=1).T[: s.nocc]

    def arrived(dst, recv_sem):
        pltpu.make_async_remote_copy(
            src_ref=dst, dst_ref=dst, send_sem=recv_sem, recv_sem=recv_sem, device_id={"occ": c}, device_id_type=MESH
        ).wait_recv()

    ahead, behind = vid((g + 1) % side, r), vid((g + 3) % side, r)
    halves = (pl.ds(0, nz // 2), pl.ds(nz // 2, nz // 2))

    def gather(group):
        for d in near_first:
            source = (z + d) % nz
            arrived(hg[group].at[0, source], h_r.at[group, source])
        for n in range(2):
            for to, slot, part in ((behind, 1, n), (ahead, 3, 1 - n)):
                part_ref = hg[group].at[0, halves[part]]
                go(
                    part_ref, hg[group].at[slot, halves[part]], g_s.at[group, slot - 1, part], g_r.at[group, slot - 1, part],
                    vir=to,
                )

    def relay(group):
        for slot, to, part in ((1, behind, 0), (3, ahead, 1)):
            arrived(hg[group].at[slot, halves[part]], g_r.at[group, slot - 1, part])
            go(
                hg[group].at[slot, halves[part]], hg[group].at[2, halves[part]], g_s.at[group, 1, part],
                g_r.at[group, 1, part], vir=to,
            )

    def gathered(group, slot):
        for part in range(2):
            if (slot, part) not in ((1, 0), (3, 1)):
                arrived(hg[group].at[slot, halves[part]], g_r.at[group, slot - 1, part])

    def term(group, d):
        return dot_nt(hg[group][d].reshape(nz * s.packs[group], s.nu), vb[d])

    def product(group, slots):
        value = term(group, slots[0])
        for d in slots[1:]:
            value = value + term(group, d)
        acc[group][...] = value if slots[0] == 0 else value + acc[group][...]

    def columns_of(w):
        return pl.ds(pl.multiple_of(w * s.lanes, 128), s.lanes)

    right, left = vid(g, (r + 1) % side), vid(g, (r + 3) % side)

    def parts_of(group):
        size = nz * s.packs[group] // 2
        return pl.ds(0, size), pl.ds(size, size)

    def reduce_start(group):
        low, high = parts_of(group)
        for e in (2, 1, 3):
            bs[group][e - 1] = acc[group][:, columns_of((r + e) % side)].astype(BF16)
            if e == 2:
                go(bs[group].at[1, low], bm[group].at[0], m_s.at[group, 0], m_r.at[group, 0], vir=right)
                go(bs[group].at[1, high], bm[group].at[1], m_s.at[group, 1], m_r.at[group, 1], vir=left)
            if e == 1:
                go(bs[group].at[0, high], bx[group].at[0, high], b_s.at[group, 0, 1], b_r.at[group, 0, 1], vir=right)
            if e == 3:
                go(bs[group].at[2, low], bx[group].at[1, low], b_s.at[group, 1, 0], b_r.at[group, 1, 0], vir=left)

    def reduce_merge(group):
        low, high = parts_of(group)
        arrived(bm[group].at[0], m_r.at[group, 0])
        merged = acc[group][low, columns_of((r + 1) % side)] + bm[group][0].astype(F32)
        bs[group][0, low, :] = merged.astype(BF16)
        go(bs[group].at[0, low], bx[group].at[0, low], b_s.at[group, 0, 0], b_r.at[group, 0, 0], vir=right)
        arrived(bm[group].at[1], m_r.at[group, 1])
        merged = acc[group][high, columns_of((r + 3) % side)] + bm[group][1].astype(F32)
        bs[group][2, high, :] = merged.astype(BF16)
        go(bs[group].at[2, high], bx[group].at[1, high], b_s.at[group, 1, 1], b_r.at[group, 1, 1], vir=left)

    nq8 = s.nq * s.nvec
    gather(0)
    total = rp[...]
    for d in range(1, side):
        arrived(rg.at[d], rg_r.at[d - 1])
        total = total + rg[d]
    rx[0] = total
    for e in range(1, side):
        go(rx.at[0], rx.at[side - e], rx_s.at[e - 1], rx_r.at[side - e - 1], vir=vid(g, (r + e) % side))
    for w in range(side):
        own_v[w].wait()
    product(0, (0,))
    relay(0)
    total = rx[0]
    for d in range(1, side):
        arrived(rx.at[d], rx_r.at[d - 1])
        total = total + rx[d]
    rmsg[...] = total.astype(BF16)
    own_rows = pl.ds(pl.multiple_of(z * nq8, 16), nq8)
    for e in near_first:
        go(rmsg, rall.at[c, own_rows, :], rz_s.at[e - 1], rz_r.at[z], aux=(z + e) % nz)
    rall[c, own_rows, :] = rmsg[...]
    gathered(0, 1)
    gathered(0, 3)
    for d in range(1, side):
        for w in range(side):
            v_copies[d, w].wait_recv()
    product(0, (1, 3))
    gather(1)
    gathered(0, 2)
    product(0, (2,))
    reduce_start(0)
    relay(1)
    product(1, (0,))
    reduce_merge(0)
    gathered(1, 1)
    gathered(1, 3)
    product(1, (1, 3))
    for d in near_first:
        source = (z + d) % nz
        arrived(rall.at[c, pl.ds(pl.multiple_of(source * nq8, 16), nq8), :], rz_r.at[source])
        arrived(sh.at[source], sh_r.at[source])
    go(rall.at[c], rall.at[c], rc_s, rc_r, occ=1 - c)
    gathered(1, 2)
    product(1, (2,))
    reduce_start(1)
    arrived(rall.at[1 - c], rc_r)
    for h in range(2):
        for part in range(s.parts):
            rl[h, part] = rall[h, :, part * 128 : (part + 1) * 128].astype(F32)
    for n in range(s.nvec):
        for h in range(2):
            sides = []
            for part in range(s.parts):
                rows = [rl[h, part, pl.ds(q * s.nvec + n, nz, stride=nq8), :] for q in range(s.nq)]
                sides.append(jnp.concatenate(rows, axis=0))
            rm32[n, h * s.half : (h + 1) * s.half, :] = jnp.concatenate(sides, axis=1).T[: s.half]
        rm[n * s.nocc : (n + 1) * s.nocc, :] = rm32[n].astype(BF16)
        row[n * s.nocc : (n + 1) * s.nocc, :] = jnp.broadcast_to(sh[n][0:1, :], (s.nocc, 128)) - eob[...]
    reduce_merge(1)

    def build(group):
        j0, count = s.groups[group]
        pack = s.packs[group]
        for side_of in range(2):
            for part, rows in enumerate(parts_of(group)):
                arrived(bx[group].at[side_of, rows], b_r.at[group, side_of, part])

        @pl.loop(0, nz)
        def _(source):
            rows = pl.ds(pl.multiple_of(source * pack, 16), pack)
            value = acc[group][rows, columns_of(r)] + bx[group][0, rows, :].astype(F32) + bx[group][1, rows, :].astype(F32)
            full = pltpu.roll(value.astype(BF16).astype(F32), s.lanes - v, 1)
            for part in range(s.lanes // 128):
                bf[part, rows, :] = full[:, part * 128 : (part + 1) * 128]

        for j in range(count):
            parts = []
            for part in range(s.lanes // 128):
                rows = [bf[part, pl.ds(q * count + j, nz, stride=pack), :] for q in range(s.nq)]
                parts.append(jnp.concatenate(rows, axis=0))
            bflat[:, (j0 + j) * s.na : (j0 + j + 1) * s.na] = jnp.concatenate(parts, axis=1)[:, : s.na]

    def tiles_ready(first_tile, last_tile):
        for tile in range(first_tile, last_tile):
            flat = bflat[:, tile * s.tile : (tile + 1) * s.tile]
            bj[tile] = flat.astype(BF16)
            bjt[tile] = flat.T.astype(BF16)

    tall = 2 * s.nocc
    coupled, weighted = (coupled0, coupled1), (weighted0, weighted1)

    def rows_of(step, tiles):
        return pl.ds(pl.multiple_of(step // tiles * tall, 16), tall)

    def couple(step, slot, start, tiles):
        coupled[slot][...] = dot(rm[rows_of(step, tiles), :], bj[start + step % tiles])

    def weigh(step, slot, start, tiles):
        own = row[rows_of(step, tiles), :]
        divisor = jnp.concatenate([own] * (s.tile // 128), axis=1) + base[start + step % tiles, 0:1, :]
        weighted[slot][...] = (coupled[slot][...] * pl.reciprocal(divisor, approx=True, full_range=False)).astype(BF16)

    def fold(step, slot, start, tiles):
        fa[rows_of(step, tiles), :] += dot(weighted[slot][...], bjt[start + step % tiles])

    def begin(*span):
        couple(0, 0, *span)
        couple(1, 1, *span)
        weigh(0, 0, *span)

    def advance(first, last, span):
        @pl.loop(first, last)
        def _(half):
            for slot in range(2):
                step = 2 * half + slot
                fold(step - 2, slot, *span)
                weigh(step - 1, 1 - slot, *span)
                couple(step, slot, *span)

    def end(steps, span):
        fold(steps - 2, 0, *span)
        weigh(steps - 1, 1, *span)
        fold(steps - 1, 1, *span)

    fa[...] = jnp.zeros(fa.shape, F32)
    build(0)
    tiles_ready(0, s.early)
    span = (0, s.early)
    steps = s.pairs * s.early
    begin(*span)
    advance(1, steps // 2, span)
    end(steps, span)

    rows2 = 2 * s.nq

    def to_core(p):
        return pltpu.make_async_remote_copy(
            src_ref=fl.at[p, 1 - c], dst_ref=fx.at[p], send_sem=fc_s.at[p], recv_sem=fc_r.at[p],
            device_id={"occ": 1 - c}, device_id_type=MESH,
        )

    def along_z(p, e):
        to = (z + e) % nz
        return pltpu.make_async_remote_copy(
            src_ref=fz.at[p, :, pl.ds(pl.multiple_of(to * rows2, 8), rows2), :], dst_ref=fr.at[p, z],
            send_sem=fz_s.at[p, e - 1], recv_sem=fz_r.at[p, z], device_id={"aux": to}, device_id_type=MESH,
        )

    def pass_on(p):
        to_core(p).wait_recv()
        fz[p] = fl[p, c] + fx[p]
        for e in near_first:
            along_z(p, e).start()

    def finish(p):
        for m in range(2):
            for h in range(2):
                start = pl.multiple_of(p * tall, 8) + m * s.nocc + h * s.half
                flip = fa[pl.ds(start, s.half), :].T
                flip = jnp.concatenate([flip, jnp.zeros((s.q, s.parts * 128 - s.half), F32)], axis=1)
                for part in range(s.parts):
                    for q in range(s.nq):
                        fl[p, h, part, pl.ds(m * s.nq + q, nz, stride=rows2), :] = flip[
                            q * nz : (q + 1) * nz, part * 128 : (part + 1) * 128
                        ]
        to_core(p).start()

    bflat[:, s.tiles * s.tile - 128 :] = jnp.zeros((s.q, 128), F32)
    build(1)
    tiles_ready(s.early, s.tiles)
    span = (s.early, s.tiles - s.early)
    each = (s.tiles - s.early) // 2
    begin(*span)

    @pl.loop(0, s.pairs)
    def _(p):
        advance(p * each + 1 - (p + s.pairs - 1) // s.pairs, (p + 1) * each, span)

        @pl.when(p > 0)
        def _():
            finish(p - 1)

        @pl.when(p > 1)
        def _():
            pass_on(p - 2)

    end(s.pairs * (s.tiles - s.early), span)
    finish(s.pairs - 1)
    pass_on(s.pairs - 2)
    for p in range(s.pairs - 1):
        total = fz[p, :, pl.ds(pl.multiple_of(z * rows2, 8), rows2), :]
        for d in near_first:
            source = (z + d) % nz
            arrived(fr.at[p, source], fz_r.at[p, source])
            total = total + fr[p, source]
        fg[0, p] = total
    pass_on(s.pairs - 1)
    for copy in started:
        copy.wait_send()
    started.clear()
    p = s.pairs - 1
    total = fz[p, :, pl.ds(pl.multiple_of(z * rows2, 8), rows2), :]
    for d in near_first:
        source = (z + d) % nz
        arrived(fr.at[p, source], fz_r.at[p, source])
        total = total + fr[p, source]
    fg[0, p] = total
    for e in range(1, side):
        go(fg.at[0], fg.at[side - e], fg_s.at[e - 1], fg_r.at[side - e - 1], vir=vid((g + e) % side, r))
    total = fg[0]
    for p in range(s.pairs):
        to_core(p).wait_send()
        for e in near_first:
            along_z(p, e).wait_send()
    for d in range(1, side):
        arrived(fg.at[d], fg_r.at[d - 1])
        total = total + fg[d]
    fgx[0] = total
    for e in range(1, side):
        go(fgx.at[0], fgx.at[side - e], fx_s.at[e - 1], fx_r.at[side - e - 1], vir=vid(g, (r + e) % side))
    for d in range(1, side):
        arrived(fgx.at[d], fx_r.at[d - 1])
        total = total + fgx[d]

    tall = nq8
    folded = jnp.concatenate([total[:, part].reshape(tall, 128) for part in range(s.parts)], axis=1)[:, : s.half]
    folded = split(folded)
    owner = lax.broadcasted_iota(jnp.int32, folded.shape, 0) % s.nq
    both = None
    for q in range(s.nq):
        term = dot(jnp.where(owner == q, folded.astype(F32), 0.0).astype(BF16), hq[q])
        both = term if both is None else both + term
    both = dot_nt(split(both[:tall] + both[tall:]), sec[...])
    spart[...] = both[:tall] + both[tall:]
    for n in range(s.nvec):
        value = spart[n * s.nq : n * s.nq + 1, :]
        for q in range(1, s.nq):
            value = value + spart[n * s.nq + q : n * s.nq + q + 1, :]
        sgs[n] = value
    for d in range(1, 2 * nz):
        other = (me + d) % (2 * nz)
        go(sgs.at[other // 2], sgr.at[me], s1_s.at[d - 1], s1_r.at[me], aux=other // 2, occ=other % 2)
    sgr[me] = sgs[z]
    for d in range(1, 2 * nz):
        other = (me + d) % (2 * nz)
        arrived(sgr.at[other], s1_r.at[other])
    total = sgr[0]
    for d in range(1, 2 * nz):
        total = total + sgr[d]
    spp[...] = total
    for d in range(1, side * side):
        go(spp, spr.at[v], s2_s.at[d - 1], s2_r.at[v], vir=(v + d) % (side * side))
    spr[v] = total
    for d in range(1, side * side):
        other = (v + d) % (side * side)
        arrived(spr.at[other], s2_r.at[other])
    total = spr[0]
    for d in range(1, side * side):
        total = total + spr[d]
    out[...] = total
    for copy in started:
        copy.wait_send()


def output_kernel(terms, trial, eo_row, sigma_out, sub_out, t32):
    t32[...] = trial[...].astype(F32)
    sigma = eo_row[...] * t32[pl.ds(lax.axis_index("aux"), 1), :] + terms[...]
    sigma_out[...] = sigma
    column = jnp.sum(t32[...] * sigma, axis=1, keepdims=True)
    sub_out[...] = jnp.broadcast_to(column, (column.shape[0], 128)).T[0:1]


def local(mesh, integrals, occ_coeffs, vir_coeffs, occ_energy, vir_energy, trial_vectors, shifts):
    s = Sizes(mesh, integrals, occ_coeffs, vir_energy)
    nz, side = s.nz, s.side
    vmem = pltpu.VMEM
    nq8 = s.nq * s.nvec
    rows2 = 2 * s.nq
    dma = lambda *shape: pltpu.SemaphoreType.DMA(shape)
    near = side - 1
    one = pltpu.SemaphoreType.DMA
    tall = 2 * s.nocc
    flat = s.parts * 128
    scratch = [
        vmem((s.tiles, s.q, s.tile), BF16),
        vmem((s.tiles, s.tile, s.q), BF16),
        vmem((s.tiles, 8, s.tile), F32),
        vmem((s.nvec * s.nocc, s.q), BF16),
        vmem((s.nvec * s.nocc, 128), F32),
        vmem((s.nq, s.half, s.nu), BF16),
        vmem((s.nocc, s.nu), BF16),
        vmem((s.nvec * s.nocc, s.q), F32),
        vmem((tall, s.tile), F32),
        vmem((tall, s.tile), F32),
        vmem((tall, s.tile), BF16),
        vmem((tall, s.tile), BF16),
        vmem((s.pairs, 2, s.parts, nz * rows2, 128), F32),
        vmem((s.pairs, s.parts, nz * rows2, 128), F32),
        vmem((s.pairs, s.parts, nz * rows2, 128), F32),
        vmem((s.pairs, nz, s.parts, rows2, 128), F32),
        vmem((side, s.pairs, s.parts, rows2, 128), F32),
        vmem((side, s.pairs, s.parts, rows2, 128), F32),
        vmem((nq8, s.nocc), F32),
        vmem((nz, 1, s.nocc), F32),
        vmem((2 * nz, 1, s.nocc), F32),
        vmem((1, s.nocc), F32),
        vmem((side * side, 1, s.nocc), F32),
        vmem((s.nq, s.window, s.nu), BF16),
        vmem((s.nocc, s.ao), BF16),
        vmem((s.nq, s.nocc, s.nu), F32),
        vmem((s.nq, s.half, s.nu), F32),
        *[vmem((nz, pack, s.nu), F32) for pack in s.packs],
        *[vmem((nz, pack, s.nu), BF16) for pack in s.packs],
        *[vmem((side, nz, pack, s.nu), BF16) for pack in s.packs],
        vmem((side, side * s.lanes, s.nu), BF16),
        *[vmem((nz * pack, side * s.lanes), F32) for pack in s.packs],
        *[vmem((side - 1, nz * pack, s.lanes), BF16) for pack in s.packs],
        *[vmem((2, nz * pack, s.lanes), BF16) for pack in s.packs],
        *[vmem((2, nz * pack // 2, s.lanes), BF16) for pack in s.packs],
        vmem((s.lanes // 128, nz * max(s.packs), 128), F32),
        vmem((s.q, s.tiles * s.tile), F32),
        vmem((s.nocc, 128), F32),
        vmem((8, s.lanes), F32),
        vmem((8, 128), F32),
        vmem((nq8, flat), F32),
        vmem((side, nq8, flat), F32),
        vmem((side, nq8, flat), F32),
        vmem((nq8, flat), BF16),
        vmem((2, nz * nq8, flat), BF16),
        vmem((2, s.parts, nz * nq8, 128), F32),
        vmem((s.nvec, s.nocc, s.q), F32),
        vmem((nz, 8, 128), F32),
        dma(s.nq + 1), dma(side), dma(near, side), dma(near, side), dma(nz), dma(nz),
        dma(s.nq), dma(s.nq), dma(2, nz), dma(2, nz), dma(2, near, 2), dma(2, near, 2),
        dma(near), dma(near), dma(near), dma(near), dma(nz), dma(nz), one, one,
        dma(2, 2, 2), dma(2, 2, 2), dma(2, 2), dma(2, 2),
        dma(s.pairs), dma(s.pairs), dma(s.pairs, nz), dma(s.pairs, nz),
        dma(near), dma(near), dma(near), dma(near), dma(2 * nz), dma(2 * nz), dma(side * side), dma(side * side),
    ]
    hbm = pl.BlockSpec(memory_space=pl.ANY)
    fast = pl.BlockSpec(memory_space=pltpu.VMEM)
    scalars = pl.BlockSpec(memory_space=pltpu.SMEM)
    shape = jax.ShapeDtypeStruct
    limit = 56 * 1024 * 1024
    occ_row, trial_rows = occ_energy[None], trial_vectors.T
    terms = pl.pallas_call(
        functools.partial(kernel, s),
        out_shape=shape((1, s.nocc), F32),
        in_specs=[hbm, hbm, hbm, fast, fast, scalars, fast, scalars],
        out_specs=fast,
        scratch_shapes=scratch,
        compiler_params=pltpu.CompilerParams(collective_id=0, has_side_effects=True, vmem_limit_bytes=limit),
    )(integrals, occ_coeffs.T, vir_coeffs.T, trial_rows, occ_row, occ_energy, vir_energy[None], shifts)
    sigma, sub = pl.pallas_call(
        output_kernel,
        out_shape=(shape((1, s.nocc), F32), shape((1, s.nvec), F32)),
        in_specs=[fast] * 3,
        out_specs=(fast, fast),
        scratch_shapes=[vmem((s.nvec, s.nocc), F32)],
    )(terms, trial_rows, occ_row)
    return sigma.T, sub.T


def solution(mesh):
    return jax.shard_map(
        functools.partial(local, dict(mesh.shape)),
        mesh=mesh,
        in_specs=(P("aux", "occ", "vir"), P(), P("vir", None), P(), P("vir"), P(), P("aux")),
        out_specs=(P(None, "aux"), P(None, "aux")),
        check_vma=False,
    )
```

```python
import functools
import math

import jax
import jax.numpy as jnp
from jax import lax
from jax.experimental import pallas as pl
from jax.experimental.pallas import tpu as pltpu
from jax.sharding import PartitionSpec as P

MESH = pl.DeviceIdType.MESH
F32 = jnp.float32
BF16 = jnp.bfloat16


def dot(a, b):
    return jnp.dot(a, b, preferred_element_type=F32)


def dot_nt(a, b):
    return lax.dot_general(a, b, (((1,), (1,)), ((), ())), preferred_element_type=F32)


def split(value):
    high = value.astype(BF16)
    low = (value - high.astype(F32)).astype(BF16)
    return jnp.concatenate([high.astype(F32), low.astype(F32)], axis=0).astype(BF16)


def send(src, dst, send_sem, recv_sem, **device):
    copy = pltpu.make_async_remote_copy(
        src_ref=src, dst_ref=dst, send_sem=send_sem, recv_sem=recv_sem, device_id=device, device_id_type=MESH
    )
    copy.start()
    return copy


class Sizes:
    def __init__(self, mesh, integrals, occ_coeffs, vir_energy):
        self.nz = mesh["aux"]
        self.side = math.isqrt(mesh["vir"])
        self.nq, self.mu, self.nu = integrals.shape
        self.ao, self.nocc = occ_coeffs.shape
        self.half = self.nocc // 2
        self.jb = self.half // self.nz
        self.na = vir_energy.shape[0]
        self.block = 16 * (self.na // 16)
        self.rows = self.block + 16
        assert self.na == self.block + 1 and self.side == 4
        first = (self.jb + 1) // 2
        rows = -(-(self.nq * first) // 16) * 16
        self.groups = [(0, first), (first, self.jb - first)]
        rest = self.jb - first
        self.packs = (rows, -(-(self.nq * rest) // 16) * 16)
        self.tile = 512
        self.tiles = -(-(self.jb * self.na) // self.tile)
        self.early = first * self.na // self.tile
        self.quads = self.nz // 4
        self.lane0 = self.mu // 128 * 128
        self.shift = self.mu - self.lane0
        self.window = self.mu + self.shift
        self.lanes = -(-self.rows // 128) * 128
        self.q = self.nq * self.nz
        self.nvec = self.nz
        self.parts = -(-self.half // 128)
        last = 128 * (self.nu * (mesh["vir"] - 1) // 128) - 128
        self.view = self.ao - last
        for v in range(mesh["vir"]):
            start = 128 * (self.nu * v // 128) - 128 * ((v + 1) // mesh["vir"])
            assert start + self.view <= self.ao and self.nu * v - start + self.nu <= self.view


def kernel(
    s, int_h, occ_h, vir_h, trial, eo_row, eo_s, ve, shift_s,
    out,
    bj, bjt, base, rm, row, hq, sec, fa, coupled0, coupled1, weighted0, weighted1,
    hp, fl, fb, fr, fp, fq, spart, sgs, sgr, spp, spr,
    ibuf, occ_v, pf, xf, pk0, pk1, hs0, hs1, hg0, hg1, vb, acc0, acc1, bs0, bs1, bx0, bx1, bm0, bm1, bf, bflat, eob, ve8, shift,
    rp, rg, rx, rmsg, rall, rl, rm32, sh,
    in_sem, v_own, v_s, v_r, sh_s, sh_r, x_s, x_r, h_s, h_r, g_s, g_r, rg_s, rg_r, rx_s, rx_r, rz_s, rz_r, rc_s, rc_r,
    b_s, b_r, m_s, m_r, fz_s, fz_r, fp_s, fp_r, s1_s, s1_r, s2_s, s2_r,
):
    nz, side = s.nz, s.side
    z, c, v = lax.axis_index("aux"), lax.axis_index("occ"), lax.axis_index("vir")
    y, x = v // side, v % side
    g = y + c * (x - y)
    r = x + c * (y - x)
    sg = side - (side - 1) * c
    sr = 1 + (side - 1) * c

    def vid(gather, reduce):
        return gather * sg + reduce * sr

    pk, hs, hg, acc, bs, bx, bm = (pk0, pk1), (hs0, hs1), (hg0, hg1), (acc0, acc1), (bs0, bs1), (bx0, bx1), (bm0, bm1)
    started = []

    def go(*args, **device):
        copy = send(*args, **device)
        started.append(copy)
        return copy

    occ_in = pltpu.make_async_copy(occ_h, occ_v, in_sem.at[s.nq])
    occ_in.start()
    zero_rows = jnp.zeros((s.shift, s.nu), BF16)
    loads = []
    for q in range(s.nq):
        if s.shift:
            ibuf[q, 0 : s.shift, :] = zero_rows
            ibuf[q, s.mu : s.mu + s.shift, :] = zero_rows
        copy = pltpu.make_async_copy(
            int_h.at[q], ibuf.at[q, pl.ds(pl.multiple_of(s.shift * c, 16), s.mu), :], in_sem.at[q]
        )
        copy.start()
        loads.append(copy)
    own_v = []
    for w in range(side):
        start = pl.multiple_of(s.block * vid(g, w), 16)
        copy = pltpu.make_async_copy(
            vir_h.at[pl.ds(start, s.rows), :], vb.at[0, pl.ds(w * s.lanes, s.rows), :], v_own.at[w]
        )
        copy.start()
        own_v.append(copy)

    for group in range(2):
        pk[group][...] = jnp.zeros(pk[group].shape, F32)
    rp[...] = jnp.zeros(rp.shape, F32)
    for d in range(side):
        for w in range(side):
            vb[d, w * s.lanes + s.rows : (w + 1) * s.lanes, :] = jnp.zeros((s.lanes - s.rows, s.nu), BF16)

    barrier = pltpu.get_barrier_semaphore()
    me = 2 * z + c
    for d in range(1, 2 * nz):
        other = (me + d) % (2 * nz)
        pl.semaphore_signal(barrier, inc=1, device_id={"aux": other // 2, "occ": other % 2}, device_id_type=MESH)
    for d in range(1, side * side):
        pl.semaphore_signal(barrier, inc=1, device_id={"vir": (v + d) % (side * side)}, device_id_type=MESH)
    pl.semaphore_wait(barrier, 2 * nz + side * side - 2)

    v_copies = {}
    for e in range(1, side):
        to = (g + e) % side
        for w in range(side):
            start = pl.multiple_of(s.block * vid(to, w), 16)
            v_copies[side - e, w] = go(
                vir_h.at[pl.ds(start, s.rows), :], vb.at[side - e, pl.ds(w * s.lanes, s.rows), :], v_s.at[e - 1, w], v_r.at[side - e - 1, w],
                vir=vid(to, r),
            )
    shift[...] = jnp.full((8, 128), shift_s[0], F32)
    for e in range(1, nz):
        go(shift, sh.at[z], sh_s.at[e - 1], sh_r.at[z], aux=(z + e) % nz)
    sh[z] = shift[...]

    occ_in.wait()
    x_copies = []
    for q in range(s.nq):
        loads[q].wait()
        columns = occ_v[:, pl.ds(pl.multiple_of(s.lane0 * c, 128), s.window)]
        pf[q] = dot(columns, ibuf[q])
        x_copies.append(
            go(pf.at[q, pl.ds(pl.multiple_of(s.half * (1 - c), 8), s.half), :], xf.at[q], x_s.at[q], x_r.at[q], occ=1 - c)
        )
    start = 128 * ((s.nu * v) // 128) - 128 * ((v + 1) // (side * side))
    view = occ_v[:, pl.ds(pl.multiple_of(start, 128), s.view)].astype(F32)
    wide = -(-s.view // 128) * 128
    view = jnp.concatenate([view, jnp.zeros((s.nocc, wide - s.view), F32)], axis=1)
    sec[...] = pltpu.roll(view, wide - (s.nu * v - start), 1)[:, : s.nu].astype(BF16)
    weights = split(dot(trial[...], sec[...]))
    for q in range(s.nq):
        x_copies[q].wait_recv()
        xf[q] = xf[q] + pf[q, pl.ds(pl.multiple_of(s.half * c, 8), s.half), :]
    near_first = [d for pair in zip(range(1, nz // 2), range(nz - 1, nz // 2, -1)) for d in pair] + [nz // 2]
    for group in range(2):
        j0, count = s.groups[group]
        for q in range(s.nq):
            for to in range(nz):
                pk[group][to, q * count : (q + 1) * count, :] = xf[q, to * s.jb + j0 : to * s.jb + j0 + count, :]
        hs[group][...] = pk[group][...].astype(BF16)
        for e in near_first:
            to = (z + e) % nz
            go(hs[group].at[to], hg[group].at[0, z], h_s.at[group, e - 1], h_r.at[group, z], aux=to)
        hg[group][0, z] = hs[group][z]
    for q in range(s.nq):
        hq[q] = xf[q].astype(BF16)

    for q in range(s.nq):
        hp[q] = dot_nt(hq[q], sec[...]).astype(BF16)
    for q in range(s.nq):
        both = dot_nt(weights, hq[q])
        rp[q * s.nvec : (q + 1) * s.nvec, 0 : s.half] = both[: s.nvec] + both[s.nvec :]
    for e in range(1, side):
        go(rp, rg.at[side - e], rg_s.at[e - 1], rg_r.at[side - e - 1], vir=vid((g + e) % side, r))

    ve8[...] = jnp.ones(ve8.shape, F32)
    ve8[:, 0 : s.na] = jnp.broadcast_to(ve[...], (8, s.na))
    bflat[...] = jnp.ones(bflat.shape, F32)
    first = s.half * c + s.jb * z
    for j in range(s.jb):
        bflat[0:8, j * s.na : (j + 1) * s.na] = ve8[:, 0 : s.na] - eo_s[first + j]
    for tile in range(s.tiles):
        base[tile] = bflat[0:8, tile * s.tile : (tile + 1) * s.tile]
    square = jnp.broadcast_to(eo_row[...], (128, s.nocc))
    fill = -(-s.nocc // 128) * 128 - s.nocc
    eob[...] = jnp.concatenate([square, jnp.zeros((128, fill), F32)], axis=1).T[: s.nocc]

    def arrived(dst, recv_sem):
        pltpu.make_async_remote_copy(
            src_ref=dst, dst_ref=dst, send_sem=recv_sem, recv_sem=recv_sem, device_id={"occ": c}, device_id_type=MESH
        ).wait_recv()

    ahead, behind = vid((g + 1) % side, r), vid((g + 3) % side, r)
    halves = (pl.ds(0, nz // 2), pl.ds(nz // 2, nz // 2))

    def gather(group):
        for d in near_first:
            source = (z + d) % nz
            arrived(hg[group].at[0, source], h_r.at[group, source])
        for n in range(2):
            for to, slot, part in ((behind, 1, n), (ahead, 3, 1 - n)):
                part_ref = hg[group].at[0, halves[part]]
                go(
                    part_ref, hg[group].at[slot, halves[part]], g_s.at[group, slot - 1, part], g_r.at[group, slot - 1, part],
                    vir=to,
                )

    def relay(group):
        for slot, to, part in ((1, behind, 0), (3, ahead, 1)):
            arrived(hg[group].at[slot, halves[part]], g_r.at[group, slot - 1, part])
            go(
                hg[group].at[slot, halves[part]], hg[group].at[2, halves[part]], g_s.at[group, 1, part],
                g_r.at[group, 1, part], vir=to,
            )

    def gathered(group, slot):
        for part in range(2):
            if (slot, part) not in ((1, 0), (3, 1)):
                arrived(hg[group].at[slot, halves[part]], g_r.at[group, slot - 1, part])

    def term(group, d):
        return dot_nt(hg[group][d].reshape(nz * s.packs[group], s.nu), vb[d])

    def product(group, slots):
        value = term(group, slots[0])
        for d in slots[1:]:
            value = value + term(group, d)
        acc[group][...] = value if slots[0] == 0 else value + acc[group][...]

    def columns_of(w):
        return pl.ds(pl.multiple_of(w * s.lanes, 128), s.lanes)

    right, left = vid(g, (r + 1) % side), vid(g, (r + 3) % side)

    def parts_of(group):
        size = nz * s.packs[group] // 2
        return pl.ds(0, size), pl.ds(size, size)

    def reduce_start(group):
        low, high = parts_of(group)
        for e in (2, 1, 3):
            bs[group][e - 1] = acc[group][:, columns_of((r + e) % side)].astype(BF16)
            if e == 2:
                go(bs[group].at[1, low], bm[group].at[0], m_s.at[group, 0], m_r.at[group, 0], vir=right)
                go(bs[group].at[1, high], bm[group].at[1], m_s.at[group, 1], m_r.at[group, 1], vir=left)
            if e == 1:
                go(bs[group].at[0, high], bx[group].at[0, high], b_s.at[group, 0, 1], b_r.at[group, 0, 1], vir=right)
            if e == 3:
                go(bs[group].at[2, low], bx[group].at[1, low], b_s.at[group, 1, 0], b_r.at[group, 1, 0], vir=left)

    def reduce_merge(group):
        low, high = parts_of(group)
        arrived(bm[group].at[0], m_r.at[group, 0])
        merged = acc[group][low, columns_of((r + 1) % side)] + bm[group][0].astype(F32)
        bs[group][0, low, :] = merged.astype(BF16)
        go(bs[group].at[0, low], bx[group].at[0, low], b_s.at[group, 0, 0], b_r.at[group, 0, 0], vir=right)
        arrived(bm[group].at[1], m_r.at[group, 1])
        merged = acc[group][high, columns_of((r + 3) % side)] + bm[group][1].astype(F32)
        bs[group][2, high, :] = merged.astype(BF16)
        go(bs[group].at[2, high], bx[group].at[1, high], b_s.at[group, 1, 1], b_r.at[group, 1, 1], vir=left)

    nq8 = s.nq * s.nvec
    gather(0)
    total = rp[...]
    for d in range(1, side):
        arrived(rg.at[d], rg_r.at[d - 1])
        total = total + rg[d]
    rx[0] = total
    for e in range(1, side):
        go(rx.at[0], rx.at[side - e], rx_s.at[e - 1], rx_r.at[side - e - 1], vir=vid(g, (r + e) % side))
    for w in range(side):
        own_v[w].wait()
    product(0, (0,))
    relay(0)
    total = rx[0]
    for d in range(1, side):
        arrived(rx.at[d], rx_r.at[d - 1])
        total = total + rx[d]
    rmsg[...] = total.astype(BF16)
    own_rows = pl.ds(pl.multiple_of(z * nq8, 16), nq8)
    for e in near_first:
        go(rmsg, rall.at[c, own_rows, :], rz_s.at[e - 1], rz_r.at[z], aux=(z + e) % nz)
    rall[c, own_rows, :] = rmsg[...]
    gathered(0, 1)
    gathered(0, 3)
    for d in range(1, side):
        for w in range(side):
            v_copies[d, w].wait_recv()
    product(0, (1, 3))
    gather(1)
    gathered(0, 2)
    product(0, (2,))
    reduce_start(0)
    relay(1)
    product(1, (0,))
    reduce_merge(0)
    gathered(1, 1)
    gathered(1, 3)
    product(1, (1, 3))
    for d in near_first:
        source = (z + d) % nz
        arrived(rall.at[c, pl.ds(pl.multiple_of(source * nq8, 16), nq8), :], rz_r.at[source])
        arrived(sh.at[source], sh_r.at[source])
    go(rall.at[c], rall.at[c], rc_s, rc_r, occ=1 - c)
    gathered(1, 2)
    product(1, (2,))
    reduce_start(1)
    arrived(rall.at[1 - c], rc_r)
    for h in range(2):
        for part in range(s.parts):
            rl[h, part] = rall[h, :, part * 128 : (part + 1) * 128].astype(F32)
    for n in range(s.nvec):
        for h in range(2):
            sides = []
            for part in range(s.parts):
                rows = [rl[h, part, pl.ds(q * s.nvec + n, nz, stride=nq8), :] for q in range(s.nq)]
                sides.append(jnp.concatenate(rows, axis=0))
            rm32[n, h * s.half : (h + 1) * s.half, :] = jnp.concatenate(sides, axis=1).T[: s.half]
        rm[n * s.nocc : (n + 1) * s.nocc, :] = rm32[n].astype(BF16)
        row[n * s.nocc : (n + 1) * s.nocc, :] = jnp.broadcast_to(sh[n][0:1, :], (s.nocc, 128)) - eob[...]
    reduce_merge(1)

    def build(group):
        j0, count = s.groups[group]
        pack = s.packs[group]
        for side_of in range(2):
            for part, rows in enumerate(parts_of(group)):
                arrived(bx[group].at[side_of, rows], b_r.at[group, side_of, part])

        @pl.loop(0, nz)
        def _(source):
            rows = pl.ds(pl.multiple_of(source * pack, 16), pack)
            value = acc[group][rows, columns_of(r)] + bx[group][0, rows, :].astype(F32) + bx[group][1, rows, :].astype(F32)
            full = pltpu.roll(value.astype(BF16).astype(F32), s.lanes - v, 1)
            for part in range(s.lanes // 128):
                bf[part, rows, :] = full[:, part * 128 : (part + 1) * 128]

        for j in range(count):
            parts = []
            for part in range(s.lanes // 128):
                rows = [bf[part, pl.ds(q * count + j, nz, stride=pack), :] for q in range(s.nq)]
                parts.append(jnp.concatenate(rows, axis=0))
            bflat[:, (j0 + j) * s.na : (j0 + j + 1) * s.na] = jnp.concatenate(parts, axis=1)[:, : s.na]

    def tiles_ready(first_tile, last_tile):
        for tile in range(first_tile, last_tile):
            flat = bflat[:, tile * s.tile : (tile + 1) * s.tile]
            bj[tile] = flat.astype(BF16)
            bjt[tile] = flat.T.astype(BF16)

    tall = 4 * s.nocc
    coupled, weighted = (coupled0, coupled1), (weighted0, weighted1)

    def rows_of(step, tiles):
        return pl.ds(pl.multiple_of(step // tiles * tall, 16), tall)

    def couple(step, slot, start, tiles):
        coupled[slot][...] = dot(rm[rows_of(step, tiles), :], bj[start + step % tiles])

    def weigh(step, slot, start, tiles):
        own = row[rows_of(step, tiles), :]
        divisor = jnp.concatenate([own] * (s.tile // 128), axis=1) + base[start + step % tiles, 0:1, :]
        weighted[slot][...] = (coupled[slot][...] * pl.reciprocal(divisor, approx=True, full_range=False)).astype(BF16)

    def fold(step, slot, start, tiles):
        fa[rows_of(step, tiles), :] += dot(weighted[slot][...], bjt[start + step % tiles])

    def begin(*span):
        couple(0, 0, *span)
        couple(1, 1, *span)
        weigh(0, 0, *span)

    def advance(last, span, after=None):
        @pl.loop(1, last)
        def _(half):
            for slot in range(2):
                step = 2 * half + slot
                fold(step - 2, slot, *span)
                weigh(step - 1, 1 - slot, *span)
                couple(step, slot, *span)
            if after is not None:
                after(half)

    def end(steps, span):
        fold(steps - 2, 0, *span)
        weigh(steps - 1, 1, *span)
        fold(steps - 1, 1, *span)

    fa[...] = jnp.zeros(fa.shape, F32)
    build(0)
    tiles_ready(0, s.early)
    span = (0, s.early)
    steps = s.quads * s.early
    begin(*span)
    advance(steps // 2, span)
    end(steps, span)

    rows4 = 4 * s.nq
    around = side * side

    def to_owner(u, d):
        other = (me + d) % (2 * nz)
        return pltpu.make_async_remote_copy(
            src_ref=fb.at[u, other % 2, pl.ds(pl.multiple_of(other // 2 * rows4, 16), rows4), :], dst_ref=fr.at[u, me],
            send_sem=fz_s.at[u, d - 1], recv_sem=fz_r.at[u, me],
            device_id={"aux": other // 2, "occ": other % 2}, device_id_type=MESH,
        )

    def to_plane(u, d):
        return pltpu.make_async_remote_copy(
            src_ref=fp.at[u], dst_ref=fq.at[u, v], send_sem=fp_s.at[u, d - 1], recv_sem=fp_r.at[u, v],
            device_id={"vir": (v + d) % around}, device_id_type=MESH,
        )

    def finish(u):
        for m in range(4):
            for h in range(2):
                start = u * tall + m * s.nocc + h * s.half
                flip = fa[start : start + s.half, :].T
                flip = jnp.concatenate([flip, jnp.zeros((s.q, s.parts * 128 - s.half), F32)], axis=1)
                for part in range(s.parts):
                    for q in range(s.nq):
                        fl[h, part, pl.ds(m * s.nq + q, nz, stride=rows4), :] = flip[
                            q * nz : (q + 1) * nz, part * 128 : (part + 1) * 128
                        ]
        for h in range(2):
            fb[u, h] = jnp.concatenate([fl[h, part] for part in range(s.parts)], axis=1).astype(BF16)
        for d in range(1, 2 * nz):
            to_owner(u, d).start()
        fr[u, me] = fb[u, c, pl.ds(pl.multiple_of(z * rows4, 16), rows4), :]

    def pass_on(u):
        for d in range(1, 2 * nz):
            other = (me + d) % (2 * nz)
            arrived(fr.at[u, other], fz_r.at[u, other])
        total = fr[u, 0].astype(F32)
        for other in range(1, 2 * nz):
            total = total + fr[u, other].astype(F32)
        fp[u] = total.astype(BF16)
        for d in range(1, around):
            to_plane(u, d).start()
        fq[u, v] = fp[u]

    def apply(u):
        for d in range(1, around):
            other = (v + d) % around
            arrived(fq.at[u, other], fp_r.at[u, other])
        total = fq[u, 0].astype(F32)
        for other in range(1, around):
            total = total + fq[u, other].astype(F32)
        folded = split(total[:, : s.half])
        owner = lax.broadcasted_iota(jnp.int32, folded.shape, 0) % s.nq
        both = None
        for q in range(s.nq):
            value = dot(jnp.where(owner == q, folded.astype(F32), 0.0).astype(BF16), hp[q])
            both = value if both is None else both + value
        spart[...] = both[:rows4] + both[rows4:]
        for m in range(4):
            value = spart[m * s.nq : m * s.nq + 1, :]
            for q in range(1, s.nq):
                value = value + spart[m * s.nq + q : m * s.nq + q + 1, :]
            sgs[4 * u + m] = value

    bflat[:, s.tiles * s.tile - 128 :] = jnp.zeros((s.q, 128), F32)
    build(1)
    tiles_ready(s.early, s.tiles)
    late = s.tiles - s.early
    span = (s.early, late)
    begin(*span)

    def serve(half):
        @pl.when(half == late // 2)
        def _():
            finish(0)

        @pl.when(half == late - 1)
        def _():
            pass_on(0)

    advance(late, span, serve)
    end(2 * late, span)
    finish(1)
    for copy in started:
        copy.wait_send()
    started.clear()
    apply(0)
    pass_on(1)
    for u in range(2):
        for d in range(1, 2 * nz):
            to_owner(u, d).wait_send()
    apply(1)
    for d in range(1, 2 * nz):
        other = (me + d) % (2 * nz)
        go(sgs.at[other // 2], sgr.at[me], s1_s.at[d - 1], s1_r.at[me], aux=other // 2, occ=other % 2)
    sgr[me] = sgs[z]
    for d in range(1, 2 * nz):
        other = (me + d) % (2 * nz)
        arrived(sgr.at[other], s1_r.at[other])
    total = sgr[0]
    for d in range(1, 2 * nz):
        total = total + sgr[d]
    spp[...] = total
    for d in range(1, side * side):
        go(spp, spr.at[v], s2_s.at[d - 1], s2_r.at[v], vir=(v + d) % (side * side))
    spr[v] = total
    for d in range(1, side * side):
        other = (v + d) % (side * side)
        arrived(spr.at[other], s2_r.at[other])
    total = spr[0]
    for d in range(1, side * side):
        total = total + spr[d]
    out[...] = total
    for copy in started:
        copy.wait_send()
    for u in range(2):
        for d in range(1, around):
            to_plane(u, d).wait_send()


def output_kernel(terms, trial, eo_row, sigma_out, sub_out, t32):
    t32[...] = trial[...].astype(F32)
    sigma = eo_row[...] * t32[pl.ds(lax.axis_index("aux"), 1), :] + terms[...]
    sigma_out[...] = sigma
    column = jnp.sum(t32[...] * sigma, axis=1, keepdims=True)
    sub_out[...] = jnp.broadcast_to(column, (column.shape[0], 128)).T[0:1]


def local(mesh, integrals, occ_coeffs, vir_coeffs, occ_energy, vir_energy, trial_vectors, shifts):
    s = Sizes(mesh, integrals, occ_coeffs, vir_energy)
    nz, side = s.nz, s.side
    vmem = pltpu.VMEM
    nq8 = s.nq * s.nvec
    rows4 = 4 * s.nq
    dma = lambda *shape: pltpu.SemaphoreType.DMA(shape)
    near = side - 1
    one = pltpu.SemaphoreType.DMA
    tall = 4 * s.nocc
    flat = s.parts * 128
    scratch = [
        vmem((s.tiles, s.q, s.tile), BF16),
        vmem((s.tiles, s.tile, s.q), BF16),
        vmem((s.tiles, 8, s.tile), F32),
        vmem((s.nvec * s.nocc, s.q), BF16),
        vmem((s.nvec * s.nocc, 128), F32),
        vmem((s.nq, s.half, s.nu), BF16),
        vmem((s.nocc, s.nu), BF16),
        vmem((s.nvec * s.nocc, s.q), F32),
        vmem((tall, s.tile), F32),
        vmem((tall, s.tile), F32),
        vmem((tall, s.tile), BF16),
        vmem((tall, s.tile), BF16),
        vmem((s.nq, s.half, s.nocc), BF16),
        vmem((2, s.parts, nz * rows4, 128), F32),
        vmem((s.quads, 2, nz * rows4, flat), BF16),
        vmem((s.quads, 2 * nz, rows4, flat), BF16),
        vmem((s.quads, rows4, flat), BF16),
        vmem((s.quads, side * side, rows4, flat), BF16),
        vmem((rows4, s.nocc), F32),
        vmem((nz, 1, s.nocc), F32),
        vmem((2 * nz, 1, s.nocc), F32),
        vmem((1, s.nocc), F32),
        vmem((side * side, 1, s.nocc), F32),
        vmem((s.nq, s.window, s.nu), BF16),
        vmem((s.nocc, s.ao), BF16),
        vmem((s.nq, s.nocc, s.nu), F32),
        vmem((s.nq, s.half, s.nu), F32),
        *[vmem((nz, pack, s.nu), F32) for pack in s.packs],
        *[vmem((nz, pack, s.nu), BF16) for pack in s.packs],
        *[vmem((side, nz, pack, s.nu), BF16) for pack in s.packs],
        vmem((side, side * s.lanes, s.nu), BF16),
        *[vmem((nz * pack, side * s.lanes), F32) for pack in s.packs],
        *[vmem((side - 1, nz * pack, s.lanes), BF16) for pack in s.packs],
        *[vmem((2, nz * pack, s.lanes), BF16) for pack in s.packs],
        *[vmem((2, nz * pack // 2, s.lanes), BF16) for pack in s.packs],
        vmem((s.lanes // 128, nz * max(s.packs), 128), F32),
        vmem((s.q, s.tiles * s.tile), F32),
        vmem((s.nocc, 128), F32),
        vmem((8, s.lanes), F32),
        vmem((8, 128), F32),
        vmem((nq8, flat), F32),
        vmem((side, nq8, flat), F32),
        vmem((side, nq8, flat), F32),
        vmem((nq8, flat), BF16),
        vmem((2, nz * nq8, flat), BF16),
        vmem((2, s.parts, nz * nq8, 128), F32),
        vmem((s.nvec, s.nocc, s.q), F32),
        vmem((nz, 8, 128), F32),
        dma(s.nq + 1), dma(side), dma(near, side), dma(near, side), dma(nz), dma(nz),
        dma(s.nq), dma(s.nq), dma(2, nz), dma(2, nz), dma(2, near, 2), dma(2, near, 2),
        dma(near), dma(near), dma(near), dma(near), dma(nz), dma(nz), one, one,
        dma(2, 2, 2), dma(2, 2, 2), dma(2, 2), dma(2, 2),
        dma(s.quads, 2 * nz), dma(s.quads, 2 * nz), dma(s.quads, side * side), dma(s.quads, side * side), dma(2 * nz), dma(2 * nz), dma(side * side), dma(side * side),
    ]
    hbm = pl.BlockSpec(memory_space=pl.ANY)
    fast = pl.BlockSpec(memory_space=pltpu.VMEM)
    scalars = pl.BlockSpec(memory_space=pltpu.SMEM)
    shape = jax.ShapeDtypeStruct
    limit = 56 * 1024 * 1024
    occ_row, trial_rows = occ_energy[None], trial_vectors.T
    terms = pl.pallas_call(
        functools.partial(kernel, s),
        out_shape=shape((1, s.nocc), F32),
        in_specs=[hbm, hbm, hbm, fast, fast, scalars, fast, scalars],
        out_specs=fast,
        scratch_shapes=scratch,
        compiler_params=pltpu.CompilerParams(collective_id=0, has_side_effects=True, vmem_limit_bytes=limit),
    )(integrals, occ_coeffs.T, vir_coeffs.T, trial_rows, occ_row, occ_energy, vir_energy[None], shifts)
    sigma, sub = pl.pallas_call(
        output_kernel,
        out_shape=(shape((1, s.nocc), F32), shape((1, s.nvec), F32)),
        in_specs=[fast] * 3,
        out_specs=(fast, fast),
        scratch_shapes=[vmem((s.nvec, s.nocc), F32)],
    )(terms, trial_rows, occ_row)
    return sigma.T, sub.T


def solution(mesh):
    return jax.shard_map(
        functools.partial(local, dict(mesh.shape)),
        mesh=mesh,
        in_specs=(P("aux", "occ", "vir"), P(), P("vir", None), P(), P("vir"), P(), P("aux")),
        out_specs=(P(None, "aux"), P(None, "aux")),
        check_vma=False,
    )
```

```python
import functools
import math

import jax
import jax.numpy as jnp
from jax import lax
from jax.experimental import pallas as pl
from jax.experimental.pallas import tpu as pltpu
from jax.sharding import PartitionSpec as P

MESH = pl.DeviceIdType.MESH
F32 = jnp.float32
BF16 = jnp.bfloat16


def dot(a, b):
    return jnp.dot(a, b, preferred_element_type=F32)


def dot_nt(a, b):
    return lax.dot_general(a, b, (((1,), (1,)), ((), ())), preferred_element_type=F32)


def split(value):
    high = value.astype(BF16)
    low = (value - high.astype(F32)).astype(BF16)
    return jnp.concatenate([high.astype(F32), low.astype(F32)], axis=0).astype(BF16)


def send(src, dst, send_sem, recv_sem, **device):
    copy = pltpu.make_async_remote_copy(
        src_ref=src, dst_ref=dst, send_sem=send_sem, recv_sem=recv_sem, device_id=device, device_id_type=MESH
    )
    copy.start()
    return copy


class Sizes:
    def __init__(self, mesh, integrals, occ_coeffs, vir_energy):
        self.nz = mesh["aux"]
        self.side = math.isqrt(mesh["vir"])
        self.nq, self.mu, self.nu = integrals.shape
        self.ao, self.nocc = occ_coeffs.shape
        self.half = self.nocc // 2
        self.jb = self.half // self.nz
        self.na = vir_energy.shape[0]
        self.block = 16 * (self.na // 16)
        self.rows = self.block + 16
        assert self.na == self.block + 1 and self.side == 4
        third = self.jb // 12 * 4
        self.groups = [(0, third), (third, third), (2 * third, self.jb - 2 * third)]
        self.packs = [-(-(self.nq * count) // 16) * 16 for _, count in self.groups]
        self.tile = 512
        self.tiles = -(-(self.jb * self.na) // self.tile)
        ends = [(j0 + count) * self.na // self.tile for j0, count in self.groups[:-1]] + [self.tiles]
        self.spans = [(start, end - start) for start, end in zip([0] + ends, ends)]
        self.quads = self.nz // 4
        self.lane0 = self.mu // 128 * 128
        self.shift = self.mu - self.lane0
        self.window = self.mu + self.shift
        self.lanes = -(-self.rows // 128) * 128
        self.q = self.nq * self.nz
        self.nvec = self.nz
        self.parts = -(-self.half // 128)
        last = 128 * (self.nu * (mesh["vir"] - 1) // 128) - 128
        self.view = self.ao - last
        for v in range(mesh["vir"]):
            start = 128 * (self.nu * v // 128) - 128 * ((v + 1) // mesh["vir"])
            assert start + self.view <= self.ao and self.nu * v - start + self.nu <= self.view


def kernel(
    s, int_h, occ_h, vir_h, trial, eo_row, eo_s, ve, shift_s,
    out,
    bj, bjt, base, rm, row, hq, sec, fa, coupled0, coupled1, weighted0, weighted1,
    hp, fl, fb, fr, fp, fq, spart, sgs, sgr, spp, spr,
    ibuf, occ_v, pf, xf, pk0, pk1, pk2, hs0, hs1, hs2, hg0, hg1, hg2, vb,
    acc0, acc1, acc2, bs0, bs1, bs2, bx0, bx1, bx2, bm0, bm1, bm2, bf, bflat, eob, ve8, shift,
    rp, rg, rx, rmsg, rall, rl, rm32, sh,
    in_sem, v_own, v_s, v_r, sh_s, sh_r, x_s, x_r, h_s, h_r, g_s, g_r, rg_s, rg_r, rx_s, rx_r, rz_s, rz_r, rc_s, rc_r,
    b_s, b_r, m_s, m_r, fz_s, fz_r, fp_s, fp_r, s1_s, s1_r, s2_s, s2_r,
):
    nz, side = s.nz, s.side
    z, c, v = lax.axis_index("aux"), lax.axis_index("occ"), lax.axis_index("vir")
    y, x = v // side, v % side
    g = y + c * (x - y)
    r = x + c * (y - x)
    sg = side - (side - 1) * c
    sr = 1 + (side - 1) * c

    def vid(gather, reduce):
        return gather * sg + reduce * sr

    pk, hs, hg, acc = (pk0, pk1, pk2), (hs0, hs1, hs2), (hg0, hg1, hg2), (acc0, acc1, acc2)
    bs, bx, bm = (bs0, bs1, bs2), (bx0, bx1, bx2), (bm0, bm1, bm2)
    started = []

    def go(*args, **device):
        copy = send(*args, **device)
        started.append(copy)
        return copy

    occ_in = pltpu.make_async_copy(occ_h, occ_v, in_sem.at[s.nq])
    occ_in.start()
    zero_rows = jnp.zeros((s.shift, s.nu), BF16)
    loads = []
    for q in range(s.nq):
        if s.shift:
            ibuf[q, 0 : s.shift, :] = zero_rows
            ibuf[q, s.mu : s.mu + s.shift, :] = zero_rows
        copy = pltpu.make_async_copy(
            int_h.at[q], ibuf.at[q, pl.ds(pl.multiple_of(s.shift * c, 16), s.mu), :], in_sem.at[q]
        )
        copy.start()
        loads.append(copy)
    own_v = []
    for w in range(side):
        start = pl.multiple_of(s.block * vid(g, w), 16)
        copy = pltpu.make_async_copy(
            vir_h.at[pl.ds(start, s.rows), :], vb.at[0, pl.ds(w * s.lanes, s.rows), :], v_own.at[w]
        )
        copy.start()
        own_v.append(copy)

    for group in range(3):
        pk[group][...] = jnp.zeros(pk[group].shape, F32)
    rp[...] = jnp.zeros(rp.shape, F32)
    for d in range(side):
        for w in range(side):
            vb[d, w * s.lanes + s.rows : (w + 1) * s.lanes, :] = jnp.zeros((s.lanes - s.rows, s.nu), BF16)

    barrier = pltpu.get_barrier_semaphore()
    me = 2 * z + c
    for d in range(1, 2 * nz):
        other = (me + d) % (2 * nz)
        pl.semaphore_signal(barrier, inc=1, device_id={"aux": other // 2, "occ": other % 2}, device_id_type=MESH)
    for d in range(1, side * side):
        pl.semaphore_signal(barrier, inc=1, device_id={"vir": (v + d) % (side * side)}, device_id_type=MESH)
    pl.semaphore_wait(barrier, 2 * nz + side * side - 2)

    v_copies = {}
    for e in range(1, side):
        to = (g + e) % side
        for w in range(side):
            start = pl.multiple_of(s.block * vid(to, w), 16)
            v_copies[side - e, w] = go(
                vir_h.at[pl.ds(start, s.rows), :], vb.at[side - e, pl.ds(w * s.lanes, s.rows), :], v_s.at[e - 1, w], v_r.at[side - e - 1, w],
                vir=vid(to, r),
            )
    shift[...] = jnp.full((8, 128), shift_s[0], F32)
    for e in range(1, nz):
        go(shift, sh.at[z], sh_s.at[e - 1], sh_r.at[z], aux=(z + e) % nz)
    sh[z] = shift[...]

    occ_in.wait()
    x_copies = []
    for q in range(s.nq):
        loads[q].wait()
        columns = occ_v[:, pl.ds(pl.multiple_of(s.lane0 * c, 128), s.window)]
        pf[q] = dot(columns, ibuf[q])
        x_copies.append(
            go(pf.at[q, pl.ds(pl.multiple_of(s.half * (1 - c), 8), s.half), :], xf.at[q], x_s.at[q], x_r.at[q], occ=1 - c)
        )
    for q in range(s.nq):
        x_copies[q].wait_recv()
        xf[q] = xf[q] + pf[q, pl.ds(pl.multiple_of(s.half * c, 8), s.half), :]
        for group, (j0, count) in enumerate(s.groups):
            for to in range(nz):
                pk[group][to, q * count : (q + 1) * count, :] = xf[q, to * s.jb + j0 : to * s.jb + j0 + count, :]
    near_first = [d for pair in zip(range(1, nz // 2), range(nz - 1, nz // 2, -1)) for d in pair] + [nz // 2]

    def scatter(group):
        hs[group][...] = pk[group][...].astype(BF16)
        for e in near_first:
            to = (z + e) % nz
            go(hs[group].at[to], hg[group].at[0, z], h_s.at[group, e - 1], h_r.at[group, z], aux=to)
        hg[group][0, z] = hs[group][z]

    scatter(0)
    scatter(1)
    for q in range(s.nq):
        hq[q] = xf[q].astype(BF16)
    start = 128 * ((s.nu * v) // 128) - 128 * ((v + 1) // (side * side))
    view = occ_v[:, pl.ds(pl.multiple_of(start, 128), s.view)].astype(F32)
    wide = -(-s.view // 128) * 128
    view = jnp.concatenate([view, jnp.zeros((s.nocc, wide - s.view), F32)], axis=1)
    sec[...] = pltpu.roll(view, wide - (s.nu * v - start), 1)[:, : s.nu].astype(BF16)
    weights = split(dot(trial[...], sec[...]))

    for q in range(s.nq):
        both = dot_nt(weights, hq[q])
        rp[q * s.nvec : (q + 1) * s.nvec, 0 : s.half] = both[: s.nvec] + both[s.nvec :]
    for e in range(1, side):
        go(rp, rg.at[side - e], rg_s.at[e - 1], rg_r.at[side - e - 1], vir=vid((g + e) % side, r))
    for q in range(s.nq):
        hp[q] = dot_nt(hq[q], sec[...]).astype(BF16)

    ve8[...] = jnp.ones(ve8.shape, F32)
    ve8[:, 0 : s.na] = jnp.broadcast_to(ve[...], (8, s.na))
    bflat[...] = jnp.ones(bflat.shape, F32)
    first = s.half * c + s.jb * z
    for j in range(s.jb):
        bflat[0:8, j * s.na : (j + 1) * s.na] = ve8[:, 0 : s.na] - eo_s[first + j]
    for tile in range(s.tiles):
        base[tile] = bflat[0:8, tile * s.tile : (tile + 1) * s.tile]
    square = jnp.broadcast_to(eo_row[...], (128, s.nocc))
    fill = -(-s.nocc // 128) * 128 - s.nocc
    eob[...] = jnp.concatenate([square, jnp.zeros((128, fill), F32)], axis=1).T[: s.nocc]

    def arrived(dst, recv_sem):
        pltpu.make_async_remote_copy(
            src_ref=dst, dst_ref=dst, send_sem=recv_sem, recv_sem=recv_sem, device_id={"occ": c}, device_id_type=MESH
        ).wait_recv()

    ahead, behind = vid((g + 1) % side, r), vid((g + 3) % side, r)
    halves = (pl.ds(0, nz // 2), pl.ds(nz // 2, nz // 2))

    def gather(group):
        for d in near_first:
            source = (z + d) % nz
            arrived(hg[group].at[0, source], h_r.at[group, source])
        for n in range(2):
            for to, slot, part in ((behind, 1, n), (ahead, 3, 1 - n)):
                part_ref = hg[group].at[0, halves[part]]
                go(
                    part_ref, hg[group].at[slot, halves[part]], g_s.at[group, slot - 1, part], g_r.at[group, slot - 1, part],
                    vir=to,
                )

    def relay(group):
        for slot, to, part in ((1, behind, 0), (3, ahead, 1)):
            arrived(hg[group].at[slot, halves[part]], g_r.at[group, slot - 1, part])
            go(
                hg[group].at[slot, halves[part]], hg[group].at[2, halves[part]], g_s.at[group, 1, part],
                g_r.at[group, 1, part], vir=to,
            )

    def gathered(group, slot):
        for part in range(2):
            if (slot, part) not in ((1, 0), (3, 1)):
                arrived(hg[group].at[slot, halves[part]], g_r.at[group, slot - 1, part])

    def term(group, d):
        return dot_nt(hg[group][d].reshape(nz * s.packs[group], s.nu), vb[d])

    def product(group, slots):
        value = term(group, slots[0])
        for d in slots[1:]:
            value = value + term(group, d)
        acc[group][...] = value if slots[0] == 0 else value + acc[group][...]

    def columns_of(w):
        return pl.ds(pl.multiple_of(w * s.lanes, 128), s.lanes)

    right, left = vid(g, (r + 1) % side), vid(g, (r + 3) % side)

    def parts_of(group):
        size = nz * s.packs[group] // 2
        return pl.ds(0, size), pl.ds(size, size)

    def reduce_start(group):
        low, high = parts_of(group)
        for e in (2, 1, 3):
            bs[group][e - 1] = acc[group][:, columns_of((r + e) % side)].astype(BF16)
            if e == 2:
                go(bs[group].at[1, low], bm[group].at[0], m_s.at[group, 0], m_r.at[group, 0], vir=right)
                go(bs[group].at[1, high], bm[group].at[1], m_s.at[group, 1], m_r.at[group, 1], vir=left)
            if e == 1:
                go(bs[group].at[0, high], bx[group].at[0, high], b_s.at[group, 0, 1], b_r.at[group, 0, 1], vir=right)
            if e == 3:
                go(bs[group].at[2, low], bx[group].at[1, low], b_s.at[group, 1, 0], b_r.at[group, 1, 0], vir=left)

    def reduce_merge(group):
        low, high = parts_of(group)
        arrived(bm[group].at[0], m_r.at[group, 0])
        merged = acc[group][low, columns_of((r + 1) % side)] + bm[group][0].astype(F32)
        bs[group][0, low, :] = merged.astype(BF16)
        go(bs[group].at[0, low], bx[group].at[0, low], b_s.at[group, 0, 0], b_r.at[group, 0, 0], vir=right)
        arrived(bm[group].at[1], m_r.at[group, 1])
        merged = acc[group][high, columns_of((r + 3) % side)] + bm[group][1].astype(F32)
        bs[group][2, high, :] = merged.astype(BF16)
        go(bs[group].at[2, high], bx[group].at[1, high], b_s.at[group, 1, 1], b_r.at[group, 1, 1], vir=left)

    nq8 = s.nq * s.nvec
    total = rp[...]
    for d in range(1, side):
        arrived(rg.at[d], rg_r.at[d - 1])
        total = total + rg[d]
    rx[0] = total
    for e in range(1, side):
        go(rx.at[0], rx.at[side - e], rx_s.at[e - 1], rx_r.at[side - e - 1], vir=vid(g, (r + e) % side))
    gather(0)
    total = rx[0]
    for d in range(1, side):
        arrived(rx.at[d], rx_r.at[d - 1])
        total = total + rx[d]
    rmsg[...] = total.astype(BF16)
    own_rows = pl.ds(pl.multiple_of(z * nq8, 16), nq8)
    for e in near_first:
        go(rmsg, rall.at[c, own_rows, :], rz_s.at[e - 1], rz_r.at[z], aux=(z + e) % nz)
    rall[c, own_rows, :] = rmsg[...]
    scatter(2)
    for w in range(side):
        own_v[w].wait()
    product(0, (0,))
    relay(0)
    gather(1)
    gathered(0, 1)
    gathered(0, 3)
    for d in range(1, side):
        for w in range(side):
            v_copies[d, w].wait_recv()
    product(0, (1, 3))
    gathered(0, 2)
    product(0, (2,))
    reduce_start(0)
    product(1, (0,))
    relay(1)
    reduce_merge(0)
    gathered(1, 1)
    gathered(1, 3)
    product(1, (1, 3))
    gathered(1, 2)
    product(1, (2,))
    reduce_start(1)
    for d in near_first:
        source = (z + d) % nz
        arrived(rall.at[c, pl.ds(pl.multiple_of(source * nq8, 16), nq8), :], rz_r.at[source])
        arrived(sh.at[source], sh_r.at[source])
    go(rall.at[c], rall.at[c], rc_s, rc_r, occ=1 - c)
    gather(2)
    arrived(rall.at[1 - c], rc_r)
    for h in range(2):
        for part in range(s.parts):
            rl[h, part] = rall[h, :, part * 128 : (part + 1) * 128].astype(F32)
    for n in range(s.nvec):
        for h in range(2):
            sides = []
            for part in range(s.parts):
                rows = [rl[h, part, pl.ds(q * s.nvec + n, nz, stride=nq8), :] for q in range(s.nq)]
                sides.append(jnp.concatenate(rows, axis=0))
            rm32[n, h * s.half : (h + 1) * s.half, :] = jnp.concatenate(sides, axis=1).T[: s.half]
        rm[n * s.nocc : (n + 1) * s.nocc, :] = rm32[n].astype(BF16)
        row[n * s.nocc : (n + 1) * s.nocc, :] = jnp.broadcast_to(sh[n][0:1, :], (s.nocc, 128)) - eob[...]
    reduce_merge(1)
    product(2, (0,))
    relay(2)

    def build(group):
        j0, count = s.groups[group]
        pack = s.packs[group]
        for side_of in range(2):
            for part, rows in enumerate(parts_of(group)):
                arrived(bx[group].at[side_of, rows], b_r.at[group, side_of, part])

        @pl.loop(0, nz)
        def _(source):
            rows = pl.ds(pl.multiple_of(source * pack, 16), pack)
            value = acc[group][rows, columns_of(r)] + bx[group][0, rows, :].astype(F32) + bx[group][1, rows, :].astype(F32)
            full = pltpu.roll(value.astype(BF16).astype(F32), s.lanes - v, 1)
            for part in range(s.lanes // 128):
                bf[part, rows, :] = full[:, part * 128 : (part + 1) * 128]

        for j in range(count):
            parts = []
            for part in range(s.lanes // 128):
                rows = [bf[part, pl.ds(q * count + j, nz, stride=pack), :] for q in range(s.nq)]
                parts.append(jnp.concatenate(rows, axis=0))
            bflat[:, (j0 + j) * s.na : (j0 + j + 1) * s.na] = jnp.concatenate(parts, axis=1)[:, : s.na]

    def ready(group):
        build(group)
        start, count = s.spans[group]
        for tile in range(start, start + count):
            flat = bflat[:, tile * s.tile : (tile + 1) * s.tile]
            bj[tile] = flat.astype(BF16)
            bjt[tile] = flat.T.astype(BF16)

    tall = 4 * s.nocc
    coupled, weighted = (coupled0, coupled1), (weighted0, weighted1)

    def rows_of(step, tiles):
        return pl.ds(pl.multiple_of(step // tiles * tall, 16), tall)

    def couple(step, slot, start, tiles):
        coupled[slot][...] = dot(rm[rows_of(step, tiles), :], bj[start + step % tiles])

    def weigh(step, slot, start, tiles):
        own = row[rows_of(step, tiles), :]
        divisor = jnp.concatenate([own] * (s.tile // 128), axis=1) + base[start + step % tiles, 0:1, :]
        weighted[slot][...] = (coupled[slot][...] * pl.reciprocal(divisor, approx=True, full_range=False)).astype(BF16)

    def fold(step, slot, start, tiles):
        fa[rows_of(step, tiles), :] += dot(weighted[slot][...], bjt[start + step % tiles])

    def half_step(half, span):
        for slot in range(2):
            step = 2 * half + slot
            fold(step - 2, slot, *span)
            weigh(step - 1, 1 - slot, *span)
            couple(step, slot, *span)

    def advance(span, after=None):
        @pl.loop(1, span[1])
        def _(half):
            half_step(half, span)
            if after is not None:
                after(half)

    def bridge(span, later):
        last = 2 * span[1] - 1
        fold(last - 1, 0, *span)
        weigh(last, 1, *span)
        couple(0, 0, *later)
        fold(last, 1, *span)
        weigh(0, 0, *later)
        couple(1, 1, *later)

    fa[...] = jnp.zeros(fa.shape, F32)
    bflat[:, s.tiles * s.tile - 128 :] = jnp.zeros((s.q, 128), F32)
    ready(0)
    spans = s.spans
    couple(0, 0, *spans[0])
    couple(1, 1, *spans[0])
    weigh(0, 0, *spans[0])
    for half in range(1, spans[0][1]):
        half_step(half, spans[0])
        if half == 1:
            gathered(2, 1)
            gathered(2, 3)
            product(2, (1, 3))
            gathered(2, 2)
            product(2, (2,))
            reduce_start(2)
    reduce_merge(2)
    ready(1)
    bridge(spans[0], spans[1])
    advance(spans[1])
    ready(2)
    bridge(spans[1], spans[2])

    rows4 = 4 * s.nq
    around = side * side

    def to_owner(u, d):
        other = (me + d) % (2 * nz)
        return pltpu.make_async_remote_copy(
            src_ref=fb.at[u, other % 2, pl.ds(pl.multiple_of(other // 2 * rows4, 16), rows4), :], dst_ref=fr.at[u, me],
            send_sem=fz_s.at[u, d - 1], recv_sem=fz_r.at[u, me],
            device_id={"aux": other // 2, "occ": other % 2}, device_id_type=MESH,
        )

    def to_plane(u, d):
        return pltpu.make_async_remote_copy(
            src_ref=fp.at[u], dst_ref=fq.at[u, v], send_sem=fp_s.at[u, d - 1], recv_sem=fp_r.at[u, v],
            device_id={"vir": (v + d) % around}, device_id_type=MESH,
        )

    def finish(u):
        for m in range(4):
            for h in range(2):
                start = u * tall + m * s.nocc + h * s.half
                flip = fa[start : start + s.half, :].T
                flip = jnp.concatenate([flip, jnp.zeros((s.q, s.parts * 128 - s.half), F32)], axis=1)
                for part in range(s.parts):
                    for q in range(s.nq):
                        fl[h, part, pl.ds(m * s.nq + q, nz, stride=rows4), :] = flip[
                            q * nz : (q + 1) * nz, part * 128 : (part + 1) * 128
                        ]
        for h in range(2):
            fb[u, h] = jnp.concatenate([fl[h, part] for part in range(s.parts)], axis=1).astype(BF16)
        for d in range(1, 2 * nz):
            to_owner(u, d).start()
        fr[u, me] = fb[u, c, pl.ds(pl.multiple_of(z * rows4, 16), rows4), :]

    def pass_on(u):
        for d in range(1, 2 * nz):
            other = (me + d) % (2 * nz)
            arrived(fr.at[u, other], fz_r.at[u, other])
        total = fr[u, 0].astype(F32)
        for other in range(1, 2 * nz):
            total = total + fr[u, other].astype(F32)
        fp[u] = total.astype(BF16)
        for d in range(1, around):
            to_plane(u, d).start()
        fq[u, v] = fp[u]

    def apply(u):
        for d in range(1, around):
            other = (v + d) % around
            arrived(fq.at[u, other], fp_r.at[u, other])
        total = fq[u, 0].astype(F32)
        for other in range(1, around):
            total = total + fq[u, other].astype(F32)
        folded = split(total[:, : s.half])
        owner = lax.broadcasted_iota(jnp.int32, folded.shape, 0) % s.nq
        both = None
        for q in range(s.nq):
            value = dot(jnp.where(owner == q, folded.astype(F32), 0.0).astype(BF16), hp[q])
            both = value if both is None else both + value
        spart[...] = both[:rows4] + both[rows4:]
        for m in range(4):
            value = spart[m * s.nq : m * s.nq + 1, :]
            for q in range(1, s.nq):
                value = value + spart[m * s.nq + q : m * s.nq + q + 1, :]
            sgs[4 * u + m] = value

    late = spans[2][1]

    def serve(half):
        @pl.when(half == late // 2)
        def _():
            finish(0)

        @pl.when(half == late - 1)
        def _():
            pass_on(0)

    advance(spans[2], serve)
    fold(2 * late - 2, 0, *spans[2])
    weigh(2 * late - 1, 1, *spans[2])
    fold(2 * late - 1, 1, *spans[2])
    finish(1)
    for copy in started:
        copy.wait_send()
    started.clear()
    apply(0)
    pass_on(1)
    for u in range(2):
        for d in range(1, 2 * nz):
            to_owner(u, d).wait_send()
    apply(1)
    for d in range(1, 2 * nz):
        other = (me + d) % (2 * nz)
        go(sgs.at[other // 2], sgr.at[me], s1_s.at[d - 1], s1_r.at[me], aux=other // 2, occ=other % 2)
    sgr[me] = sgs[z]
    for d in range(1, 2 * nz):
        other = (me + d) % (2 * nz)
        arrived(sgr.at[other], s1_r.at[other])
    total = sgr[0]
    for d in range(1, 2 * nz):
        total = total + sgr[d]
    spp[...] = total
    for d in range(1, side * side):
        go(spp, spr.at[v], s2_s.at[d - 1], s2_r.at[v], vir=(v + d) % (side * side))
    spr[v] = total
    for d in range(1, side * side):
        other = (v + d) % (side * side)
        arrived(spr.at[other], s2_r.at[other])
    total = spr[0]
    for d in range(1, side * side):
        total = total + spr[d]
    out[...] = total
    for copy in started:
        copy.wait_send()
    for u in range(2):
        for d in range(1, around):
            to_plane(u, d).wait_send()


def output_kernel(terms, trial, eo_row, sigma_out, sub_out, t32):
    t32[...] = trial[...].astype(F32)
    sigma = eo_row[...] * t32[pl.ds(lax.axis_index("aux"), 1), :] + terms[...]
    sigma_out[...] = sigma
    column = jnp.sum(t32[...] * sigma, axis=1, keepdims=True)
    sub_out[...] = jnp.broadcast_to(column, (column.shape[0], 128)).T[0:1]


def local(mesh, integrals, occ_coeffs, vir_coeffs, occ_energy, vir_energy, trial_vectors, shifts):
    s = Sizes(mesh, integrals, occ_coeffs, vir_energy)
    nz, side = s.nz, s.side
    vmem = pltpu.VMEM
    nq8 = s.nq * s.nvec
    rows4 = 4 * s.nq
    dma = lambda *shape: pltpu.SemaphoreType.DMA(shape)
    near = side - 1
    one = pltpu.SemaphoreType.DMA
    tall = 4 * s.nocc
    flat = s.parts * 128
    scratch = [
        vmem((s.tiles, s.q, s.tile), BF16),
        vmem((s.tiles, s.tile, s.q), BF16),
        vmem((s.tiles, 8, s.tile), F32),
        vmem((s.nvec * s.nocc, s.q), BF16),
        vmem((s.nvec * s.nocc, 128), F32),
        vmem((s.nq, s.half, s.nu), BF16),
        vmem((s.nocc, s.nu), BF16),
        vmem((s.nvec * s.nocc, s.q), F32),
        vmem((tall, s.tile), F32),
        vmem((tall, s.tile), F32),
        vmem((tall, s.tile), BF16),
        vmem((tall, s.tile), BF16),
        vmem((s.nq, s.half, s.nocc), BF16),
        vmem((2, s.parts, nz * rows4, 128), F32),
        vmem((s.quads, 2, nz * rows4, flat), BF16),
        vmem((s.quads, 2 * nz, rows4, flat), BF16),
        vmem((s.quads, rows4, flat), BF16),
        vmem((s.quads, side * side, rows4, flat), BF16),
        vmem((rows4, s.nocc), F32),
        vmem((nz, 1, s.nocc), F32),
        vmem((2 * nz, 1, s.nocc), F32),
        vmem((1, s.nocc), F32),
        vmem((side * side, 1, s.nocc), F32),
        vmem((s.nq, s.window, s.nu), BF16),
        vmem((s.nocc, s.ao), BF16),
        vmem((s.nq, s.nocc, s.nu), F32),
        vmem((s.nq, s.half, s.nu), F32),
        *[vmem((nz, pack, s.nu), F32) for pack in s.packs],
        *[vmem((nz, pack, s.nu), BF16) for pack in s.packs],
        *[vmem((side, nz, pack, s.nu), BF16) for pack in s.packs],
        vmem((side, side * s.lanes, s.nu), BF16),
        *[vmem((nz * pack, side * s.lanes), F32) for pack in s.packs],
        *[vmem((side - 1, nz * pack, s.lanes), BF16) for pack in s.packs],
        *[vmem((2, nz * pack, s.lanes), BF16) for pack in s.packs],
        *[vmem((2, nz * pack // 2, s.lanes), BF16) for pack in s.packs],
        vmem((s.lanes // 128, nz * max(s.packs), 128), F32),
        vmem((s.q, s.tiles * s.tile), F32),
        vmem((s.nocc, 128), F32),
        vmem((8, s.lanes), F32),
        vmem((8, 128), F32),
        vmem((nq8, flat), F32),
        vmem((side, nq8, flat), F32),
        vmem((side, nq8, flat), F32),
        vmem((nq8, flat), BF16),
        vmem((2, nz * nq8, flat), BF16),
        vmem((2, s.parts, nz * nq8, 128), F32),
        vmem((s.nvec, s.nocc, s.q), F32),
        vmem((nz, 8, 128), F32),
        dma(s.nq + 1), dma(side), dma(near, side), dma(near, side), dma(nz), dma(nz),
        dma(s.nq), dma(s.nq), dma(3, nz), dma(3, nz), dma(3, near, 2), dma(3, near, 2),
        dma(near), dma(near), dma(near), dma(near), dma(nz), dma(nz), one, one,
        dma(3, 2, 2), dma(3, 2, 2), dma(3, 2), dma(3, 2),
        dma(s.quads, 2 * nz), dma(s.quads, 2 * nz), dma(s.quads, side * side), dma(s.quads, side * side), dma(2 * nz), dma(2 * nz), dma(side * side), dma(side * side),
    ]
    hbm = pl.BlockSpec(memory_space=pl.ANY)
    fast = pl.BlockSpec(memory_space=pltpu.VMEM)
    scalars = pl.BlockSpec(memory_space=pltpu.SMEM)
    shape = jax.ShapeDtypeStruct
    limit = 56 * 1024 * 1024
    occ_row, trial_rows = occ_energy[None], trial_vectors.T
    terms = pl.pallas_call(
        functools.partial(kernel, s),
        out_shape=shape((1, s.nocc), F32),
        in_specs=[hbm, hbm, hbm, fast, fast, scalars, fast, scalars],
        out_specs=fast,
        scratch_shapes=scratch,
        compiler_params=pltpu.CompilerParams(collective_id=0, has_side_effects=True, vmem_limit_bytes=limit),
    )(integrals, occ_coeffs.T, vir_coeffs.T, trial_rows, occ_row, occ_energy, vir_energy[None], shifts)
    sigma, sub = pl.pallas_call(
        output_kernel,
        out_shape=(shape((1, s.nocc), F32), shape((1, s.nvec), F32)),
        in_specs=[fast] * 3,
        out_specs=(fast, fast),
        scratch_shapes=[vmem((s.nvec, s.nocc), F32)],
    )(terms, trial_rows, occ_row)
    return sigma.T, sub.T


def solution(mesh):
    return jax.shard_map(
        functools.partial(local, dict(mesh.shape)),
        mesh=mesh,
        in_specs=(P("aux", "occ", "vir"), P(), P("vir", None), P(), P("vir"), P(), P("aux")),
        out_specs=(P(None, "aux"), P(None, "aux")),
        check_vma=False,
    )
```

```python
import functools
import math

import jax
import jax.numpy as jnp
from jax import lax
from jax.experimental import pallas as pl
from jax.experimental.pallas import tpu as pltpu
from jax.sharding import PartitionSpec as P

MESH = pl.DeviceIdType.MESH
F32 = jnp.float32
BF16 = jnp.bfloat16


def dot(a, b):
    return jnp.dot(a, b, preferred_element_type=F32)


def dot_nt(a, b):
    return lax.dot_general(a, b, (((1,), (1,)), ((), ())), preferred_element_type=F32)


def split(value):
    high = value.astype(BF16)
    low = (value - high.astype(F32)).astype(BF16)
    return jnp.concatenate([high.astype(F32), low.astype(F32)], axis=0).astype(BF16)


def remote(src, dst, send_sem, recv_sem, **device):
    return pltpu.make_async_remote_copy(
        src_ref=src, dst_ref=dst, send_sem=send_sem, recv_sem=recv_sem, device_id=device, device_id_type=MESH
    )


class Sizes:
    def __init__(self, mesh, integrals, occ_coeffs, vir_energy):
        self.nz = mesh["aux"]
        self.side = math.isqrt(mesh["vir"])
        self.nq, self.mu, self.nu = integrals.shape
        self.ao, self.nocc = occ_coeffs.shape
        self.half = self.nocc // 2
        self.jb = self.half // self.nz
        self.na = vir_energy.shape[0]
        self.block = 16 * (self.na // 16)
        self.rows = self.block + 16
        assert self.na == self.block + 1 and self.side == 4
        third = self.jb // 12 * 4
        self.groups = [(0, third), (third, third), (2 * third, self.jb - 2 * third)]
        self.packs = [-(-(self.nq * count) // 16) * 16 for _, count in self.groups]
        self.tile = 512
        self.tiles = -(-(self.jb * self.na) // self.tile)
        ends = [(j0 + count) * self.na // self.tile for j0, count in self.groups[:-1]] + [self.tiles]
        self.spans = [(start, end - start) for start, end in zip([0] + ends, ends)]
        self.quads = self.nz // 4
        self.lane0 = self.mu // 128 * 128
        self.shift = self.mu - self.lane0
        self.window = self.mu + self.shift
        self.lanes = -(-self.rows // 128) * 128
        self.q = self.nq * self.nz
        self.nvec = self.nz
        self.parts = -(-self.half // 128)
        last = 128 * (self.nu * (mesh["vir"] - 1) // 128) - 128
        self.view = self.ao - last
        for v in range(mesh["vir"]):
            start = 128 * (self.nu * v // 128) - 128 * ((v + 1) // mesh["vir"])
            assert start + self.view <= self.ao and self.nu * v - start + self.nu <= self.view


def kernel(
    s, int_h, occ_h, vir_h, trial, eo_row, eo_s, ve, shift_s,
    out,
    bj, bjt, base, rm, row, hq, sec, fa, coupled0, coupled1, weighted0, weighted1,
    hp, fl, fb, fr, fp, fq, spart, sgs, sgr, spp, spr,
    ibuf, occ_v, pf, xf, pk0, pk1, pk2, hs0, hs1, hs2, hg0, hg1, hg2, vb,
    acc0, acc1, acc2, bs0, bs1, bs2, bx0, bx1, bx2, bm0, bm1, bm2, bf, bflat, eob, ve8, shift,
    rp, rg, rx, rmsg, rall, rl, rm32, sh,
    in_sem, v_own, v_s, v_r, sh_s, sh_r, x_s, x_r, h_s, h_r, g_s, g_r, rg_s, rg_r, rx_s, rx_r, rz_s, rz_r, rc_s, rc_r,
    b_s, b_r, m_r, fz_s, fz_r, fp_s, fp_r, s1_s, s1_r, s2_s, s2_r,
):
    nz, side = s.nz, s.side
    z, c, v = lax.axis_index("aux"), lax.axis_index("occ"), lax.axis_index("vir")
    y, x = v // side, v % side
    g = y + c * (x - y)
    r = x + c * (y - x)
    sg = side - (side - 1) * c
    sr = 1 + (side - 1) * c

    def vid(gather, reduce):
        return gather * sg + reduce * sr

    pk, hs, hg, acc = (pk0, pk1, pk2), (hs0, hs1, hs2), (hg0, hg1, hg2), (acc0, acc1, acc2)
    bs, bx, bm = (bs0, bs1, bs2), (bx0, bx1, bx2), (bm0, bm1, bm2)
    me = 2 * z + c
    around = side * side

    def fan(first, last, copy):
        @pl.loop(first, last)
        def _(d):
            copy(d).start()

    def go(*args, **device):
        remote(*args, **device).start()

    def arrived(ref, sem):
        remote(ref, ref, sem, sem, occ=c).wait_recv()

    def sent(ref, sem):
        remote(ref, ref, sem, sem, occ=c).wait_send()

    occ_in = pltpu.make_async_copy(occ_h, occ_v, in_sem.at[s.nq])
    occ_in.start()
    zero_rows = jnp.zeros((s.shift, s.nu), BF16)

    def load(q):
        return pltpu.make_async_copy(
            int_h.at[q], ibuf.at[q, pl.ds(pl.multiple_of(s.shift * c, 16), s.mu), :], in_sem.at[q]
        )

    for q in range(s.nq):
        if s.shift:
            ibuf[q, 0 : s.shift, :] = zero_rows
            ibuf[q, s.mu : s.mu + s.shift, :] = zero_rows
    fan(0, s.nq, load)

    def window(gather, w):
        return vir_h.at[pl.ds(pl.multiple_of(s.block * vid(gather, w), 16), s.rows), :]

    def place(slot, w):
        return vb.at[slot, pl.ds(pl.multiple_of(w * s.lanes, 16), s.rows), :]

    fan(0, side, lambda w: pltpu.make_async_copy(window(g, w), place(0, w), v_own))
    for group in range(3):
        pk[group][...] = jnp.zeros(pk[group].shape, F32)
    rp[...] = jnp.zeros(rp.shape, F32)
    for d in range(side):
        for w in range(side):
            vb[d, w * s.lanes + s.rows : (w + 1) * s.lanes, :] = jnp.zeros((s.lanes - s.rows, s.nu), BF16)

    barrier = pltpu.get_barrier_semaphore()

    @pl.loop(1, 2 * nz)
    def _(d):
        other = (me + d) % (2 * nz)
        pl.semaphore_signal(barrier, inc=1, device_id={"aux": other // 2, "occ": other % 2}, device_id_type=MESH)

    @pl.loop(1, around)
    def _(d):
        pl.semaphore_signal(barrier, inc=1, device_id={"vir": (v + d) % around}, device_id_type=MESH)

    pl.semaphore_wait(barrier, 2 * nz + around - 2)

    def v_copy(d):
        e, w = 1 + d // side, d % side
        to = (g + e) % side
        return remote(window(to, w), place(side - e, w), v_s, v_r, vir=vid(to, r))

    fan(0, (side - 1) * side, v_copy)
    shift[...] = jnp.full((8, 128), shift_s[0], F32)
    fan(1, nz, lambda d: remote(shift, sh.at[z], sh_s, sh_r, aux=(z + d) % nz))
    sh[z] = shift[...]

    occ_in.wait()

    @pl.loop(0, s.nq)
    def _(q):
        load(q).wait()
        columns = occ_v[:, pl.ds(pl.multiple_of(s.lane0 * c, 128), s.window)]
        pf[q] = dot(columns, ibuf[q])
        theirs = pf.at[q, pl.ds(pl.multiple_of(s.half * (1 - c), 8), s.half), :]
        go(theirs, xf.at[q], x_s, x_r.at[q], occ=1 - c)

    for q in range(s.nq):
        arrived(xf.at[q], x_r.at[q])
        xf[q] = xf[q] + pf[q, pl.ds(pl.multiple_of(s.half * c, 8), s.half), :]
        for group, (j0, count) in enumerate(s.groups):
            for to in range(nz):
                pk[group][to, q * count : (q + 1) * count, :] = xf[q, to * s.jb + j0 : to * s.jb + j0 + count, :]

    def scatter(group):
        hs[group][...] = pk[group][...].astype(BF16)

        def copy(d):
            to = (z + d) % nz
            return remote(hs[group].at[to], hg[group].at[0, z], h_s.at[group], h_r.at[group], aux=to)

        fan(1, nz, copy)
        hg[group][0, z] = hs[group][z]

    scatter(0)
    scatter(1)
    for q in range(s.nq):
        hq[q] = xf[q].astype(BF16)
    start = 128 * ((s.nu * v) // 128) - 128 * ((v + 1) // (side * side))
    view = occ_v[:, pl.ds(pl.multiple_of(start, 128), s.view)].astype(F32)
    wide = -(-s.view // 128) * 128
    view = jnp.concatenate([view, jnp.zeros((s.nocc, wide - s.view), F32)], axis=1)
    sec[...] = pltpu.roll(view, wide - (s.nu * v - start), 1)[:, : s.nu].astype(BF16)
    weights = split(dot(trial[...], sec[...]))

    for q in range(s.nq):
        both = dot_nt(weights, hq[q])
        rp[q * s.nvec : (q + 1) * s.nvec, 0 : s.half] = both[: s.nvec] + both[s.nvec :]
    def to_gather(d):
        return remote(rp, rg.at[side - d], rg_s, rg_r, vir=vid((g + d) % side, r))

    def to_reduce(d):
        return remote(rx.at[0], rx.at[side - d], rx_s, rx_r, vir=vid(g, (r + d) % side))

    fan(1, side, to_gather)
    for q in range(s.nq):
        hp[q] = dot_nt(hq[q], sec[...]).astype(BF16)

    ve8[...] = jnp.ones(ve8.shape, F32)
    ve8[:, 0 : s.na] = jnp.broadcast_to(ve[...], (8, s.na))
    bflat[...] = jnp.ones(bflat.shape, F32)
    first = s.half * c + s.jb * z
    for j in range(s.jb):
        bflat[0:8, j * s.na : (j + 1) * s.na] = ve8[:, 0 : s.na] - eo_s[first + j]
    for tile in range(s.tiles):
        base[tile] = bflat[0:8, tile * s.tile : (tile + 1) * s.tile]
    square = jnp.broadcast_to(eo_row[...], (128, s.nocc))
    fill = -(-s.nocc // 128) * 128 - s.nocc
    eob[...] = jnp.concatenate([square, jnp.zeros((128, fill), F32)], axis=1).T[: s.nocc]

    ahead, behind = vid((g + 1) % side, r), vid((g + 3) % side, r)
    halves = (pl.ds(0, nz // 2), pl.ds(nz // 2, nz // 2))

    def gather(group):
        arrived(hg[group].at[0, pl.ds(0, nz - 1)], h_r.at[group])
        for to, slot, part, sem in ((behind, 1, 0, 0), (ahead, 3, 1, 1), (behind, 1, 1, 2), (ahead, 3, 0, 2)):
            block = hg[group].at[0, halves[part]]
            go(block, hg[group].at[slot, halves[part]], g_s.at[group], g_r.at[group, sem], vir=to)

    def relay(group):
        for slot, to, part in ((1, behind, 0), (3, ahead, 1)):
            block = hg[group].at[slot, halves[part]]
            arrived(block, g_r.at[group, part])
            go(block, hg[group].at[2, halves[part]], g_s.at[group], g_r.at[group, 3], vir=to)

    def near_in(group):
        arrived(hg[group].at[1], g_r.at[group, 2])

    def far_in(group):
        arrived(hg[group].at[2], g_r.at[group, 3])

    def term(group, d):
        return dot_nt(hg[group][d].reshape(nz * s.packs[group], s.nu), vb[d])

    def product(group, slots):
        value = term(group, slots[0])
        for d in slots[1:]:
            value = value + term(group, d)
        acc[group][...] = value if slots[0] == 0 else value + acc[group][...]

    def columns_of(w):
        return pl.ds(pl.multiple_of(w * s.lanes, 128), s.lanes)

    right, left = vid(g, (r + 1) % side), vid(g, (r + 3) % side)

    def parts_of(group):
        size = nz * s.packs[group] // 2
        return pl.ds(0, size), pl.ds(size, size)

    def reduce_start(group):
        low, high = parts_of(group)
        for e in (2, 1, 3):
            bs[group][e - 1] = acc[group][:, columns_of((r + e) % side)].astype(BF16)
            if e == 2:
                go(bs[group].at[1, low], bm[group].at[0], b_s.at[group], m_r.at[group], vir=right)
                go(bs[group].at[1, high], bm[group].at[1], b_s.at[group], m_r.at[group], vir=left)
            if e == 1:
                go(bs[group].at[0, high], bx[group].at[0, high], b_s.at[group], b_r.at[group], vir=right)
            if e == 3:
                go(bs[group].at[2, low], bx[group].at[1, low], b_s.at[group], b_r.at[group], vir=left)

    def reduce_merge(group):
        low, high = parts_of(group)
        arrived(bm[group], m_r.at[group])
        merged = acc[group][low, columns_of((r + 1) % side)] + bm[group][0].astype(F32)
        bs[group][0, low, :] = merged.astype(BF16)
        go(bs[group].at[0, low], bx[group].at[0, low], b_s.at[group], b_r.at[group], vir=right)
        merged = acc[group][high, columns_of((r + 3) % side)] + bm[group][1].astype(F32)
        bs[group][2, high, :] = merged.astype(BF16)
        go(bs[group].at[2, high], bx[group].at[1, high], b_s.at[group], b_r.at[group], vir=left)

    nq8 = s.nq * s.nvec
    arrived(rg.at[pl.ds(1, side - 1)], rg_r)
    total = rp[...]
    for d in range(1, side):
        total = total + rg[d]
    rx[0] = total
    fan(1, side, to_reduce)
    gather(0)
    arrived(rx.at[pl.ds(1, side - 1)], rx_r)
    total = rx[0]
    for d in range(1, side):
        total = total + rx[d]
    rmsg[...] = total.astype(BF16)
    own_rows = pl.ds(pl.multiple_of(z * nq8, 16), nq8)
    fan(1, nz, lambda d: remote(rmsg, rall.at[c, own_rows, :], rz_s, rz_r, aux=(z + d) % nz))
    rall[c, own_rows, :] = rmsg[...]
    scatter(2)
    pltpu.make_async_copy(vir_h.at[pl.ds(0, side * s.rows), :], vb.at[0, pl.ds(0, side * s.rows), :], v_own).wait()
    product(0, (0,))
    relay(0)
    gather(1)
    near_in(0)
    arrived(vb.at[pl.ds(1, side - 1), pl.ds(0, side * s.rows), :], v_r)
    product(0, (1, 3))
    far_in(0)
    product(0, (2,))
    reduce_start(0)
    product(1, (0,))
    relay(1)
    reduce_merge(0)
    near_in(1)
    product(1, (1, 3))
    far_in(1)
    product(1, (2,))
    reduce_start(1)
    arrived(rall.at[c, pl.ds(0, (nz - 1) * nq8), :], rz_r)
    arrived(sh.at[pl.ds(0, nz - 1)], sh_r)
    go(rall.at[c], rall.at[c], rc_s, rc_r, occ=1 - c)
    gather(2)
    arrived(rall.at[1 - c], rc_r)
    for h in range(2):
        for part in range(s.parts):
            rl[h, part] = rall[h, :, part * 128 : (part + 1) * 128].astype(F32)
    for n in range(s.nvec):
        for h in range(2):
            sides = []
            for part in range(s.parts):
                rows = [rl[h, part, pl.ds(q * s.nvec + n, nz, stride=nq8), :] for q in range(s.nq)]
                sides.append(jnp.concatenate(rows, axis=0))
            rm32[n, h * s.half : (h + 1) * s.half, :] = jnp.concatenate(sides, axis=1).T[: s.half]
        rm[n * s.nocc : (n + 1) * s.nocc, :] = rm32[n].astype(BF16)
        row[n * s.nocc : (n + 1) * s.nocc, :] = jnp.broadcast_to(sh[n][0:1, :], (s.nocc, 128)) - eob[...]
    reduce_merge(1)
    product(2, (0,))
    relay(2)

    def build(group):
        j0, count = s.groups[group]
        pack = s.packs[group]
        arrived(bx[group], b_r.at[group])

        @pl.loop(0, nz)
        def _(source):
            rows = pl.ds(pl.multiple_of(source * pack, 16), pack)
            value = acc[group][rows, columns_of(r)] + bx[group][0, rows, :].astype(F32) + bx[group][1, rows, :].astype(F32)
            full = pltpu.roll(value.astype(BF16).astype(F32), s.lanes - v, 1)
            for part in range(s.lanes // 128):
                bf[part, rows, :] = full[:, part * 128 : (part + 1) * 128]

        for j in range(count):
            parts = []
            for part in range(s.lanes // 128):
                rows = [bf[part, pl.ds(q * count + j, nz, stride=pack), :] for q in range(s.nq)]
                parts.append(jnp.concatenate(rows, axis=0))
            bflat[:, (j0 + j) * s.na : (j0 + j + 1) * s.na] = jnp.concatenate(parts, axis=1)[:, : s.na]

    def ready(group):
        build(group)
        start, count = s.spans[group]
        for tile in range(start, start + count):
            flat = bflat[:, tile * s.tile : (tile + 1) * s.tile]
            bj[tile] = flat.astype(BF16)
            bjt[tile] = flat.T.astype(BF16)

    tall = 4 * s.nocc
    coupled, weighted = (coupled0, coupled1), (weighted0, weighted1)

    def couple(slot, tile, quad):
        coupled[slot][...] = dot(rm[pl.ds(pl.multiple_of(quad * tall, 16), tall), :], bj[tile])

    def weigh(slot, tile, quad):
        own = row[pl.ds(pl.multiple_of(quad * tall, 8), tall), :]
        divisor = jnp.concatenate([own] * (s.tile // 128), axis=1) + base[tile, 0:1, :]
        weighted[slot][...] = (coupled[slot][...] * pl.reciprocal(divisor, approx=True, full_range=False)).astype(BF16)

    def fold(slot, tile, quad):
        fa[pl.ds(pl.multiple_of(quad * tall, 8), tall), :] += dot(weighted[slot][...], bjt[tile])

    def advance(older, old, new, newer):
        fold(0, *older)
        weigh(1, *old)
        couple(0, *new)
        fold(1, *old)
        weigh(0, *new)
        couple(1, *newer)

    fa[...] = jnp.zeros(fa.shape, F32)
    bflat[:, s.tiles * s.tile - 128 :] = jnp.zeros((s.q, 128), F32)
    ready(0)
    couple(0, 0, 0)
    couple(1, 0, 1)
    weigh(0, 0, 0)
    second, third = s.spans[1][0], s.spans[2][0]

    @pl.loop(1, third)
    def _(tile):
        @pl.when(tile == 2)
        def _():
            near_in(2)
            product(2, (1, 3))
            far_in(2)
            product(2, (2,))
            reduce_start(2)

        @pl.when(tile == second)
        def _():
            reduce_merge(2)
            ready(1)

        advance((tile - 1, 0), (tile - 1, 1), (tile, 0), (tile, 1))

    ready(2)
    advance((third - 1, 0), (third - 1, 1), (third, 0), (third + 1, 0))

    rows4 = 4 * s.nq

    def to_owner(u, d):
        other = (me + d) % (2 * nz)
        return pltpu.make_async_remote_copy(
            src_ref=fb.at[u, other % 2, pl.ds(pl.multiple_of(other // 2 * rows4, 16), rows4), :], dst_ref=fr.at[u, me],
            send_sem=fz_s.at[u], recv_sem=fz_r.at[u],
            device_id={"aux": other // 2, "occ": other % 2}, device_id_type=MESH,
        )

    def to_plane(u, d):
        return pltpu.make_async_remote_copy(
            src_ref=fp.at[u], dst_ref=fq.at[u, v], send_sem=fp_s.at[u], recv_sem=fp_r.at[u],
            device_id={"vir": (v + d) % around}, device_id_type=MESH,
        )

    def finish(u):
        for m in range(4):
            for h in range(2):
                start = u * tall + m * s.nocc + h * s.half
                flip = fa[start : start + s.half, :].T
                flip = jnp.concatenate([flip, jnp.zeros((s.q, s.parts * 128 - s.half), F32)], axis=1)
                for part in range(s.parts):
                    for q in range(s.nq):
                        fl[h, part, pl.ds(m * s.nq + q, nz, stride=rows4), :] = flip[
                            q * nz : (q + 1) * nz, part * 128 : (part + 1) * 128
                        ]
        for h in range(2):
            fb[u, h] = jnp.concatenate([fl[h, part] for part in range(s.parts)], axis=1).astype(BF16)
        fan(1, 2 * nz, functools.partial(to_owner, u))
        fr[u, me] = fb[u, c, pl.ds(pl.multiple_of(z * rows4, 16), rows4), :]

    def pass_on(u):
        arrived(fr.at[u, pl.ds(0, 2 * nz - 1)], fz_r.at[u])
        total = fr[u, 0].astype(F32)
        for other in range(1, 2 * nz):
            total = total + fr[u, other].astype(F32)
        fp[u] = total.astype(BF16)
        fan(1, around, functools.partial(to_plane, u))
        fq[u, v] = fp[u]

    def apply(u):
        arrived(fq.at[u, pl.ds(0, around - 1)], fp_r.at[u])
        total = fq[u, 0].astype(F32)
        for other in range(1, around):
            total = total + fq[u, other].astype(F32)
        folded = split(total[:, : s.half])
        owner = lax.broadcasted_iota(jnp.int32, folded.shape, 0) % s.nq
        both = None
        for q in range(s.nq):
            value = dot(jnp.where(owner == q, folded.astype(F32), 0.0).astype(BF16), hp[q])
            both = value if both is None else both + value
        spart[...] = both[:rows4] + both[rows4:]
        for m in range(4):
            value = spart[m * s.nq : m * s.nq + 1, :]
            for q in range(1, s.nq):
                value = value + spart[m * s.nq + q : m * s.nq + q + 1, :]
            sgs[4 * u + m] = value

    late = s.spans[2][1]

    def pair(step):
        return third + step % late, step // late

    @pl.loop(1, late)
    def _(half):
        step = 2 * half
        advance(pair(step - 2), pair(step - 1), pair(step), pair(step + 1))

        @pl.when(half == late // 2)
        def _():
            finish(0)

        @pl.when(half == late - 1)
        def _():
            pass_on(0)

    last = 2 * late - 1
    fold(0, *pair(last - 1))
    weigh(1, *pair(last))
    fold(1, *pair(last))
    finish(1)
    for group in range(3):
        sent(hs[group].at[pl.ds(0, nz - 1)], h_s.at[group])
        sent(hg[group].at[pl.ds(0, side - 1)], g_s.at[group])
        sent(bs[group], b_s.at[group])
    sent(vir_h.at[pl.ds(0, (side - 1) * side * s.rows), :], v_s)
    sent(sh.at[pl.ds(0, nz - 1)], sh_s)
    sent(xf, x_s)
    sent(rg.at[pl.ds(1, side - 1)], rg_s)
    sent(rx.at[pl.ds(1, side - 1)], rx_s)
    sent(rall.at[c, pl.ds(0, (nz - 1) * nq8), :], rz_s)
    sent(rall.at[c], rc_s)
    apply(0)
    pass_on(1)
    for u in range(2):
        sent(fr.at[u, pl.ds(0, 2 * nz - 1)], fz_s.at[u])
    apply(1)

    def to_aux(d):
        other = (me + d) % (2 * nz)
        return remote(sgs.at[other // 2], sgr.at[me], s1_s, s1_r, aux=other // 2, occ=other % 2)

    fan(1, 2 * nz, to_aux)
    sgr[me] = sgs[z]
    arrived(sgr.at[pl.ds(0, 2 * nz - 1)], s1_r)
    total = sgr[0]
    for d in range(1, 2 * nz):
        total = total + sgr[d]
    spp[...] = total
    fan(1, around, lambda d: remote(spp, spr.at[v], s2_s, s2_r, vir=(v + d) % around))
    spr[v] = total
    arrived(spr.at[pl.ds(0, around - 1)], s2_r)
    total = spr[0]
    for d in range(1, side * side):
        total = total + spr[d]
    out[...] = total
    for u in range(2):
        sent(fq.at[u, pl.ds(0, around - 1)], fp_s.at[u])
    sent(sgr.at[pl.ds(0, 2 * nz - 1)], s1_s)
    sent(spr.at[pl.ds(0, around - 1)], s2_s)


def output_kernel(terms, trial, eo_row, sigma_out, sub_out, t32):
    t32[...] = trial[...].astype(F32)
    sigma = eo_row[...] * t32[pl.ds(lax.axis_index("aux"), 1), :] + terms[...]
    sigma_out[...] = sigma
    column = jnp.sum(t32[...] * sigma, axis=1, keepdims=True)
    sub_out[...] = jnp.broadcast_to(column, (column.shape[0], 128)).T[0:1]


def local(mesh, integrals, occ_coeffs, vir_coeffs, occ_energy, vir_energy, trial_vectors, shifts):
    s = Sizes(mesh, integrals, occ_coeffs, vir_energy)
    nz, side = s.nz, s.side
    vmem = pltpu.VMEM
    nq8 = s.nq * s.nvec
    rows4 = 4 * s.nq
    dma = lambda *shape: pltpu.SemaphoreType.DMA(shape)
    one = pltpu.SemaphoreType.DMA
    tall = 4 * s.nocc
    flat = s.parts * 128
    scratch = [
        vmem((s.tiles, s.q, s.tile), BF16),
        vmem((s.tiles, s.tile, s.q), BF16),
        vmem((s.tiles, 8, s.tile), F32),
        vmem((s.nvec * s.nocc, s.q), BF16),
        vmem((s.nvec * s.nocc, 128), F32),
        vmem((s.nq, s.half, s.nu), BF16),
        vmem((s.nocc, s.nu), BF16),
        vmem((s.nvec * s.nocc, s.q), F32),
        vmem((tall, s.tile), F32),
        vmem((tall, s.tile), F32),
        vmem((tall, s.tile), BF16),
        vmem((tall, s.tile), BF16),
        vmem((s.nq, s.half, s.nocc), BF16),
        vmem((2, s.parts, nz * rows4, 128), F32),
        vmem((s.quads, 2, nz * rows4, flat), BF16),
        vmem((s.quads, 2 * nz, rows4, flat), BF16),
        vmem((s.quads, rows4, flat), BF16),
        vmem((s.quads, side * side, rows4, flat), BF16),
        vmem((rows4, s.nocc), F32),
        vmem((nz, 1, s.nocc), F32),
        vmem((2 * nz, 1, s.nocc), F32),
        vmem((1, s.nocc), F32),
        vmem((side * side, 1, s.nocc), F32),
        vmem((s.nq, s.window, s.nu), BF16),
        vmem((s.nocc, s.ao), BF16),
        vmem((s.nq, s.nocc, s.nu), F32),
        vmem((s.nq, s.half, s.nu), F32),
        *[vmem((nz, pack, s.nu), F32) for pack in s.packs],
        *[vmem((nz, pack, s.nu), BF16) for pack in s.packs],
        *[vmem((side, nz, pack, s.nu), BF16) for pack in s.packs],
        vmem((side, side * s.lanes, s.nu), BF16),
        *[vmem((nz * pack, side * s.lanes), F32) for pack in s.packs],
        *[vmem((side - 1, nz * pack, s.lanes), BF16) for pack in s.packs],
        *[vmem((2, nz * pack, s.lanes), BF16) for pack in s.packs],
        *[vmem((2, nz * pack // 2, s.lanes), BF16) for pack in s.packs],
        vmem((s.lanes // 128, nz * max(s.packs), 128), F32),
        vmem((s.q, s.tiles * s.tile), F32),
        vmem((s.nocc, 128), F32),
        vmem((8, s.lanes), F32),
        vmem((8, 128), F32),
        vmem((nq8, flat), F32),
        vmem((side, nq8, flat), F32),
        vmem((side, nq8, flat), F32),
        vmem((nq8, flat), BF16),
        vmem((2, nz * nq8, flat), BF16),
        vmem((2, s.parts, nz * nq8, 128), F32),
        vmem((s.nvec, s.nocc, s.q), F32),
        vmem((nz, 8, 128), F32),
        dma(s.nq + 1), one, one, one, one, one,
        one, dma(s.nq), dma(3), dma(3), dma(3), dma(3, 4),
        one, one, one, one, one, one, one, one,
        dma(3), dma(3), dma(3),
        dma(s.quads), dma(s.quads), dma(s.quads), dma(s.quads), one, one, one, one,
    ]
    hbm = pl.BlockSpec(memory_space=pl.ANY)
    fast = pl.BlockSpec(memory_space=pltpu.VMEM)
    scalars = pl.BlockSpec(memory_space=pltpu.SMEM)
    shape = jax.ShapeDtypeStruct
    limit = 56 * 1024 * 1024
    occ_row, trial_rows = occ_energy[None], trial_vectors.T
    terms = pl.pallas_call(
        functools.partial(kernel, s),
        out_shape=shape((1, s.nocc), F32),
        in_specs=[hbm, hbm, hbm, fast, fast, scalars, fast, scalars],
        out_specs=fast,
        scratch_shapes=scratch,
        compiler_params=pltpu.CompilerParams(collective_id=0, has_side_effects=True, vmem_limit_bytes=limit),
    )(integrals, occ_coeffs.T, vir_coeffs.T, trial_rows, occ_row, occ_energy, vir_energy[None], shifts)
    sigma, sub = pl.pallas_call(
        output_kernel,
        out_shape=(shape((1, s.nocc), F32), shape((1, s.nvec), F32)),
        in_specs=[fast] * 3,
        out_specs=(fast, fast),
        scratch_shapes=[vmem((s.nvec, s.nocc), F32)],
    )(terms, trial_rows, occ_row)
    return sigma.T, sub.T


def solution(mesh):
    return jax.shard_map(
        functools.partial(local, dict(mesh.shape)),
        mesh=mesh,
        in_specs=(P("aux", "occ", "vir"), P(), P("vir", None), P(), P("vir"), P(), P("aux")),
        out_specs=(P(None, "aux"), P(None, "aux")),
        check_vma=False,
    )
```

```python
import functools
import math

import jax
import jax.numpy as jnp
from jax import lax
from jax.experimental import pallas as pl
from jax.experimental.pallas import tpu as pltpu
from jax.sharding import PartitionSpec as P

MESH = pl.DeviceIdType.MESH
F32 = jnp.float32
BF16 = jnp.bfloat16


def dot(a, b):
    return jnp.dot(a, b, preferred_element_type=F32)


def dot_nt(a, b):
    return lax.dot_general(a, b, (((1,), (1,)), ((), ())), preferred_element_type=F32)


def split(value):
    high = value.astype(BF16)
    low = (value - high.astype(F32)).astype(BF16)
    return jnp.concatenate([high.astype(F32), low.astype(F32)], axis=0).astype(BF16)


def remote(src, dst, send_sem, recv_sem, **device):
    return pltpu.make_async_remote_copy(
        src_ref=src, dst_ref=dst, send_sem=send_sem, recv_sem=recv_sem, device_id=device, device_id_type=MESH
    )


class Sizes:
    def __init__(self, mesh, integrals, occ_coeffs, vir_energy):
        self.nz = mesh["aux"]
        self.side = math.isqrt(mesh["vir"])
        self.nq, self.mu, self.nu = integrals.shape
        self.ao, self.nocc = occ_coeffs.shape
        self.half = self.nocc // 2
        self.jb = self.half // self.nz
        self.na = vir_energy.shape[0]
        self.block = 16 * (self.na // 16)
        self.rows = self.block + 16
        assert self.na == self.block + 1 and self.side == 4
        third = self.jb // 12 * 4
        self.groups = [(0, third), (third, third), (2 * third, self.jb - 2 * third)]
        self.packs = [-(-(self.nq * count) // 16) * 16 for _, count in self.groups]
        self.tile = 512
        self.tiles = -(-(self.jb * self.na) // self.tile)
        ends = [(j0 + count) * self.na // self.tile for j0, count in self.groups[:-1]] + [self.tiles]
        self.spans = [(start, end - start) for start, end in zip([0] + ends, ends)]
        self.quads = self.nz // 4
        self.lane0 = self.mu // 128 * 128
        self.shift = self.mu - self.lane0
        self.window = self.mu + self.shift
        self.lanes = -(-self.rows // 128) * 128
        self.q = self.nq * self.nz
        self.nvec = self.nz
        self.parts = -(-self.half // 128)
        last = 128 * (self.nu * (mesh["vir"] - 1) // 128) - 128
        self.view = self.ao - last
        for v in range(mesh["vir"]):
            start = 128 * (self.nu * v // 128) - 128 * ((v + 1) // mesh["vir"])
            assert start + self.view <= self.ao and self.nu * v - start + self.nu <= self.view


def kernel(
    s, int_h, occ_h, vir_h, trial, eo_row, eo_s, ve, shift_s,
    out,
    bj, bjt, base, rm, row, hq, sec, fa, coupled0, coupled1, weighted0, weighted1,
    hp, fl, fb, fr, fp, fq, spart, sgs, sgr, spp, spr,
    ibuf, occ_v, pf, xf, pk0, pk1, pk2, hs0, hs1, hs2, hg0, hg1, hg2, vb, vbt, vst,
    acc0, acc1, acc2, bs0, bs1, bs2, bx0, bx1, bx2, bm0, bm1, bm2, bf, bflat, eob, ve8, shift,
    rp, rg, rx, rmsg, rall, rl, rm32, sh,
    in_sem, v_own, v_s, v_r, st_r, sh_s, sh_r, x_s, x_r, h_s, h_r, g_s, g_r, rg_s, rg_r, rx_s, rx_r, rz_s, rz_r, rc_s, rc_r,
    b_s, b_r, m_r, fz_s, fz_r, fp_s, fp_r, s1_s, s1_r, s2_s, s2_r,
):
    nz, side = s.nz, s.side
    z, c, v = lax.axis_index("aux"), lax.axis_index("occ"), lax.axis_index("vir")
    y, x = v // side, v % side
    g = y + c * (x - y)
    r = x + c * (y - x)
    sg = side - (side - 1) * c
    sr = 1 + (side - 1) * c

    def vid(gather, reduce):
        return gather * sg + reduce * sr

    pk, hs, hg, acc = (pk0, pk1, pk2), (hs0, hs1, hs2), (hg0, hg1, hg2), (acc0, acc1, acc2)
    bs, bx, bm = (bs0, bs1, bs2), (bx0, bx1, bx2), (bm0, bm1, bm2)
    me = 2 * z + c
    around = side * side

    def fan(first, last, copy):
        @pl.loop(first, last)
        def _(d):
            copy(d).start()

    def go(*args, **device):
        remote(*args, **device).start()

    def arrived(ref, sem):
        remote(ref, ref, sem, sem, occ=c).wait_recv()

    def sent(ref, sem):
        remote(ref, ref, sem, sem, occ=c).wait_send()

    occ_in = pltpu.make_async_copy(occ_h, occ_v, in_sem.at[s.nq])
    occ_in.start()
    zero_rows = jnp.zeros((s.shift, s.nu), BF16)

    def load(q):
        return pltpu.make_async_copy(
            int_h.at[q], ibuf.at[q, pl.ds(pl.multiple_of(s.shift * c, 16), s.mu), :], in_sem.at[q]
        )

    for q in range(s.nq):
        if s.shift:
            ibuf[q, 0 : s.shift, :] = zero_rows
            ibuf[q, s.mu : s.mu + s.shift, :] = zero_rows
    fan(0, s.nq, load)

    def window(gather, w):
        return vir_h.at[pl.ds(pl.multiple_of(s.block * vid(gather, w), 16), s.rows), :]

    def place(slot, w):
        return vb.at[slot, pl.ds(pl.multiple_of(w * s.lanes, 16), s.rows), :]

    fan(0, side, lambda w: pltpu.make_async_copy(window(g, w), place(0, w), v_own))
    for group in range(3):
        pk[group][...] = jnp.zeros(pk[group].shape, F32)
    rp[...] = jnp.zeros(rp.shape, F32)
    for d in range(side):
        for w in range(side):
            vb[d, w * s.lanes + s.rows : (w + 1) * s.lanes, :] = jnp.zeros((s.lanes - s.rows, s.nu), BF16)

    barrier = pltpu.get_barrier_semaphore()

    @pl.loop(1, 2 * nz)
    def _(d):
        other = (me + d) % (2 * nz)
        pl.semaphore_signal(barrier, inc=1, device_id={"aux": other // 2, "occ": other % 2}, device_id_type=MESH)

    @pl.loop(1, around)
    def _(d):
        pl.semaphore_signal(barrier, inc=1, device_id={"vir": (v + d) % around}, device_id_type=MESH)

    pl.semaphore_wait(barrier, 2 * nz + around - 2)

    ahead, behind = vid((g + 1) % side, r), vid((g + 3) % side, r)
    opposite = (g + 2) % side

    @pl.loop(0, 2)
    def _(w):
        go(window(opposite, w), vst.at[0, w], v_s, st_r.at[0], vir=ahead)
        go(window(opposite, w + 2), vst.at[1, w], v_s, st_r.at[1], vir=behind)

    @pl.loop(0, side)
    def _(w):
        go(window((g + 1) % side, w), place(3, w), v_s, v_r.at[0], vir=ahead)
        go(window((g + 3) % side, w), place(1, w), v_s, v_r.at[0], vir=behind)

    shift[...] = jnp.full((8, 128), shift_s[0], F32)
    fan(1, nz, lambda d: remote(shift, sh.at[z], sh_s, sh_r, aux=(z + d) % nz))
    sh[z] = shift[...]

    occ_in.wait()

    @pl.loop(0, s.nq)
    def _(q):
        load(q).wait()
        columns = occ_v[:, pl.ds(pl.multiple_of(s.lane0 * c, 128), s.window)]
        pf[q] = dot(columns, ibuf[q])
        theirs = pf.at[q, pl.ds(pl.multiple_of(s.half * (1 - c), 8), s.half), :]
        go(theirs, xf.at[q], x_s, x_r.at[q], occ=1 - c)

    arrived(vst.at[0], st_r.at[0])
    arrived(vst.at[1], st_r.at[1])

    @pl.loop(0, 2)
    def _(w):
        go(vst.at[0, w], place(2, w), v_s, v_r.at[1], vir=ahead)
        go(vst.at[1, w], place(2, w + 2), v_s, v_r.at[1], vir=behind)

    for q in range(s.nq):
        arrived(xf.at[q], x_r.at[q])
        xf[q] = xf[q] + pf[q, pl.ds(pl.multiple_of(s.half * c, 8), s.half), :]
        for group, (j0, count) in enumerate(s.groups):
            for to in range(nz):
                pk[group][to, q * count : (q + 1) * count, :] = xf[q, to * s.jb + j0 : to * s.jb + j0 + count, :]

    def scatter(group):
        hs[group][...] = pk[group][...].astype(BF16)

        def copy(d):
            to = (z + d) % nz
            return remote(hs[group].at[to], hg[group].at[0, z], h_s.at[group], h_r.at[group], aux=to)

        fan(1, nz, copy)
        hg[group][0, z] = hs[group][z]

    scatter(0)
    scatter(1)
    for q in range(s.nq):
        hq[q] = xf[q].astype(BF16)
    start = 128 * ((s.nu * v) // 128) - 128 * ((v + 1) // (side * side))
    view = occ_v[:, pl.ds(pl.multiple_of(start, 128), s.view)].astype(F32)
    wide = -(-s.view // 128) * 128
    view = jnp.concatenate([view, jnp.zeros((s.nocc, wide - s.view), F32)], axis=1)
    sec[...] = pltpu.roll(view, wide - (s.nu * v - start), 1)[:, : s.nu].astype(BF16)
    weights = split(dot(trial[...], sec[...]))

    for q in range(s.nq):
        both = dot_nt(weights, hq[q])
        rp[q * s.nvec : (q + 1) * s.nvec, 0 : s.half] = both[: s.nvec] + both[s.nvec :]
    def to_gather(d):
        return remote(rp, rg.at[side - d], rg_s, rg_r, vir=vid((g + d) % side, r))

    def to_reduce(d):
        return remote(rx.at[0], rx.at[side - d], rx_s, rx_r, vir=vid(g, (r + d) % side))

    fan(1, side, to_gather)
    for q in range(s.nq):
        hp[q] = dot_nt(hq[q], sec[...]).astype(BF16)

    ve8[...] = jnp.ones(ve8.shape, F32)
    ve8[:, 0 : s.na] = jnp.broadcast_to(ve[...], (8, s.na))
    bflat[...] = jnp.ones(bflat.shape, F32)
    first = s.half * c + s.jb * z
    for j in range(s.jb):
        bflat[0:8, j * s.na : (j + 1) * s.na] = ve8[:, 0 : s.na] - eo_s[first + j]
    for tile in range(s.tiles):
        base[tile] = bflat[0:8, tile * s.tile : (tile + 1) * s.tile]
    square = jnp.broadcast_to(eo_row[...], (128, s.nocc))
    fill = -(-s.nocc // 128) * 128 - s.nocc
    eob[...] = jnp.concatenate([square, jnp.zeros((128, fill), F32)], axis=1).T[: s.nocc]

    halves = (pl.ds(0, nz // 2), pl.ds(nz // 2, nz // 2))

    def gather(group):
        arrived(hg[group].at[0, pl.ds(0, nz - 1)], h_r.at[group])
        for to, slot, part, sem in ((behind, 1, 0, 0), (ahead, 3, 1, 1), (behind, 1, 1, 2), (ahead, 3, 0, 2)):
            block = hg[group].at[0, halves[part]]
            go(block, hg[group].at[slot, halves[part]], g_s.at[group], g_r.at[group, sem], vir=to)

    def relay(group):
        for slot, to, part in ((1, behind, 0), (3, ahead, 1)):
            block = hg[group].at[slot, halves[part]]
            arrived(block, g_r.at[group, part])
            go(block, hg[group].at[2, halves[part]], g_s.at[group], g_r.at[group, 3], vir=to)

    def near_in(group):
        arrived(hg[group].at[1], g_r.at[group, 2])

    def far_in(group):
        arrived(hg[group].at[2], g_r.at[group, 3])

    def term(group, d):
        return dot(hg[group][d].reshape(nz * s.packs[group], s.nu), vbt[d])

    def product(group, slots):
        value = term(group, slots[0])
        for d in slots[1:]:
            value = value + term(group, d)
        acc[group][...] = value if slots[0] == 0 else value + acc[group][...]

    def columns_of(w):
        return pl.ds(pl.multiple_of(w * s.lanes, 128), s.lanes)

    right, left = vid(g, (r + 1) % side), vid(g, (r + 3) % side)

    def parts_of(group):
        size = nz * s.packs[group] // 2
        return pl.ds(0, size), pl.ds(size, size)

    def reduce_start(group):
        low, high = parts_of(group)
        for e in (2, 1, 3):
            bs[group][e - 1] = acc[group][:, columns_of((r + e) % side)].astype(BF16)
            if e == 2:
                go(bs[group].at[1, low], bm[group].at[0], b_s.at[group], m_r.at[group], vir=right)
                go(bs[group].at[1, high], bm[group].at[1], b_s.at[group], m_r.at[group], vir=left)
            if e == 1:
                go(bs[group].at[0, high], bx[group].at[0, high], b_s.at[group], b_r.at[group], vir=right)
            if e == 3:
                go(bs[group].at[2, low], bx[group].at[1, low], b_s.at[group], b_r.at[group], vir=left)

    def reduce_merge(group):
        low, high = parts_of(group)
        arrived(bm[group], m_r.at[group])
        merged = acc[group][low, columns_of((r + 1) % side)] + bm[group][0].astype(F32)
        bs[group][0, low, :] = merged.astype(BF16)
        go(bs[group].at[0, low], bx[group].at[0, low], b_s.at[group], b_r.at[group], vir=right)
        merged = acc[group][high, columns_of((r + 3) % side)] + bm[group][1].astype(F32)
        bs[group][2, high, :] = merged.astype(BF16)
        go(bs[group].at[2, high], bx[group].at[1, high], b_s.at[group], b_r.at[group], vir=left)

    nq8 = s.nq * s.nvec
    iota = functools.partial(lax.broadcasted_iota, jnp.int32, (s.nu, s.nu))
    identity = jnp.where(iota(0) == iota(1), 1.0, 0.0).astype(BF16)

    def turn(d):
        vbt[d] = dot_nt(identity, vb[d]).astype(BF16)

    pltpu.make_async_copy(vir_h.at[pl.ds(0, side * s.rows), :], vb.at[0, pl.ds(0, side * s.rows), :], v_own).wait()
    turn(0)
    arrived(rg.at[pl.ds(1, side - 1)], rg_r)
    total = rp[...]
    for d in range(1, side):
        total = total + rg[d]
    rx[0] = total
    fan(1, side, to_reduce)
    gather(0)
    arrived(rx.at[pl.ds(1, side - 1)], rx_r)
    total = rx[0]
    for d in range(1, side):
        total = total + rx[d]
    rmsg[...] = total.astype(BF16)
    own_rows = pl.ds(pl.multiple_of(z * nq8, 16), nq8)
    fan(1, nz, lambda d: remote(rmsg, rall.at[c, own_rows, :], rz_s, rz_r, aux=(z + d) % nz))
    rall[c, own_rows, :] = rmsg[...]
    scatter(2)
    product(0, (0,))
    arrived(vb.at[pl.ds(1, 2), pl.ds(0, side * s.rows), :], v_r.at[0])
    relay(0)
    turn(1)
    turn(3)
    near_in(0)
    product(0, (1, 3))
    arrived(vb.at[2, pl.ds(0, side * s.rows), :], v_r.at[1])
    turn(2)
    gather(1)
    far_in(0)
    product(0, (2,))
    reduce_start(0)
    product(1, (0,))
    relay(1)
    reduce_merge(0)
    near_in(1)
    product(1, (1, 3))
    far_in(1)
    product(1, (2,))
    reduce_start(1)
    arrived(rall.at[c, pl.ds(0, (nz - 1) * nq8), :], rz_r)
    arrived(sh.at[pl.ds(0, nz - 1)], sh_r)
    go(rall.at[c], rall.at[c], rc_s, rc_r, occ=1 - c)
    gather(2)
    arrived(rall.at[1 - c], rc_r)
    for h in range(2):
        for part in range(s.parts):
            rl[h, part] = rall[h, :, part * 128 : (part + 1) * 128].astype(F32)
    for n in range(s.nvec):
        for h in range(2):
            sides = []
            for part in range(s.parts):
                rows = [rl[h, part, pl.ds(q * s.nvec + n, nz, stride=nq8), :] for q in range(s.nq)]
                sides.append(jnp.concatenate(rows, axis=0))
            rm32[n, h * s.half : (h + 1) * s.half, :] = jnp.concatenate(sides, axis=1).T[: s.half]
        rm[n * s.nocc : (n + 1) * s.nocc, :] = rm32[n].astype(BF16)
        row[n * s.nocc : (n + 1) * s.nocc, :] = jnp.broadcast_to(sh[n][0:1, :], (s.nocc, 128)) - eob[...]
    reduce_merge(1)
    product(2, (0,))
    relay(2)

    def build(group):
        j0, count = s.groups[group]
        pack = s.packs[group]
        arrived(bx[group], b_r.at[group])

        @pl.loop(0, nz)
        def _(source):
            rows = pl.ds(pl.multiple_of(source * pack, 16), pack)
            value = acc[group][rows, columns_of(r)] + bx[group][0, rows, :].astype(F32) + bx[group][1, rows, :].astype(F32)
            full = pltpu.roll(value.astype(BF16).astype(F32), s.lanes - v, 1)
            for part in range(s.lanes // 128):
                bf[part, rows, :] = full[:, part * 128 : (part + 1) * 128]

        for j in range(count):
            parts = []
            for part in range(s.lanes // 128):
                rows = [bf[part, pl.ds(q * count + j, nz, stride=pack), :] for q in range(s.nq)]
                parts.append(jnp.concatenate(rows, axis=0))
            bflat[:, (j0 + j) * s.na : (j0 + j + 1) * s.na] = jnp.concatenate(parts, axis=1)[:, : s.na]

    def ready(group):
        build(group)
        start, count = s.spans[group]
        for tile in range(start, start + count):
            flat = bflat[:, tile * s.tile : (tile + 1) * s.tile]
            bj[tile] = flat.astype(BF16)
            bjt[tile] = flat.T.astype(BF16)

    tall = 4 * s.nocc
    coupled, weighted = (coupled0, coupled1), (weighted0, weighted1)

    def couple(slot, tile, quad):
        coupled[slot][...] = dot(rm[pl.ds(pl.multiple_of(quad * tall, 16), tall), :], bj[tile])

    def weigh(slot, tile, quad):
        own = row[pl.ds(pl.multiple_of(quad * tall, 8), tall), :]
        divisor = jnp.concatenate([own] * (s.tile // 128), axis=1) + base[tile, 0:1, :]
        weighted[slot][...] = (coupled[slot][...] * pl.reciprocal(divisor, approx=True, full_range=False)).astype(BF16)

    def fold(slot, tile, quad):
        fa[pl.ds(pl.multiple_of(quad * tall, 8), tall), :] += dot(weighted[slot][...], bjt[tile])

    def advance(older, old, new, newer):
        fold(0, *older)
        weigh(1, *old)
        couple(0, *new)
        fold(1, *old)
        weigh(0, *new)
        couple(1, *newer)

    fa[...] = jnp.zeros(fa.shape, F32)
    bflat[:, s.tiles * s.tile - 128 :] = jnp.zeros((s.q, 128), F32)
    ready(0)
    couple(0, 0, 0)
    couple(1, 0, 1)
    weigh(0, 0, 0)
    second, third = s.spans[1][0], s.spans[2][0]

    @pl.loop(1, third)
    def _(tile):
        @pl.when(tile == 2)
        def _():
            near_in(2)
            product(2, (1, 3))
            far_in(2)
            product(2, (2,))
            reduce_start(2)

        @pl.when(tile == second)
        def _():
            reduce_merge(2)
            ready(1)

        advance((tile - 1, 0), (tile - 1, 1), (tile, 0), (tile, 1))

    ready(2)
    advance((third - 1, 0), (third - 1, 1), (third, 0), (third + 1, 0))

    rows4 = 4 * s.nq

    def to_owner(u, d):
        other = (me + d) % (2 * nz)
        return pltpu.make_async_remote_copy(
            src_ref=fb.at[u, other % 2, pl.ds(pl.multiple_of(other // 2 * rows4, 16), rows4), :], dst_ref=fr.at[u, me],
            send_sem=fz_s.at[u], recv_sem=fz_r.at[u],
            device_id={"aux": other // 2, "occ": other % 2}, device_id_type=MESH,
        )

    def to_plane(u, d):
        return pltpu.make_async_remote_copy(
            src_ref=fp.at[u], dst_ref=fq.at[u, v], send_sem=fp_s.at[u], recv_sem=fp_r.at[u],
            device_id={"vir": (v + d) % around}, device_id_type=MESH,
        )

    def finish(u):
        for m in range(4):
            for h in range(2):
                start = u * tall + m * s.nocc + h * s.half
                flip = fa[start : start + s.half, :].T
                flip = jnp.concatenate([flip, jnp.zeros((s.q, s.parts * 128 - s.half), F32)], axis=1)
                for part in range(s.parts):
                    for q in range(s.nq):
                        fl[h, part, pl.ds(m * s.nq + q, nz, stride=rows4), :] = flip[
                            q * nz : (q + 1) * nz, part * 128 : (part + 1) * 128
                        ]
        for h in range(2):
            fb[u, h] = jnp.concatenate([fl[h, part] for part in range(s.parts)], axis=1).astype(BF16)
        fan(1, 2 * nz, functools.partial(to_owner, u))
        fr[u, me] = fb[u, c, pl.ds(pl.multiple_of(z * rows4, 16), rows4), :]

    def pass_on(u):
        arrived(fr.at[u, pl.ds(0, 2 * nz - 1)], fz_r.at[u])
        total = fr[u, 0].astype(F32)
        for other in range(1, 2 * nz):
            total = total + fr[u, other].astype(F32)
        fp[u] = total.astype(BF16)
        fan(1, around, functools.partial(to_plane, u))
        fq[u, v] = fp[u]

    def apply(u):
        arrived(fq.at[u, pl.ds(0, around - 1)], fp_r.at[u])
        total = fq[u, 0].astype(F32)
        for other in range(1, around):
            total = total + fq[u, other].astype(F32)
        folded = split(total[:, : s.half])
        owner = lax.broadcasted_iota(jnp.int32, folded.shape, 0) % s.nq
        both = None
        for q in range(s.nq):
            value = dot(jnp.where(owner == q, folded.astype(F32), 0.0).astype(BF16), hp[q])
            both = value if both is None else both + value
        spart[...] = both[:rows4] + both[rows4:]
        for m in range(4):
            value = spart[m * s.nq : m * s.nq + 1, :]
            for q in range(1, s.nq):
                value = value + spart[m * s.nq + q : m * s.nq + q + 1, :]
            sgs[4 * u + m] = value

    late = s.spans[2][1]

    def pair(step):
        return third + step % late, step // late

    @pl.loop(1, late)
    def _(half):
        step = 2 * half
        advance(pair(step - 2), pair(step - 1), pair(step), pair(step + 1))

        @pl.when(half == late // 2)
        def _():
            finish(0)

        @pl.when(half == late - 1)
        def _():
            pass_on(0)

    last = 2 * late - 1
    fold(0, *pair(last - 1))
    weigh(1, *pair(last))
    fold(1, *pair(last))
    finish(1)
    for group in range(3):
        sent(hs[group].at[pl.ds(0, nz - 1)], h_s.at[group])
        sent(hg[group].at[pl.ds(0, side - 1)], g_s.at[group])
        sent(bs[group], b_s.at[group])
    sent(vb.at[:, pl.ds(0, side * s.rows), :], v_s)
    sent(sh.at[pl.ds(0, nz - 1)], sh_s)
    sent(xf, x_s)
    sent(rg.at[pl.ds(1, side - 1)], rg_s)
    sent(rx.at[pl.ds(1, side - 1)], rx_s)
    sent(rall.at[c, pl.ds(0, (nz - 1) * nq8), :], rz_s)
    sent(rall.at[c], rc_s)
    apply(0)
    pass_on(1)
    for u in range(2):
        sent(fr.at[u, pl.ds(0, 2 * nz - 1)], fz_s.at[u])
    apply(1)

    def to_aux(d):
        other = (me + d) % (2 * nz)
        return remote(sgs.at[other // 2], sgr.at[me], s1_s, s1_r, aux=other // 2, occ=other % 2)

    fan(1, 2 * nz, to_aux)
    sgr[me] = sgs[z]
    arrived(sgr.at[pl.ds(0, 2 * nz - 1)], s1_r)
    total = sgr[0]
    for d in range(1, 2 * nz):
        total = total + sgr[d]
    spp[...] = total
    fan(1, around, lambda d: remote(spp, spr.at[v], s2_s, s2_r, vir=(v + d) % around))
    spr[v] = total
    arrived(spr.at[pl.ds(0, around - 1)], s2_r)
    total = spr[0]
    for d in range(1, side * side):
        total = total + spr[d]
    out[...] = total
    for u in range(2):
        sent(fq.at[u, pl.ds(0, around - 1)], fp_s.at[u])
    sent(sgr.at[pl.ds(0, 2 * nz - 1)], s1_s)
    sent(spr.at[pl.ds(0, around - 1)], s2_s)


def output_kernel(terms, trial, eo_row, sigma_out, sub_out, t32):
    t32[...] = trial[...].astype(F32)
    sigma = eo_row[...] * t32[pl.ds(lax.axis_index("aux"), 1), :] + terms[...]
    sigma_out[...] = sigma
    column = jnp.sum(t32[...] * sigma, axis=1, keepdims=True)
    sub_out[...] = jnp.broadcast_to(column, (column.shape[0], 128)).T[0:1]


def local(mesh, integrals, occ_coeffs, vir_coeffs, occ_energy, vir_energy, trial_vectors, shifts):
    s = Sizes(mesh, integrals, occ_coeffs, vir_energy)
    nz, side = s.nz, s.side
    vmem = pltpu.VMEM
    nq8 = s.nq * s.nvec
    rows4 = 4 * s.nq
    dma = lambda *shape: pltpu.SemaphoreType.DMA(shape)
    one = pltpu.SemaphoreType.DMA
    tall = 4 * s.nocc
    flat = s.parts * 128
    scratch = [
        vmem((s.tiles, s.q, s.tile), BF16),
        vmem((s.tiles, s.tile, s.q), BF16),
        vmem((s.tiles, 8, s.tile), F32),
        vmem((s.nvec * s.nocc, s.q), BF16),
        vmem((s.nvec * s.nocc, 128), F32),
        vmem((s.nq, s.half, s.nu), BF16),
        vmem((s.nocc, s.nu), BF16),
        vmem((s.nvec * s.nocc, s.q), F32),
        vmem((tall, s.tile), F32),
        vmem((tall, s.tile), F32),
        vmem((tall, s.tile), BF16),
        vmem((tall, s.tile), BF16),
        vmem((s.nq, s.half, s.nocc), BF16),
        vmem((2, s.parts, nz * rows4, 128), F32),
        vmem((s.quads, 2, nz * rows4, flat), BF16),
        vmem((s.quads, 2 * nz, rows4, flat), BF16),
        vmem((s.quads, rows4, flat), BF16),
        vmem((s.quads, side * side, rows4, flat), BF16),
        vmem((rows4, s.nocc), F32),
        vmem((nz, 1, s.nocc), F32),
        vmem((2 * nz, 1, s.nocc), F32),
        vmem((1, s.nocc), F32),
        vmem((side * side, 1, s.nocc), F32),
        vmem((s.nq, s.window, s.nu), BF16),
        vmem((s.nocc, s.ao), BF16),
        vmem((s.nq, s.nocc, s.nu), F32),
        vmem((s.nq, s.half, s.nu), F32),
        *[vmem((nz, pack, s.nu), F32) for pack in s.packs],
        *[vmem((nz, pack, s.nu), BF16) for pack in s.packs],
        *[vmem((side, nz, pack, s.nu), BF16) for pack in s.packs],
        vmem((side, side * s.lanes, s.nu), BF16),
        vmem((side, s.nu, side * s.lanes), BF16),
        vmem((2, 2, s.rows, s.nu), BF16),
        *[vmem((nz * pack, side * s.lanes), F32) for pack in s.packs],
        *[vmem((side - 1, nz * pack, s.lanes), BF16) for pack in s.packs],
        *[vmem((2, nz * pack, s.lanes), BF16) for pack in s.packs],
        *[vmem((2, nz * pack // 2, s.lanes), BF16) for pack in s.packs],
        vmem((s.lanes // 128, nz * max(s.packs), 128), F32),
        vmem((s.q, s.tiles * s.tile), F32),
        vmem((s.nocc, 128), F32),
        vmem((8, s.lanes), F32),
        vmem((8, 128), F32),
        vmem((nq8, flat), F32),
        vmem((side, nq8, flat), F32),
        vmem((side, nq8, flat), F32),
        vmem((nq8, flat), BF16),
        vmem((2, nz * nq8, flat), BF16),
        vmem((2, s.parts, nz * nq8, 128), F32),
        vmem((s.nvec, s.nocc, s.q), F32),
        vmem((nz, 8, 128), F32),
        dma(s.nq + 1), one, one, dma(2), dma(2), one, one,
        one, dma(s.nq), dma(3), dma(3), dma(3), dma(3, 4),
        one, one, one, one, one, one, one, one,
        dma(3), dma(3), dma(3),
        dma(s.quads), dma(s.quads), dma(s.quads), dma(s.quads), one, one, one, one,
    ]
    hbm = pl.BlockSpec(memory_space=pl.ANY)
    fast = pl.BlockSpec(memory_space=pltpu.VMEM)
    scalars = pl.BlockSpec(memory_space=pltpu.SMEM)
    shape = jax.ShapeDtypeStruct
    limit = 56 * 1024 * 1024
    occ_row, trial_rows = occ_energy[None], trial_vectors.T
    terms = pl.pallas_call(
        functools.partial(kernel, s),
        out_shape=shape((1, s.nocc), F32),
        in_specs=[hbm, hbm, hbm, fast, fast, scalars, fast, scalars],
        out_specs=fast,
        scratch_shapes=scratch,
        compiler_params=pltpu.CompilerParams(collective_id=0, has_side_effects=True, vmem_limit_bytes=limit),
    )(integrals, occ_coeffs.T, vir_coeffs.T, trial_rows, occ_row, occ_energy, vir_energy[None], shifts)
    sigma, sub = pl.pallas_call(
        output_kernel,
        out_shape=(shape((1, s.nocc), F32), shape((1, s.nvec), F32)),
        in_specs=[fast] * 3,
        out_specs=(fast, fast),
        scratch_shapes=[vmem((s.nvec, s.nocc), F32)],
    )(terms, trial_rows, occ_row)
    return sigma.T, sub.T


def solution(mesh):
    return jax.shard_map(
        functools.partial(local, dict(mesh.shape)),
        mesh=mesh,
        in_specs=(P("aux", "occ", "vir"), P(), P("vir", None), P(), P("vir"), P(), P("aux")),
        out_specs=(P(None, "aux"), P(None, "aux")),
        check_vma=False,
    )
```

```python
import functools
import math

import jax
import jax.numpy as jnp
from jax import lax
from jax.experimental import pallas as pl
from jax.experimental.pallas import tpu as pltpu
from jax.sharding import PartitionSpec as P

MESH = pl.DeviceIdType.MESH
F32 = jnp.float32
BF16 = jnp.bfloat16


def dot(a, b):
    return jnp.dot(a, b, preferred_element_type=F32)


def dot_nt(a, b):
    return lax.dot_general(a, b, (((1,), (1,)), ((), ())), preferred_element_type=F32)


def split(value):
    high = value.astype(BF16)
    low = (value - high.astype(F32)).astype(BF16)
    return jnp.concatenate([high.astype(F32), low.astype(F32)], axis=0).astype(BF16)


def remote(src, dst, send_sem, recv_sem, **device):
    return pltpu.make_async_remote_copy(
        src_ref=src, dst_ref=dst, send_sem=send_sem, recv_sem=recv_sem, device_id=device, device_id_type=MESH
    )


class Sizes:
    def __init__(self, mesh, integrals, occ_coeffs, vir_energy):
        self.nz = mesh["aux"]
        self.side = math.isqrt(mesh["vir"])
        self.nq, self.mu, self.nu = integrals.shape
        self.ao, self.nocc = occ_coeffs.shape
        self.half = self.nocc // 2
        self.jb = self.half // self.nz
        self.na = vir_energy.shape[0]
        self.block = 16 * (self.na // 16)
        self.rows = self.block + 16
        assert self.na == self.block + 1 and self.side == 4
        third = self.jb // 12 * 4
        self.groups = [(0, third), (third, third), (2 * third, self.jb - 2 * third)]
        self.packs = [-(-(self.nq * count) // 16) * 16 for _, count in self.groups]
        self.tile = 512
        self.tiles = -(-(self.jb * self.na) // self.tile)
        ends = [(j0 + count) * self.na // self.tile for j0, count in self.groups[:-1]] + [self.tiles]
        self.spans = [(start, end - start) for start, end in zip([0] + ends, ends)]
        self.quads = self.nz // 4
        self.lane0 = self.mu // 128 * 128
        self.shift = self.mu - self.lane0
        self.window = self.mu + self.shift
        self.lanes = -(-self.rows // 128) * 128
        self.q = self.nq * self.nz
        self.nvec = self.nz
        self.parts = -(-self.half // 128)
        last = 128 * (self.nu * (mesh["vir"] - 1) // 128) - 128
        self.view = self.ao - last
        for v in range(mesh["vir"]):
            start = 128 * (self.nu * v // 128) - 128 * ((v + 1) // mesh["vir"])
            assert start + self.view <= self.ao and self.nu * v - start + self.nu <= self.view


def kernel(
    s, int_h, occ_h, vir_h, trial, eo_row, eo_s, ve, shift_s,
    out,
    bj, bjt, base, rm, row, hq, sec, fa, coupled0, coupled1, weighted0, weighted1,
    hp, fl, fb, fr, fp, fq, spart, sgs, sgr, spp, spr,
    ibuf, occ_v, pf, xf, pk0, pk1, pk2, hs0, hs1, hs2, hg0, hg1, hg2, vb, vbt, vst,
    acc0, acc1, acc2, bs0, bs1, bs2, bx0, bx1, bx2, bf, bflat, eob, ve8, shift,
    rp, rg, rmsg, rall, rl, rm32, sh,
    in_sem, v_own, v_s, v_r, st_r, sh_s, sh_r, x_s, x_r, h_s, h_r, g_s, g_r, rg_s, rg_r, rz_s, rz_r, rc_s, rc_r,
    b_s, b_r, fz_s, fz_r, fp_s, fp_r, s1_s, s1_r, s2_s, s2_r,
):
    nz, side = s.nz, s.side
    z, c, v = lax.axis_index("aux"), lax.axis_index("occ"), lax.axis_index("vir")
    y, x = v // side, v % side
    g = y + c * (x - y)
    r = x + c * (y - x)
    sg = side - (side - 1) * c
    sr = 1 + (side - 1) * c

    def vid(gather, reduce):
        return gather * sg + reduce * sr

    pk, hs, hg, acc = (pk0, pk1, pk2), (hs0, hs1, hs2), (hg0, hg1, hg2), (acc0, acc1, acc2)
    bs, bx = (bs0, bs1, bs2), (bx0, bx1, bx2)
    me = 2 * z + c
    around = side * side

    def fan(first, last, copy):
        @pl.loop(first, last)
        def _(d):
            copy(d).start()

    def go(*args, **device):
        remote(*args, **device).start()

    def arrived(ref, sem):
        remote(ref, ref, sem, sem, occ=c).wait_recv()

    def sent(ref, sem):
        remote(ref, ref, sem, sem, occ=c).wait_send()

    occ_in = pltpu.make_async_copy(occ_h, occ_v, in_sem.at[s.nq])
    occ_in.start()
    zero_rows = jnp.zeros((s.shift, s.nu), BF16)

    def load(q):
        return pltpu.make_async_copy(
            int_h.at[q], ibuf.at[q, pl.ds(pl.multiple_of(s.shift * c, 16), s.mu), :], in_sem.at[q]
        )

    for q in range(s.nq):
        if s.shift:
            ibuf[q, 0 : s.shift, :] = zero_rows
            ibuf[q, s.mu : s.mu + s.shift, :] = zero_rows
    fan(0, s.nq, load)

    def window(gather, w):
        return vir_h.at[pl.ds(pl.multiple_of(s.block * vid(gather, w), 16), s.rows), :]

    def place(slot, w):
        return vb.at[slot, pl.ds(pl.multiple_of(w * s.lanes, 16), s.rows), :]

    fan(0, side, lambda w: pltpu.make_async_copy(window(g, w), place(0, w), v_own))
    for group in range(3):
        pk[group][...] = jnp.zeros(pk[group].shape, F32)
    rp[...] = jnp.zeros(rp.shape, F32)
    for d in range(side):
        for w in range(side):
            vb[d, w * s.lanes + s.rows : (w + 1) * s.lanes, :] = jnp.zeros((s.lanes - s.rows, s.nu), BF16)

    barrier = pltpu.get_barrier_semaphore()

    @pl.loop(1, 2 * nz)
    def _(d):
        other = (me + d) % (2 * nz)
        pl.semaphore_signal(barrier, inc=1, device_id={"aux": other // 2, "occ": other % 2}, device_id_type=MESH)

    @pl.loop(1, around)
    def _(d):
        pl.semaphore_signal(barrier, inc=1, device_id={"vir": (v + d) % around}, device_id_type=MESH)

    pl.semaphore_wait(barrier, 2 * nz + around - 2)

    ahead, behind = vid((g + 1) % side, r), vid((g + 3) % side, r)
    opposite = (g + 2) % side

    @pl.loop(0, 2)
    def _(w):
        go(window(opposite, w), vst.at[0, w], v_s, st_r.at[0], vir=ahead)
        go(window(opposite, w + 2), vst.at[1, w], v_s, st_r.at[1], vir=behind)

    @pl.loop(0, side)
    def _(w):
        go(window((g + 1) % side, w), place(3, w), v_s, v_r.at[0], vir=ahead)
        go(window((g + 3) % side, w), place(1, w), v_s, v_r.at[0], vir=behind)

    shift[...] = jnp.full((8, 128), shift_s[0], F32)
    fan(1, nz, lambda d: remote(shift, sh.at[z], sh_s, sh_r, aux=(z + d) % nz))
    sh[z] = shift[...]

    occ_in.wait()

    @pl.loop(0, s.nq)
    def _(q):
        load(q).wait()
        columns = occ_v[:, pl.ds(pl.multiple_of(s.lane0 * c, 128), s.window)]
        pf[q] = dot(columns, ibuf[q])
        theirs = pf.at[q, pl.ds(pl.multiple_of(s.half * (1 - c), 8), s.half), :]
        go(theirs, xf.at[q], x_s, x_r.at[q], occ=1 - c)

    start = 128 * ((s.nu * v) // 128) - 128 * ((v + 1) // (side * side))
    view = occ_v[:, pl.ds(pl.multiple_of(start, 128), s.view)].astype(F32)
    wide = -(-s.view // 128) * 128
    view = jnp.concatenate([view, jnp.zeros((s.nocc, wide - s.view), F32)], axis=1)
    sec[...] = pltpu.roll(view, wide - (s.nu * v - start), 1)[:, : s.nu].astype(BF16)
    weights = split(dot(trial[...], sec[...]))
    arrived(vst.at[0], st_r.at[0])
    arrived(vst.at[1], st_r.at[1])

    @pl.loop(0, 2)
    def _(w):
        go(vst.at[0, w], place(2, w), v_s, v_r.at[1], vir=ahead)
        go(vst.at[1, w], place(2, w + 2), v_s, v_r.at[1], vir=behind)

    for q in range(s.nq):
        arrived(xf.at[q], x_r.at[q])
        xf[q] = xf[q] + pf[q, pl.ds(pl.multiple_of(s.half * c, 8), s.half), :]
        for group, (j0, count) in enumerate(s.groups):
            for to in range(nz):
                pk[group][to, q * count : (q + 1) * count, :] = xf[q, to * s.jb + j0 : to * s.jb + j0 + count, :]

    def scatter(group):
        hs[group][...] = pk[group][...].astype(BF16)

        def copy(d):
            to = (z + d) % nz
            return remote(hs[group].at[to], hg[group].at[0, z], h_s.at[group], h_r.at[group], aux=to)

        fan(1, nz, copy)
        hg[group][0, z] = hs[group][z]

    scatter(0)
    for q in range(s.nq):
        hq[q] = xf[q].astype(BF16)
    for q in range(s.nq):
        both = dot_nt(weights, hq[q])
        rp[q * s.nvec : (q + 1) * s.nvec, 0 : s.half] = both[: s.nvec] + both[s.nvec :]
    rg[v] = rp[...].astype(BF16)
    fan(1, around, lambda d: remote(rg.at[v], rg.at[v], rg_s, rg_r, vir=(v + d) % around))
    scatter(1)
    for q in range(s.nq):
        hp[q] = dot_nt(hq[q], sec[...]).astype(BF16)

    ve8[...] = jnp.ones(ve8.shape, F32)
    ve8[:, 0 : s.na] = jnp.broadcast_to(ve[...], (8, s.na))
    bflat[...] = jnp.ones(bflat.shape, F32)
    first = s.half * c + s.jb * z
    for j in range(s.jb):
        bflat[0:8, j * s.na : (j + 1) * s.na] = ve8[:, 0 : s.na] - eo_s[first + j]
    for tile in range(s.tiles):
        base[tile] = bflat[0:8, tile * s.tile : (tile + 1) * s.tile]
    square = jnp.broadcast_to(eo_row[...], (128, s.nocc))
    fill = -(-s.nocc // 128) * 128 - s.nocc
    eob[...] = jnp.concatenate([square, jnp.zeros((128, fill), F32)], axis=1).T[: s.nocc]

    across = vid((g + 2) % side, r)

    def gather(group):
        arrived(hg[group].at[0, pl.ds(0, nz - 1)], h_r.at[group])
        for slot, to, sem in ((1, behind, 0), (3, ahead, 0), (2, across, 1)):
            go(hg[group].at[0], hg[group].at[slot], g_s.at[group], g_r.at[group, sem], vir=to)

    def near_in(group):
        arrived(hg[group].at[pl.ds(0, 2)], g_r.at[group, 0])

    def far_in(group):
        arrived(hg[group].at[2], g_r.at[group, 1])

    def term(group, d):
        return dot(hg[group][d].reshape(nz * s.packs[group], s.nu), vbt[d])

    def product(group, slots):
        value = term(group, slots[0])
        for d in slots[1:]:
            value = value + term(group, d)
        acc[group][...] = value if slots[0] == 0 else value + acc[group][...]

    def columns_of(w):
        return pl.ds(pl.multiple_of(w * s.lanes, 128), s.lanes)

    def reduce_start(group):
        for e in (2, 1, 3):
            w = (r + e) % side
            bs[group][e - 1] = acc[group][:, columns_of(w)].astype(BF16)
            go(bs[group].at[e - 1], bx[group].at[e - 1], b_s.at[group], b_r.at[group], vir=vid(g, w))

    nq8 = s.nq * s.nvec
    iota = functools.partial(lax.broadcasted_iota, jnp.int32, (s.nu, s.nu))
    identity = jnp.where(iota(0) == iota(1), 1.0, 0.0).astype(BF16)

    def turn(d):
        vbt[d] = dot_nt(identity, vb[d]).astype(BF16)

    pltpu.make_async_copy(vir_h.at[pl.ds(0, side * s.rows), :], vb.at[0, pl.ds(0, side * s.rows), :], v_own).wait()
    turn(0)
    gather(0)
    arrived(rg.at[pl.ds(0, around - 1)], rg_r)
    total = rg[0].astype(F32)
    for other in range(1, around):
        total = total + rg[other].astype(F32)
    rmsg[...] = total.astype(BF16)
    own_rows = pl.ds(pl.multiple_of(z * nq8, 16), nq8)
    fan(1, nz, lambda d: remote(rmsg, rall.at[c, own_rows, :], rz_s, rz_r, aux=(z + d) % nz))
    rall[c, own_rows, :] = rmsg[...]
    scatter(2)
    product(0, (0,))
    arrived(vb.at[pl.ds(1, 2), pl.ds(0, side * s.rows), :], v_r.at[0])
    turn(1)
    turn(3)
    gather(1)
    near_in(0)
    product(0, (1, 3))
    arrived(vb.at[2, pl.ds(0, side * s.rows), :], v_r.at[1])
    turn(2)
    far_in(0)
    product(0, (2,))
    reduce_start(0)
    product(1, (0,))
    arrived(rall.at[c, pl.ds(0, (nz - 1) * nq8), :], rz_r)
    arrived(sh.at[pl.ds(0, nz - 1)], sh_r)
    go(rall.at[c], rall.at[c], rc_s, rc_r, occ=1 - c)
    near_in(1)
    product(1, (1, 3))
    far_in(1)
    product(1, (2,))
    reduce_start(1)
    gather(2)
    arrived(rall.at[1 - c], rc_r)
    for h in range(2):
        for part in range(s.parts):
            rl[h, part] = rall[h, :, part * 128 : (part + 1) * 128].astype(F32)
    for n in range(s.nvec):
        for h in range(2):
            sides = []
            for part in range(s.parts):
                rows = [rl[h, part, pl.ds(q * s.nvec + n, nz, stride=nq8), :] for q in range(s.nq)]
                sides.append(jnp.concatenate(rows, axis=0))
            rm32[n, h * s.half : (h + 1) * s.half, :] = jnp.concatenate(sides, axis=1).T[: s.half]
        rm[n * s.nocc : (n + 1) * s.nocc, :] = rm32[n].astype(BF16)
        row[n * s.nocc : (n + 1) * s.nocc, :] = jnp.broadcast_to(sh[n][0:1, :], (s.nocc, 128)) - eob[...]
    product(2, (0,))

    def build(group):
        j0, count = s.groups[group]
        pack = s.packs[group]
        arrived(bx[group], b_r.at[group])

        @pl.loop(0, nz)
        def _(source):
            rows = pl.ds(pl.multiple_of(source * pack, 16), pack)
            value = acc[group][rows, columns_of(r)]
            for e in range(side - 1):
                value = value + bx[group][e, rows, :].astype(F32)
            full = pltpu.roll(value.astype(BF16).astype(F32), s.lanes - v, 1)
            for part in range(s.lanes // 128):
                bf[part, rows, :] = full[:, part * 128 : (part + 1) * 128]

        for j in range(count):
            parts = []
            for part in range(s.lanes // 128):
                rows = [bf[part, pl.ds(q * count + j, nz, stride=pack), :] for q in range(s.nq)]
                parts.append(jnp.concatenate(rows, axis=0))
            bflat[:, (j0 + j) * s.na : (j0 + j + 1) * s.na] = jnp.concatenate(parts, axis=1)[:, : s.na]

    def ready(group):
        build(group)
        start, count = s.spans[group]
        for tile in range(start, start + count):
            flat = bflat[:, tile * s.tile : (tile + 1) * s.tile]
            bj[tile] = flat.astype(BF16)
            bjt[tile] = flat.T.astype(BF16)

    tall = 4 * s.nocc
    coupled, weighted = (coupled0, coupled1), (weighted0, weighted1)

    def couple(slot, tile, quad):
        coupled[slot][...] = dot(rm[pl.ds(pl.multiple_of(quad * tall, 16), tall), :], bj[tile])

    def weigh(slot, tile, quad):
        own = row[pl.ds(pl.multiple_of(quad * tall, 8), tall), :]
        divisor = jnp.concatenate([own] * (s.tile // 128), axis=1) + base[tile, 0:1, :]
        weighted[slot][...] = (coupled[slot][...] * pl.reciprocal(divisor, approx=True, full_range=False)).astype(BF16)

    def fold(slot, tile, quad):
        fa[pl.ds(pl.multiple_of(quad * tall, 8), tall), :] += dot(weighted[slot][...], bjt[tile])

    def advance(older, old, new, newer):
        fold(0, *older)
        weigh(1, *old)
        couple(0, *new)
        fold(1, *old)
        weigh(0, *new)
        couple(1, *newer)

    fa[...] = jnp.zeros(fa.shape, F32)
    bflat[:, s.tiles * s.tile - 128 :] = jnp.zeros((s.q, 128), F32)
    ready(0)
    couple(0, 0, 0)
    couple(1, 0, 1)
    weigh(0, 0, 0)
    second, third = s.spans[1][0], s.spans[2][0]

    @pl.loop(1, third)
    def _(tile):
        @pl.when(tile == 2)
        def _():
            near_in(2)
            product(2, (1, 3))
            far_in(2)
            product(2, (2,))
            reduce_start(2)

        @pl.when(tile == second)
        def _():
            ready(1)

        advance((tile - 1, 0), (tile - 1, 1), (tile, 0), (tile, 1))

    ready(2)
    advance((third - 1, 0), (third - 1, 1), (third, 0), (third + 1, 0))

    rows4 = 4 * s.nq

    def to_owner(u, d):
        other = (me + d) % (2 * nz)
        return pltpu.make_async_remote_copy(
            src_ref=fb.at[u, other % 2, pl.ds(pl.multiple_of(other // 2 * rows4, 16), rows4), :], dst_ref=fr.at[u, me],
            send_sem=fz_s.at[u], recv_sem=fz_r.at[u],
            device_id={"aux": other // 2, "occ": other % 2}, device_id_type=MESH,
        )

    def to_plane(u, d):
        return pltpu.make_async_remote_copy(
            src_ref=fp.at[u], dst_ref=fq.at[u, v], send_sem=fp_s.at[u], recv_sem=fp_r.at[u],
            device_id={"vir": (v + d) % around}, device_id_type=MESH,
        )

    def finish(u):
        for m in range(4):
            for h in range(2):
                start = u * tall + m * s.nocc + h * s.half
                flip = fa[start : start + s.half, :].T
                flip = jnp.concatenate([flip, jnp.zeros((s.q, s.parts * 128 - s.half), F32)], axis=1)
                for part in range(s.parts):
                    for q in range(s.nq):
                        fl[h, part, pl.ds(m * s.nq + q, nz, stride=rows4), :] = flip[
                            q * nz : (q + 1) * nz, part * 128 : (part + 1) * 128
                        ]
        for h in range(2):
            fb[u, h] = jnp.concatenate([fl[h, part] for part in range(s.parts)], axis=1).astype(BF16)
        fan(1, 2 * nz, functools.partial(to_owner, u))
        fr[u, me] = fb[u, c, pl.ds(pl.multiple_of(z * rows4, 16), rows4), :]

    def pass_on(u):
        arrived(fr.at[u, pl.ds(0, 2 * nz - 1)], fz_r.at[u])
        total = fr[u, 0].astype(F32)
        for other in range(1, 2 * nz):
            total = total + fr[u, other].astype(F32)
        fp[u] = total.astype(BF16)
        fan(1, around, functools.partial(to_plane, u))
        fq[u, v] = fp[u]

    def apply(u):
        arrived(fq.at[u, pl.ds(0, around - 1)], fp_r.at[u])
        total = fq[u, 0].astype(F32)
        for other in range(1, around):
            total = total + fq[u, other].astype(F32)
        folded = split(total[:, : s.half])
        owner = lax.broadcasted_iota(jnp.int32, folded.shape, 0) % s.nq
        both = None
        for q in range(s.nq):
            value = dot(jnp.where(owner == q, folded.astype(F32), 0.0).astype(BF16), hp[q])
            both = value if both is None else both + value
        spart[...] = both[:rows4] + both[rows4:]
        for m in range(4):
            value = spart[m * s.nq : m * s.nq + 1, :]
            for q in range(1, s.nq):
                value = value + spart[m * s.nq + q : m * s.nq + q + 1, :]
            sgs[4 * u + m] = value

    late = s.spans[2][1]

    def pair(step):
        return third + step % late, step // late

    @pl.loop(1, late)
    def _(half):
        step = 2 * half
        advance(pair(step - 2), pair(step - 1), pair(step), pair(step + 1))

        @pl.when(half == late // 2)
        def _():
            finish(0)

        @pl.when(half == late - 1)
        def _():
            pass_on(0)

    last = 2 * late - 1
    fold(0, *pair(last - 1))
    weigh(1, *pair(last))
    fold(1, *pair(last))
    finish(1)
    for group in range(3):
        sent(hs[group].at[pl.ds(0, nz - 1)], h_s.at[group])
        sent(hg[group].at[pl.ds(0, side - 1)], g_s.at[group])
        sent(bs[group], b_s.at[group])
    sent(vb.at[:, pl.ds(0, side * s.rows), :], v_s)
    sent(sh.at[pl.ds(0, nz - 1)], sh_s)
    sent(xf, x_s)
    sent(rg.at[pl.ds(0, around - 1)], rg_s)
    sent(rall.at[c, pl.ds(0, (nz - 1) * nq8), :], rz_s)
    sent(rall.at[c], rc_s)
    apply(0)
    pass_on(1)
    for u in range(2):
        sent(fr.at[u, pl.ds(0, 2 * nz - 1)], fz_s.at[u])
    apply(1)

    def to_aux(d):
        other = (me + d) % (2 * nz)
        return remote(sgs.at[other // 2], sgr.at[me], s1_s, s1_r, aux=other // 2, occ=other % 2)

    fan(1, 2 * nz, to_aux)
    sgr[me] = sgs[z]
    arrived(sgr.at[pl.ds(0, 2 * nz - 1)], s1_r)
    total = sgr[0]
    for d in range(1, 2 * nz):
        total = total + sgr[d]
    spp[...] = total
    fan(1, around, lambda d: remote(spp, spr.at[v], s2_s, s2_r, vir=(v + d) % around))
    spr[v] = total
    arrived(spr.at[pl.ds(0, around - 1)], s2_r)
    total = spr[0]
    for d in range(1, side * side):
        total = total + spr[d]
    out[...] = total
    for u in range(2):
        sent(fq.at[u, pl.ds(0, around - 1)], fp_s.at[u])
    sent(sgr.at[pl.ds(0, 2 * nz - 1)], s1_s)
    sent(spr.at[pl.ds(0, around - 1)], s2_s)


def output_kernel(terms, trial, eo_row, sigma_out, sub_out, t32):
    t32[...] = trial[...].astype(F32)
    sigma = eo_row[...] * t32[pl.ds(lax.axis_index("aux"), 1), :] + terms[...]
    sigma_out[...] = sigma
    column = jnp.sum(t32[...] * sigma, axis=1, keepdims=True)
    sub_out[...] = jnp.broadcast_to(column, (column.shape[0], 128)).T[0:1]


def local(mesh, integrals, occ_coeffs, vir_coeffs, occ_energy, vir_energy, trial_vectors, shifts):
    s = Sizes(mesh, integrals, occ_coeffs, vir_energy)
    nz, side = s.nz, s.side
    vmem = pltpu.VMEM
    nq8 = s.nq * s.nvec
    rows4 = 4 * s.nq
    dma = lambda *shape: pltpu.SemaphoreType.DMA(shape)
    one = pltpu.SemaphoreType.DMA
    tall = 4 * s.nocc
    flat = s.parts * 128
    scratch = [
        vmem((s.tiles, s.q, s.tile), BF16),
        vmem((s.tiles, s.tile, s.q), BF16),
        vmem((s.tiles, 8, s.tile), F32),
        vmem((s.nvec * s.nocc, s.q), BF16),
        vmem((s.nvec * s.nocc, 128), F32),
        vmem((s.nq, s.half, s.nu), BF16),
        vmem((s.nocc, s.nu), BF16),
        vmem((s.nvec * s.nocc, s.q), F32),
        vmem((tall, s.tile), F32),
        vmem((tall, s.tile), F32),
        vmem((tall, s.tile), BF16),
        vmem((tall, s.tile), BF16),
        vmem((s.nq, s.half, s.nocc), BF16),
        vmem((2, s.parts, nz * rows4, 128), F32),
        vmem((s.quads, 2, nz * rows4, flat), BF16),
        vmem((s.quads, 2 * nz, rows4, flat), BF16),
        vmem((s.quads, rows4, flat), BF16),
        vmem((s.quads, side * side, rows4, flat), BF16),
        vmem((rows4, s.nocc), F32),
        vmem((nz, 1, s.nocc), F32),
        vmem((2 * nz, 1, s.nocc), F32),
        vmem((1, s.nocc), F32),
        vmem((side * side, 1, s.nocc), F32),
        vmem((s.nq, s.window, s.nu), BF16),
        vmem((s.nocc, s.ao), BF16),
        vmem((s.nq, s.nocc, s.nu), F32),
        vmem((s.nq, s.half, s.nu), F32),
        *[vmem((nz, pack, s.nu), F32) for pack in s.packs],
        *[vmem((nz, pack, s.nu), BF16) for pack in s.packs],
        *[vmem((side, nz, pack, s.nu), BF16) for pack in s.packs],
        vmem((side, side * s.lanes, s.nu), BF16),
        vmem((side, s.nu, side * s.lanes), BF16),
        vmem((2, 2, s.rows, s.nu), BF16),
        *[vmem((nz * pack, side * s.lanes), F32) for pack in s.packs],
        *[vmem((side - 1, nz * pack, s.lanes), BF16) for pack in s.packs],
        *[vmem((side - 1, nz * pack, s.lanes), BF16) for pack in s.packs],
        vmem((s.lanes // 128, nz * max(s.packs), 128), F32),
        vmem((s.q, s.tiles * s.tile), F32),
        vmem((s.nocc, 128), F32),
        vmem((8, s.lanes), F32),
        vmem((8, 128), F32),
        vmem((nq8, flat), F32),
        vmem((side * side, nq8, flat), BF16),
        vmem((nq8, flat), BF16),
        vmem((2, nz * nq8, flat), BF16),
        vmem((2, s.parts, nz * nq8, 128), F32),
        vmem((s.nvec, s.nocc, s.q), F32),
        vmem((nz, 8, 128), F32),
        dma(s.nq + 1), one, one, dma(2), dma(2), one, one,
        one, dma(s.nq), dma(3), dma(3), dma(3), dma(3, 2),
        one, one, one, one, one, one,
        dma(3), dma(3),
        dma(s.quads), dma(s.quads), dma(s.quads), dma(s.quads), one, one, one, one,
    ]
    hbm = pl.BlockSpec(memory_space=pl.ANY)
    fast = pl.BlockSpec(memory_space=pltpu.VMEM)
    scalars = pl.BlockSpec(memory_space=pltpu.SMEM)
    shape = jax.ShapeDtypeStruct
    limit = 56 * 1024 * 1024
    occ_row, trial_rows = occ_energy[None], trial_vectors.T
    terms = pl.pallas_call(
        functools.partial(kernel, s),
        out_shape=shape((1, s.nocc), F32),
        in_specs=[hbm, hbm, hbm, fast, fast, scalars, fast, scalars],
        out_specs=fast,
        scratch_shapes=scratch,
        compiler_params=pltpu.CompilerParams(collective_id=0, has_side_effects=True, vmem_limit_bytes=limit),
    )(integrals, occ_coeffs.T, vir_coeffs.T, trial_rows, occ_row, occ_energy, vir_energy[None], shifts)
    sigma, sub = pl.pallas_call(
        output_kernel,
        out_shape=(shape((1, s.nocc), F32), shape((1, s.nvec), F32)),
        in_specs=[fast] * 3,
        out_specs=(fast, fast),
        scratch_shapes=[vmem((s.nvec, s.nocc), F32)],
    )(terms, trial_rows, occ_row)
    return sigma.T, sub.T


def solution(mesh):
    return jax.shard_map(
        functools.partial(local, dict(mesh.shape)),
        mesh=mesh,
        in_specs=(P("aux", "occ", "vir"), P(), P("vir", None), P(), P("vir"), P(), P("aux")),
        out_specs=(P(None, "aux"), P(None, "aux")),
        check_vma=False,
    )
```

```python
import functools
import math

import jax
import jax.numpy as jnp
from jax import lax
from jax.experimental import pallas as pl
from jax.experimental.pallas import tpu as pltpu
from jax.sharding import PartitionSpec as P

MESH = pl.DeviceIdType.MESH
F32 = jnp.float32
BF16 = jnp.bfloat16


def dot(a, b):
    return jnp.dot(a, b, preferred_element_type=F32)


def dot_nt(a, b):
    return lax.dot_general(a, b, (((1,), (1,)), ((), ())), preferred_element_type=F32)


def split(value):
    high = value.astype(BF16)
    low = (value - high.astype(F32)).astype(BF16)
    return jnp.concatenate([high.astype(F32), low.astype(F32)], axis=0).astype(BF16)


def remote(src, dst, send_sem, recv_sem, **device):
    return pltpu.make_async_remote_copy(
        src_ref=src, dst_ref=dst, send_sem=send_sem, recv_sem=recv_sem, device_id=device, device_id_type=MESH
    )


class Sizes:
    def __init__(self, mesh, integrals, occ_coeffs, vir_energy):
        self.nz = mesh["aux"]
        self.side = math.isqrt(mesh["vir"])
        self.nq, self.mu, self.nu = integrals.shape
        self.ao, self.nocc = occ_coeffs.shape
        self.half = self.nocc // 2
        self.jb = self.half // self.nz
        self.na = vir_energy.shape[0]
        self.block = 16 * (self.na // 16)
        self.rows = self.block + 16
        assert self.na == self.block + 1 and self.side == 4
        third = self.jb // 12 * 4
        self.groups = [(0, third), (third, third), (2 * third, self.jb - 2 * third)]
        self.packs = [-(-(self.nq * count) // 16) * 16 for _, count in self.groups]
        self.tile = 512
        self.tiles = -(-(self.jb * self.na) // self.tile)
        ends = [(j0 + count) * self.na // self.tile for j0, count in self.groups[:-1]] + [self.tiles]
        self.spans = [(start, end - start) for start, end in zip([0] + ends, ends)]
        self.quads = self.nz // 4
        self.lane0 = self.mu // 128 * 128
        self.shift = self.mu - self.lane0
        self.window = self.mu + self.shift
        self.lanes = -(-self.rows // 128) * 128
        self.q = self.nq * self.nz
        self.nvec = self.nz
        self.parts = -(-self.half // 128)
        last = 128 * (self.nu * (mesh["vir"] - 1) // 128) - 128
        self.view = self.ao - last
        for v in range(mesh["vir"]):
            start = 128 * (self.nu * v // 128) - 128 * ((v + 1) // mesh["vir"])
            assert start + self.view <= self.ao and self.nu * v - start + self.nu <= self.view


def kernel(
    s, int_h, occ_h, vir_h, trial, eo_row, eo_s, ve, shift_s,
    out,
    bj, bjt, base, rm, row, hq, sec, fa, coupled0, coupled1, weighted0, weighted1,
    hp, fl, fb, fr, fp, fq, spart, sgs, sgr, spp, spr,
    ibuf, occ_v, pf, xf, pk0, pk1, pk2, hs0, hs1, hs2, hg0, hg1, hg2, vb, vbt, vst,
    acc0, acc1, acc2, bs0, bs1, bs2, bx0, bx1, bx2, bf, bflat, eob, ve8, shift,
    rp, rg, rmsg, rall, rl, rm32, sh,
    in_sem, v_own, v_s, v_r, st_r, sh_s, sh_r, x_s, x_r, h_s, h_r, g_s, g_r, rg_s, rg_r, rz_s, rz_r, rc_s, rc_r,
    b_s, b_r, fz_s, fz_r, fp_s, fp_r, s1_s, s1_r, s2_s, s2_r,
):
    nz, side = s.nz, s.side
    z, c, v = lax.axis_index("aux"), lax.axis_index("occ"), lax.axis_index("vir")
    y, x = v // side, v % side
    g = y + c * (x - y)
    r = x + c * (y - x)
    sg = side - (side - 1) * c
    sr = 1 + (side - 1) * c

    def vid(gather, reduce):
        return gather * sg + reduce * sr

    pk, hs, hg, acc = (pk0, pk1, pk2), (hs0, hs1, hs2), (hg0, hg1, hg2), (acc0, acc1, acc2)
    bs, bx = (bs0, bs1, bs2), (bx0, bx1, bx2)
    me = 2 * z + c
    around = side * side

    def fan(first, last, copy):
        @pl.loop(first, last)
        def _(d):
            copy(d).start()

    def go(*args, **device):
        remote(*args, **device).start()

    def arrived(ref, sem):
        remote(ref, ref, sem, sem, occ=c).wait_recv()

    def sent(ref, sem):
        remote(ref, ref, sem, sem, occ=c).wait_send()

    occ_in = pltpu.make_async_copy(occ_h, occ_v, in_sem.at[s.nq])
    occ_in.start()
    zero_rows = jnp.zeros((s.shift, s.nu), BF16)

    def load(q):
        return pltpu.make_async_copy(
            int_h.at[q], ibuf.at[q, pl.ds(pl.multiple_of(s.shift * c, 16), s.mu), :], in_sem.at[q]
        )

    for q in range(s.nq):
        if s.shift:
            ibuf[q, 0 : s.shift, :] = zero_rows
            ibuf[q, s.mu : s.mu + s.shift, :] = zero_rows
    fan(0, s.nq, load)

    def window(gather, w):
        return vir_h.at[pl.ds(pl.multiple_of(s.block * vid(gather, w), 16), s.rows), :]

    def place(slot, w):
        return vb.at[slot, pl.ds(pl.multiple_of(w * s.lanes, 16), s.rows), :]

    fan(0, side, lambda w: pltpu.make_async_copy(window(g, w), place(0, w), v_own))
    for group in range(3):
        pk[group][...] = jnp.zeros(pk[group].shape, F32)
    rp[...] = jnp.zeros(rp.shape, F32)
    for d in range(side):
        for w in range(side):
            vb[d, w * s.lanes + s.rows : (w + 1) * s.lanes, :] = jnp.zeros((s.lanes - s.rows, s.nu), BF16)

    barrier = pltpu.get_barrier_semaphore()

    @pl.loop(1, 2 * nz)
    def _(d):
        other = (me + d) % (2 * nz)
        pl.semaphore_signal(barrier, inc=1, device_id={"aux": other // 2, "occ": other % 2}, device_id_type=MESH)

    @pl.loop(1, around)
    def _(d):
        pl.semaphore_signal(barrier, inc=1, device_id={"vir": (v + d) % around}, device_id_type=MESH)

    pl.semaphore_wait(barrier, 2 * nz + around - 2)

    ahead, behind = vid((g + 1) % side, r), vid((g + 3) % side, r)
    opposite = (g + 2) % side

    @pl.loop(0, 2)
    def _(w):
        go(window(opposite, w), vst.at[0, w], v_s, st_r.at[0], vir=ahead)
        go(window(opposite, w + 2), vst.at[1, w], v_s, st_r.at[1], vir=behind)

    @pl.loop(0, side)
    def _(w):
        go(window((g + 1) % side, w), place(3, w), v_s, v_r.at[0], vir=ahead)
        go(window((g + 3) % side, w), place(1, w), v_s, v_r.at[0], vir=behind)

    shift[...] = jnp.full((8, 128), shift_s[0], F32)
    fan(1, nz, lambda d: remote(shift, sh.at[z], sh_s, sh_r, aux=(z + d) % nz))
    sh[z] = shift[...]

    occ_in.wait()

    @pl.loop(0, s.nq)
    def _(q):
        load(q).wait()
        columns = occ_v[:, pl.ds(pl.multiple_of(s.lane0 * c, 128), s.window)]
        pf[q] = dot(columns, ibuf[q])
        theirs = pf.at[q, pl.ds(pl.multiple_of(s.half * (1 - c), 8), s.half), :]
        go(theirs, xf.at[q], x_s, x_r.at[q], occ=1 - c)

    start = 128 * ((s.nu * v) // 128) - 128 * ((v + 1) // (side * side))
    view = occ_v[:, pl.ds(pl.multiple_of(start, 128), s.view)].astype(F32)
    wide = -(-s.view // 128) * 128
    view = jnp.concatenate([view, jnp.zeros((s.nocc, wide - s.view), F32)], axis=1)
    sec[...] = pltpu.roll(view, wide - (s.nu * v - start), 1)[:, : s.nu].astype(BF16)
    weights = split(dot(trial[...], sec[...]))
    arrived(vst.at[0], st_r.at[0])
    arrived(vst.at[1], st_r.at[1])

    @pl.loop(0, 2)
    def _(w):
        go(vst.at[0, w], place(2, w), v_s, v_r.at[1], vir=ahead)
        go(vst.at[1, w], place(2, w + 2), v_s, v_r.at[1], vir=behind)

    for q in range(s.nq):
        arrived(xf.at[q], x_r.at[q])
        xf[q] = xf[q] + pf[q, pl.ds(pl.multiple_of(s.half * c, 8), s.half), :]
        for group, (j0, count) in enumerate(s.groups):
            for to in range(nz):
                pk[group][to, q * count : (q + 1) * count, :] = xf[q, to * s.jb + j0 : to * s.jb + j0 + count, :]

    def scatter(group):
        hs[group][...] = pk[group][...].astype(BF16)

        def copy(d):
            to = (z + d) % nz
            return remote(hs[group].at[to], hg[group].at[0, z], h_s.at[group], h_r.at[group], aux=to)

        fan(1, nz, copy)
        hg[group][0, z] = hs[group][z]

    scatter(0)
    for q in range(s.nq):
        hq[q] = xf[q].astype(BF16)
    for q in range(s.nq):
        both = dot_nt(weights, hq[q])
        rp[q * s.nvec : (q + 1) * s.nvec, 0 : s.half] = both[: s.nvec] + both[s.nvec :]
    rg[v] = rp[...].astype(BF16)
    fan(1, around, lambda d: remote(rg.at[v], rg.at[v], rg_s, rg_r, vir=(v + d) % around))
    for q in range(s.nq):
        hp[q] = dot_nt(hq[q], sec[...]).astype(BF16)

    ve8[...] = jnp.ones(ve8.shape, F32)
    ve8[:, 0 : s.na] = jnp.broadcast_to(ve[...], (8, s.na))
    bflat[...] = jnp.ones(bflat.shape, F32)
    first = s.half * c + s.jb * z
    for j in range(s.jb):
        bflat[0:8, j * s.na : (j + 1) * s.na] = ve8[:, 0 : s.na] - eo_s[first + j]
    for tile in range(s.tiles):
        base[tile] = bflat[0:8, tile * s.tile : (tile + 1) * s.tile]
    square = jnp.broadcast_to(eo_row[...], (128, s.nocc))
    fill = -(-s.nocc // 128) * 128 - s.nocc
    eob[...] = jnp.concatenate([square, jnp.zeros((128, fill), F32)], axis=1).T[: s.nocc]

    across = vid((g + 2) % side, r)

    def gather(group):
        arrived(hg[group].at[0, pl.ds(0, nz - 1)], h_r.at[group])
        for slot, to, sem in ((1, behind, 0), (3, ahead, 0), (2, across, 1)):
            go(hg[group].at[0], hg[group].at[slot], g_s.at[group], g_r.at[group, sem], vir=to)

    def near_in(group):
        arrived(hg[group].at[pl.ds(0, 2)], g_r.at[group, 0])

    def far_in(group):
        arrived(hg[group].at[2], g_r.at[group, 1])

    def term(group, d):
        return dot(hg[group][d].reshape(nz * s.packs[group], s.nu), vbt[d])

    def product(group, slots):
        value = term(group, slots[0])
        for d in slots[1:]:
            value = value + term(group, d)
        acc[group][...] = value if slots[0] == 0 else value + acc[group][...]

    def columns_of(w):
        return pl.ds(pl.multiple_of(w * s.lanes, 128), s.lanes)

    def reduce_start(group):
        for e in (2, 1, 3):
            w = (r + e) % side
            bs[group][e - 1] = acc[group][:, columns_of(w)].astype(BF16)
            go(bs[group].at[e - 1], bx[group].at[e - 1], b_s.at[group], b_r.at[group], vir=vid(g, w))

    nq8 = s.nq * s.nvec
    iota = functools.partial(lax.broadcasted_iota, jnp.int32, (s.nu, s.nu))
    identity = jnp.where(iota(0) == iota(1), 1.0, 0.0).astype(BF16)

    def turn(d):
        vbt[d] = dot_nt(identity, vb[d]).astype(BF16)

    pltpu.make_async_copy(vir_h.at[pl.ds(0, side * s.rows), :], vb.at[0, pl.ds(0, side * s.rows), :], v_own).wait()
    turn(0)
    gather(0)
    arrived(rg.at[pl.ds(0, around - 1)], rg_r)
    total = rg[0].astype(F32)
    for other in range(1, around):
        total = total + rg[other].astype(F32)
    rmsg[...] = total.astype(BF16)
    own_rows = pl.ds(pl.multiple_of(z * nq8, 16), nq8)
    fan(1, nz, lambda d: remote(rmsg, rall.at[c, own_rows, :], rz_s, rz_r, aux=(z + d) % nz))
    rall[c, own_rows, :] = rmsg[...]
    scatter(1)
    scatter(2)
    product(0, (0,))
    arrived(vb.at[pl.ds(1, 2), pl.ds(0, side * s.rows), :], v_r.at[0])
    turn(1)
    turn(3)
    gather(1)
    near_in(0)
    product(0, (1, 3))
    arrived(vb.at[2, pl.ds(0, side * s.rows), :], v_r.at[1])
    turn(2)
    far_in(0)
    product(0, (2,))
    reduce_start(0)
    product(1, (0,))
    arrived(rall.at[c, pl.ds(0, (nz - 1) * nq8), :], rz_r)
    arrived(sh.at[pl.ds(0, nz - 1)], sh_r)
    go(rall.at[c], rall.at[c], rc_s, rc_r, occ=1 - c)
    near_in(1)
    product(1, (1, 3))
    far_in(1)
    product(1, (2,))
    reduce_start(1)
    gather(2)
    for n in range(s.nvec):
        row[n * s.nocc : (n + 1) * s.nocc, :] = jnp.broadcast_to(sh[n][0:1, :], (s.nocc, 128)) - eob[...]

    def lay_out(h):
        for part in range(s.parts):
            rl[h, part] = rall[h, :, part * 128 : (part + 1) * 128].astype(F32)
        for n in range(s.nvec):
            sides = []
            for part in range(s.parts):
                rows = [rl[h, part, pl.ds(q * s.nvec + n, nz, stride=nq8), :] for q in range(s.nq)]
                sides.append(jnp.concatenate(rows, axis=0))
            rm32[n, pl.ds(pl.multiple_of(h * s.half, 8), s.half), :] = jnp.concatenate(sides, axis=1).T[: s.half]

    lay_out(c)
    arrived(rall.at[1 - c], rc_r)
    lay_out(1 - c)
    for n in range(s.nvec):
        rm[n * s.nocc : (n + 1) * s.nocc, :] = rm32[n].astype(BF16)
    product(2, (0,))

    def build(group):
        j0, count = s.groups[group]
        pack = s.packs[group]
        arrived(bx[group], b_r.at[group])

        @pl.loop(0, nz)
        def _(source):
            rows = pl.ds(pl.multiple_of(source * pack, 16), pack)
            value = acc[group][rows, columns_of(r)]
            for e in range(side - 1):
                value = value + bx[group][e, rows, :].astype(F32)
            full = pltpu.roll(value.astype(BF16).astype(F32), s.lanes - v, 1)
            for part in range(s.lanes // 128):
                bf[part, rows, :] = full[:, part * 128 : (part + 1) * 128]

        for j in range(count):
            parts = []
            for part in range(s.lanes // 128):
                rows = [bf[part, pl.ds(q * count + j, nz, stride=pack), :] for q in range(s.nq)]
                parts.append(jnp.concatenate(rows, axis=0))
            bflat[:, (j0 + j) * s.na : (j0 + j + 1) * s.na] = jnp.concatenate(parts, axis=1)[:, : s.na]

    def ready(group):
        build(group)
        start, count = s.spans[group]
        for tile in range(start, start + count):
            flat = bflat[:, tile * s.tile : (tile + 1) * s.tile]
            bj[tile] = flat.astype(BF16)
            bjt[tile] = flat.T.astype(BF16)

    tall = 4 * s.nocc
    coupled, weighted = (coupled0, coupled1), (weighted0, weighted1)

    def couple(slot, tile, quad):
        coupled[slot][...] = dot(rm[pl.ds(pl.multiple_of(quad * tall, 16), tall), :], bj[tile])

    def weigh(slot, tile, quad):
        own = row[pl.ds(pl.multiple_of(quad * tall, 8), tall), :]
        divisor = jnp.concatenate([own] * (s.tile // 128), axis=1) + base[tile, 0:1, :]
        weighted[slot][...] = (coupled[slot][...] * pl.reciprocal(divisor, approx=True, full_range=False)).astype(BF16)

    def fold(slot, tile, quad):
        fa[pl.ds(pl.multiple_of(quad * tall, 8), tall), :] += dot(weighted[slot][...], bjt[tile])

    def advance(older, old, new, newer):
        fold(0, *older)
        weigh(1, *old)
        couple(0, *new)
        fold(1, *old)
        weigh(0, *new)
        couple(1, *newer)

    fa[...] = jnp.zeros(fa.shape, F32)
    bflat[:, s.tiles * s.tile - 128 :] = jnp.zeros((s.q, 128), F32)
    ready(0)
    couple(0, 0, 0)
    couple(1, 0, 1)
    weigh(0, 0, 0)
    second, third = s.spans[1][0], s.spans[2][0]

    @pl.loop(1, third)
    def _(tile):
        @pl.when(tile == 2)
        def _():
            near_in(2)
            product(2, (1, 3))
            far_in(2)
            product(2, (2,))
            reduce_start(2)

        @pl.when(tile == second)
        def _():
            ready(1)

        advance((tile - 1, 0), (tile - 1, 1), (tile, 0), (tile, 1))

    ready(2)
    advance((third - 1, 0), (third - 1, 1), (third, 0), (third + 1, 0))

    rows4 = 4 * s.nq

    def to_owner(u, d):
        other = (me + d) % (2 * nz)
        return pltpu.make_async_remote_copy(
            src_ref=fb.at[u, other % 2, pl.ds(pl.multiple_of(other // 2 * rows4, 16), rows4), :], dst_ref=fr.at[u, me],
            send_sem=fz_s.at[u], recv_sem=fz_r.at[u],
            device_id={"aux": other // 2, "occ": other % 2}, device_id_type=MESH,
        )

    def to_plane(u, d):
        return pltpu.make_async_remote_copy(
            src_ref=fp.at[u], dst_ref=fq.at[u, v], send_sem=fp_s.at[u], recv_sem=fp_r.at[u],
            device_id={"vir": (v + d) % around}, device_id_type=MESH,
        )

    def finish(u):
        for m in range(4):
            for h in range(2):
                start = u * tall + m * s.nocc + h * s.half
                flip = fa[start : start + s.half, :].T
                flip = jnp.concatenate([flip, jnp.zeros((s.q, s.parts * 128 - s.half), F32)], axis=1)
                for part in range(s.parts):
                    for q in range(s.nq):
                        fl[h, part, pl.ds(m * s.nq + q, nz, stride=rows4), :] = flip[
                            q * nz : (q + 1) * nz, part * 128 : (part + 1) * 128
                        ]
        for h in range(2):
            fb[u, h] = jnp.concatenate([fl[h, part] for part in range(s.parts)], axis=1).astype(BF16)
        fan(1, 2 * nz, functools.partial(to_owner, u))
        fr[u, me] = fb[u, c, pl.ds(pl.multiple_of(z * rows4, 16), rows4), :]

    def pass_on(u):
        arrived(fr.at[u, pl.ds(0, 2 * nz - 1)], fz_r.at[u])
        total = fr[u, 0].astype(F32)
        for other in range(1, 2 * nz):
            total = total + fr[u, other].astype(F32)
        fp[u] = total.astype(BF16)
        fan(1, around, functools.partial(to_plane, u))
        fq[u, v] = fp[u]

    def apply(u):
        arrived(fq.at[u, pl.ds(0, around - 1)], fp_r.at[u])
        total = fq[u, 0].astype(F32)
        for other in range(1, around):
            total = total + fq[u, other].astype(F32)
        folded = split(total[:, : s.half])
        owner = lax.broadcasted_iota(jnp.int32, folded.shape, 0) % s.nq
        both = None
        for q in range(s.nq):
            value = dot(jnp.where(owner == q, folded.astype(F32), 0.0).astype(BF16), hp[q])
            both = value if both is None else both + value
        spart[...] = both[:rows4] + both[rows4:]
        for m in range(4):
            value = spart[m * s.nq : m * s.nq + 1, :]
            for q in range(1, s.nq):
                value = value + spart[m * s.nq + q : m * s.nq + q + 1, :]
            sgs[4 * u + m] = value

    late = s.spans[2][1]

    def pair(step):
        return third + step % late, step // late

    @pl.loop(1, late)
    def _(half):
        step = 2 * half
        advance(pair(step - 2), pair(step - 1), pair(step), pair(step + 1))

        @pl.when(half == late // 2)
        def _():
            finish(0)

        @pl.when(half == late - 1)
        def _():
            pass_on(0)

    last = 2 * late - 1
    fold(0, *pair(last - 1))
    weigh(1, *pair(last))
    fold(1, *pair(last))
    finish(1)
    for group in range(3):
        sent(hs[group].at[pl.ds(0, nz - 1)], h_s.at[group])
        sent(hg[group].at[pl.ds(0, side - 1)], g_s.at[group])
        sent(bs[group], b_s.at[group])
    sent(vb.at[:, pl.ds(0, side * s.rows), :], v_s)
    sent(sh.at[pl.ds(0, nz - 1)], sh_s)
    sent(xf, x_s)
    sent(rg.at[pl.ds(0, around - 1)], rg_s)
    sent(rall.at[c, pl.ds(0, (nz - 1) * nq8), :], rz_s)
    sent(rall.at[c], rc_s)
    apply(0)
    pass_on(1)
    for u in range(2):
        sent(fr.at[u, pl.ds(0, 2 * nz - 1)], fz_s.at[u])
    apply(1)

    def to_aux(d):
        other = (me + d) % (2 * nz)
        return remote(sgs.at[other // 2], sgr.at[me], s1_s, s1_r, aux=other // 2, occ=other % 2)

    fan(1, 2 * nz, to_aux)
    sgr[me] = sgs[z]
    arrived(sgr.at[pl.ds(0, 2 * nz - 1)], s1_r)
    total = sgr[0]
    for d in range(1, 2 * nz):
        total = total + sgr[d]
    spp[...] = total
    fan(1, around, lambda d: remote(spp, spr.at[v], s2_s, s2_r, vir=(v + d) % around))
    spr[v] = total
    arrived(spr.at[pl.ds(0, around - 1)], s2_r)
    total = spr[0]
    for d in range(1, side * side):
        total = total + spr[d]
    out[...] = total
    for u in range(2):
        sent(fq.at[u, pl.ds(0, around - 1)], fp_s.at[u])
    sent(sgr.at[pl.ds(0, 2 * nz - 1)], s1_s)
    sent(spr.at[pl.ds(0, around - 1)], s2_s)


def output_kernel(terms, trial, eo_row, sigma_out, sub_out, t32):
    t32[...] = trial[...].astype(F32)
    sigma = eo_row[...] * t32[pl.ds(lax.axis_index("aux"), 1), :] + terms[...]
    sigma_out[...] = sigma
    column = jnp.sum(t32[...] * sigma, axis=1, keepdims=True)
    sub_out[...] = jnp.broadcast_to(column, (column.shape[0], 128)).T[0:1]


def local(mesh, integrals, occ_coeffs, vir_coeffs, occ_energy, vir_energy, trial_vectors, shifts):
    s = Sizes(mesh, integrals, occ_coeffs, vir_energy)
    nz, side = s.nz, s.side
    vmem = pltpu.VMEM
    nq8 = s.nq * s.nvec
    rows4 = 4 * s.nq
    dma = lambda *shape: pltpu.SemaphoreType.DMA(shape)
    one = pltpu.SemaphoreType.DMA
    tall = 4 * s.nocc
    flat = s.parts * 128
    scratch = [
        vmem((s.tiles, s.q, s.tile), BF16),
        vmem((s.tiles, s.tile, s.q), BF16),
        vmem((s.tiles, 8, s.tile), F32),
        vmem((s.nvec * s.nocc, s.q), BF16),
        vmem((s.nvec * s.nocc, 128), F32),
        vmem((s.nq, s.half, s.nu), BF16),
        vmem((s.nocc, s.nu), BF16),
        vmem((s.nvec * s.nocc, s.q), F32),
        vmem((tall, s.tile), F32),
        vmem((tall, s.tile), F32),
        vmem((tall, s.tile), BF16),
        vmem((tall, s.tile), BF16),
        vmem((s.nq, s.half, s.nocc), BF16),
        vmem((2, s.parts, nz * rows4, 128), F32),
        vmem((s.quads, 2, nz * rows4, flat), BF16),
        vmem((s.quads, 2 * nz, rows4, flat), BF16),
        vmem((s.quads, rows4, flat), BF16),
        vmem((s.quads, side * side, rows4, flat), BF16),
        vmem((rows4, s.nocc), F32),
        vmem((nz, 1, s.nocc), F32),
        vmem((2 * nz, 1, s.nocc), F32),
        vmem((1, s.nocc), F32),
        vmem((side * side, 1, s.nocc), F32),
        vmem((s.nq, s.window, s.nu), BF16),
        vmem((s.nocc, s.ao), BF16),
        vmem((s.nq, s.nocc, s.nu), F32),
        vmem((s.nq, s.half, s.nu), F32),
        *[vmem((nz, pack, s.nu), F32) for pack in s.packs],
        *[vmem((nz, pack, s.nu), BF16) for pack in s.packs],
        *[vmem((side, nz, pack, s.nu), BF16) for pack in s.packs],
        vmem((side, side * s.lanes, s.nu), BF16),
        vmem((side, s.nu, side * s.lanes), BF16),
        vmem((2, 2, s.rows, s.nu), BF16),
        *[vmem((nz * pack, side * s.lanes), F32) for pack in s.packs],
        *[vmem((side - 1, nz * pack, s.lanes), BF16) for pack in s.packs],
        *[vmem((side - 1, nz * pack, s.lanes), BF16) for pack in s.packs],
        vmem((s.lanes // 128, nz * max(s.packs), 128), F32),
        vmem((s.q, s.tiles * s.tile), F32),
        vmem((s.nocc, 128), F32),
        vmem((8, s.lanes), F32),
        vmem((8, 128), F32),
        vmem((nq8, flat), F32),
        vmem((side * side, nq8, flat), BF16),
        vmem((nq8, flat), BF16),
        vmem((2, nz * nq8, flat), BF16),
        vmem((2, s.parts, nz * nq8, 128), F32),
        vmem((s.nvec, s.nocc, s.q), F32),
        vmem((nz, 8, 128), F32),
        dma(s.nq + 1), one, one, dma(2), dma(2), one, one,
        one, dma(s.nq), dma(3), dma(3), dma(3), dma(3, 2),
        one, one, one, one, one, one,
        dma(3), dma(3),
        dma(s.quads), dma(s.quads), dma(s.quads), dma(s.quads), one, one, one, one,
    ]
    hbm = pl.BlockSpec(memory_space=pl.ANY)
    fast = pl.BlockSpec(memory_space=pltpu.VMEM)
    scalars = pl.BlockSpec(memory_space=pltpu.SMEM)
    shape = jax.ShapeDtypeStruct
    limit = 56 * 1024 * 1024
    occ_row, trial_rows = occ_energy[None], trial_vectors.T
    terms = pl.pallas_call(
        functools.partial(kernel, s),
        out_shape=shape((1, s.nocc), F32),
        in_specs=[hbm, hbm, hbm, fast, fast, scalars, fast, scalars],
        out_specs=fast,
        scratch_shapes=scratch,
        compiler_params=pltpu.CompilerParams(collective_id=0, has_side_effects=True, vmem_limit_bytes=limit),
    )(integrals, occ_coeffs.T, vir_coeffs.T, trial_rows, occ_row, occ_energy, vir_energy[None], shifts)
    sigma, sub = pl.pallas_call(
        output_kernel,
        out_shape=(shape((1, s.nocc), F32), shape((1, s.nvec), F32)),
        in_specs=[fast] * 3,
        out_specs=(fast, fast),
        scratch_shapes=[vmem((s.nvec, s.nocc), F32)],
    )(terms, trial_rows, occ_row)
    return sigma.T, sub.T


def solution(mesh):
    return jax.shard_map(
        functools.partial(local, dict(mesh.shape)),
        mesh=mesh,
        in_specs=(P("aux", "occ", "vir"), P(), P("vir", None), P(), P("vir"), P(), P("aux")),
        out_specs=(P(None, "aux"), P(None, "aux")),
        check_vma=False,
    )
```
